128 devices in a mesh: space: 16 (over y, x), sub: 8 (over z, core).
Axes of the slice: x: 4, y: 4, z: 4, core: 2. Of those that a mesh axis runs over, the one named last changes fastest.
Arguments:
- seg_data: float32 [4096, 9, 128], P(('space', 'sub')), as said below
- cell_of_block: int32 [4096], P(('space', 'sub')), may hold values from 0 to 4095, as said below
- cell_center: float32 [3, 4096], replicated, as said below
- pairs: int32 [16384, 2], P(('space', 'sub')), may hold values from 0 to 4095, as said below
- live_count: int32 [128], P(('space', 'sub')), may hold values from 1 to 128, as said below
Outputs:
- force: float32 [4096, 3, 128], P(('space', 'sub'))
The draws below stay inside these ranges and needn't reach their ends.
Inputs may be any that keep to these rules, and one draw needn't show every extreme that they name: `seg_data`: offsets, line and Burgers vector components of the segments. cell_of_block[g] lies in the range of cells of the region of g's owner: its space index times 4096 / 16 and up. `cell_center`: coordinates of the cell centres. `pairs`: every slot of device d (live or not) has as target a block of d and as source a different block whose owner's space index differs from d's by at most one, cyclically. `live_count`: some device has all 128 slots live.
All inputs are finite; a program needn't handle non-finite values.
Results may differ from the reference program's by a relative error of at most 0.0003.
Values sent between devices are 32-bit elements; how exact they have to be, the bound alone decides.
A program may use at most 64 MiB of HBM per device.

```python
import math
import jax
import jax.numpy as jnp
from jax import lax

B = 128
NB_DEV = 32
PAIRS_DEV = 128
NBATCH = 32
NCELL = 4096
REGIONS = 16
SUBS = 8
NBLK = 4096
NPAIRS = 16384
DEVICES = 128


def draw_seg_data(key, part):
    key = jax.random.fold_in(key, 19)
    key_one, key_two = jax.random.split(key)
    offsets = 0.6 * jax.random.truncated_normal(key_one, -6.6, 6.6, (NBLK, 3, B), jnp.float32)
    vectors = 0.6 * jax.random.truncated_normal(key_two, -6.6, 6.6, (NBLK, 6, B), jnp.float32)
    return jnp.concatenate([offsets, vectors], axis=1).astype(jnp.float32)


def draw_cell_of_block(key, part):
    key = jax.random.fold_in(key, 7)
    block = jnp.arange(NBLK, dtype=jnp.int32)
    region = block // NB_DEV // SUBS
    per_region = NCELL // REGIONS
    cells = region * per_region + jax.random.randint(key, (NBLK,), 0, per_region)
    cells = cells.at[0].set(0)
    cells = cells.at[NBLK - 1].set(NCELL - 1)
    return cells.astype(jnp.int32)


def draw_cell_center(key, part):
    key = jax.random.fold_in(key, 13)
    spread_draw = jax.random.uniform(key, (3, NCELL), jnp.float32)
    region = (jnp.arange(NCELL, dtype=jnp.int32) // (NCELL // REGIONS)).astype(jnp.float32)
    spread = 0.5
    height = 2.0
    angle = 2.0 * math.pi * (region + spread_draw[0]) / REGIONS
    radius = REGIONS / (2.0 * math.pi) + spread * (spread_draw[1] - 0.5)
    return jnp.stack([radius * jnp.cos(angle), radius * jnp.sin(angle), height * spread_draw[2]]).astype(jnp.float32)


def draw_pairs(key, part):
    key = jax.random.fold_in(key, 11)
    key_one, key_two, key_three = jax.random.split(key, 3)
    entry = jnp.arange(NPAIRS, dtype=jnp.int32)
    owner = entry // PAIRS_DEV
    target = owner * NB_DEV + entry % PAIRS_DEV % NB_DEV
    region = owner // SUBS
    step = jax.random.randint(key_one, (NPAIRS,), -1, 2)
    near_region = (region + step) % REGIONS
    near_sub = jax.random.randint(key_two, (NPAIRS,), 0, SUBS)
    near_slot = jax.random.randint(key_three, (NPAIRS,), 0, NB_DEV)
    base = (near_region * SUBS + near_sub) * NB_DEV
    source = base + near_slot
    source = jnp.where(source == target, base + (near_slot + 1) % NB_DEV, source)
    return jnp.stack([target, source], axis=1).astype(jnp.int32)


def draw_live_count(key, part):
    key = jax.random.fold_in(key, 17)
    key_one, key_two = jax.random.split(key)
    level = jax.random.randint(key_one, (DEVICES,), 1, 17)
    counts = jnp.maximum(1, level * level * PAIRS_DEV // 256)
    top = jax.random.randint(key_two, (), 0, DEVICES)
    counts = counts.at[top].set(PAIRS_DEV)
    counts = counts.at[(top + 1) % DEVICES].set(1)
    return counts.astype(jnp.int32)


def setup_inputs(seed: int = 0) -> dict:
    arg_keys = jax.random.split(jax.random.key(seed), 6)
    seg_data = draw_seg_data(jax.random.fold_in(arg_keys[5], 71), 0)
    cell_of_block = draw_cell_of_block(jax.random.fold_in(arg_keys[5], 71), 0)
    cell_center = draw_cell_center(jax.random.fold_in(arg_keys[5], 71), 0)
    pairs = draw_pairs(jax.random.fold_in(arg_keys[5], 71), 0)
    live_count = draw_live_count(jax.random.fold_in(arg_keys[5], 71), 0)
    return dict(seg_data=seg_data, cell_of_block=cell_of_block, cell_center=cell_center, pairs=pairs, live_count=live_count)


near_a2 = 0.25
far_a2 = 1.0
group_blocks = 4
highest = lax.Precision.HIGHEST

def pair_forces(left, right):
    apart = left[:, 0:3, :, None] - right[:, 0:3, None, :]
    dist2 = lax.optimization_barrier(jnp.sum(apart * apart, axis=1)) + near_a2
    weight = 1.0 / (dist2 * jnp.sqrt(dist2))
    cross_one = jnp.einsum('nki,nkj->nij', left[:, 6:9], right[:, 3:6], precision=highest)
    cross_two = jnp.einsum('nki,nkj->nij', left[:, 3:6], right[:, 6:9], precision=highest)
    coupling = weight * cross_one * cross_two
    pushed = coupling[:, None] * apart
    return (lax.optimization_barrier(jnp.sum(pushed, axis=3)), -lax.optimization_barrier(jnp.sum(pushed, axis=2)))

def block_moments(packed):
    outer = jnp.einsum('gas,gbs->gab', packed[:, 6:9], packed[:, 3:6], precision=highest)
    return outer.reshape(packed.shape[0], 9)

def far_group(block_data, block_cells, moments, cell_center):
    count = block_data.shape[0]
    width = block_data.shape[2]
    ncell = cell_center.shape[1]
    flat = block_data.transpose(1, 0, 2).reshape(9, count * width)
    seg_cell = jnp.repeat(block_cells, width)
    dist2 = jnp.zeros((ncell, count * width), jnp.float32)
    for axis_k in range(3):
        delta = cell_center[axis_k][:, None] - flat[axis_k][None, :]
        dist2 = dist2 + delta * delta
    weight = 1.0 / (far_a2 + dist2)
    same = jnp.arange(ncell, dtype=jnp.int32)[:, None] == seg_cell[None, :]
    weight = jnp.where(same, 0.0, weight)
    grid = jnp.dot(moments, weight, precision=highest)
    result = lax.optimization_barrier(jnp.sum(grid.reshape(3, 3, -1) * flat[None, 3:6, :], axis=1))
    return result.reshape(3, count, width).transpose(1, 0, 2)

def reference(seg_data, cell_of_block, cell_center, pairs, live_count):
    centre = jnp.take(cell_center, cell_of_block, axis=1).T
    packed = jnp.concatenate([seg_data[:, 0:3, :] + centre[:, :, None], seg_data[:, 3:9, :]], axis=1)
    entry = jnp.arange(NPAIRS, dtype=jnp.int32)
    owner = entry // PAIRS_DEV
    live = (entry % PAIRS_DEV < live_count[owner]).astype(jnp.float32)
    batched = pairs.reshape(NPAIRS // NBATCH, NBATCH, 2)
    live_batched = live.reshape(NPAIRS // NBATCH, NBATCH)

    def add_batch(total, item):
        batch, alive = item
        targets = batch[:, 0]
        sources = batch[:, 1]
        on_left, on_right = pair_forces(packed[targets], packed[sources])
        total = total.at[targets].add(on_left * alive[:, None, None])
        total = total.at[sources].add(on_right * alive[:, None, None])
        return (total, None)
    near, _ = lax.scan(add_batch, jnp.zeros((NBLK, 3, B), jnp.float32), (batched, live_batched))
    moments = jax.ops.segment_sum(block_moments(packed), cell_of_block, num_segments=NCELL).T

    def one_group(item):
        return far_group(item[0], item[1], moments, cell_center)
    far = lax.map(one_group, (packed.reshape(NBLK // group_blocks, group_blocks, 9, B), cell_of_block.reshape(NBLK // group_blocks, group_blocks)))
    return near + far.reshape(NBLK, 3, B)
```

```python
import functools

import jax
import jax.numpy as jnp
from jax import lax
from jax.experimental import pallas as pl
from jax.experimental.pallas import tpu as pltpu
from jax.sharding import PartitionSpec as P

MESH = pl.DeviceIdType.MESH
f32 = jnp.float32
bf16 = jnp.bfloat16
ROWS = 296
UNROLL = 4
SEG_TILE = 2048


def three(x):
    a = x.astype(bf16).astype(f32)
    r = x - a
    b = r.astype(bf16).astype(f32)
    return a, b, (r - b).astype(bf16).astype(f32)


def exchange_and_far(
    seg_ref, cell_ref, cc_ref, pair_ref, far_ref, win_ref,
    payload, flat, mine, parts, moments, cells_f, segs_f, acc,
    x_send, w_send, r_send, w_recv, p_send, p_recv, m_send, m_recv, own_sem,
):
    space = lax.axis_index("space")
    sub = lax.axis_index("sub")
    z, core = sub // 2, sub % 2
    nblocks = seg_ref.shape[0]
    ncell = cc_ref.shape[1]
    per = ncell // 16

    barrier = pltpu.get_barrier_semaphore()

    def greet_sub(k, c):
        pl.semaphore_signal(
            barrier, inc=1, device_id=(space, (sub + k) % 8), device_id_type=MESH
        )
        return c

    def greet_space(k, c):
        pl.semaphore_signal(
            barrier, inc=1, device_id=((space + k) % 16, sub), device_id_type=MESH
        )
        return c

    lax.fori_loop(1, 8, greet_sub, 0)
    lax.fori_loop(1, 16, greet_space, 0)

    base = space * per
    own_cc = cc_ref[:, pl.ds(pl.multiple_of(base, 256), per)]
    hot = (
        cell_ref[...] - base == lax.broadcasted_iota(jnp.int32, (nblocks, per), 1)
    ).astype(f32)
    centre = lax.dot_general(
        own_cc, hot, (((1,), (1,)), ((), ())),
        precision=lax.Precision.HIGHEST, preferred_element_type=f32,
    )
    origin = centre[:, 0:1]
    total = jnp.zeros((9, per), f32)
    for g in range(nblocks):
        lanes = slice(g * 128, g * 128 + 128)
        pos = seg_ref[g, 0:3, :] + centre[:, g : g + 1]
        rest = seg_ref[g, 3:9, :]
        payload[9 * g : 9 * g + 3, :] = pos
        payload[9 * g + 3 : 9 * g + 9, :] = rest
        flat[0:3, lanes] = pos
        flat[8:11, lanes] = rest[0:3]
        line, burg = rest[0:3], rest[3:6]
        outer = jnp.concatenate([burg[a : a + 1] * line for a in range(3)], axis=0)
        total = total + jnp.sum(outer, axis=1, keepdims=True) * hot[g : g + 1, :]
    payload[288:296, :] = pair_ref[...]
    mine[0:9, :] = total
    mine[9:16, :] = jnp.zeros((7, per), f32)

    pl.semaphore_wait(barrier, 22)

    def part_copy(k):
        to = (sub + k) % 8
        return pltpu.make_async_remote_copy(
            src_ref=mine, dst_ref=parts.at[7 - k],
            send_sem=p_send.at[k - 1], recv_sem=p_recv.at[7 - k],
            device_id=(space, to), device_id_type=MESH,
        )


    def start_part(k, c):
        part_copy(k).start()
        return c

    lax.fori_loop(1, 8, start_part, 0)

    def beside(step, slot, sem):
        return pltpu.make_async_remote_copy(
            src_ref=payload, dst_ref=win_ref.at[slot, sub],
            send_sem=x_send.at[sem], recv_sem=w_recv.at[slot, sub],
            device_id=((space + step) % 16, sub), device_id_type=MESH,
        )

    right, left = beside(1, 0, 0), beside(15, 2, 1)
    right.start()
    left.start()
    own_copy = pltpu.make_async_copy(payload, win_ref.at[1, sub], own_sem)
    own_copy.start()

    def spread(slot, k):
        src = payload if slot == 1 else win_ref.at[slot, sub]
        if k == 0:
            to = z * 2 + 1 - core
        else:
            to = (z + k) % 4 * 2 + core
        return pltpu.make_async_remote_copy(
            src_ref=src, dst_ref=win_ref.at[slot, sub],
            send_sem=w_send.at[slot, k], recv_sem=w_recv.at[slot, sub],
            device_id=(space, to), device_id_type=MESH,
        )

    def arrived(slot, place):
        pltpu.make_async_copy(
            win_ref.at[slot, place], win_ref.at[slot, place], w_recv.at[slot, place]
        ).wait()

    def relay(slot, k):
        place = (z + k) % 4 * 2 + core
        return pltpu.make_async_remote_copy(
            src_ref=win_ref.at[slot, place], dst_ref=win_ref.at[slot, place],
            send_sem=r_send.at[slot, k - 1], recv_sem=w_recv.at[slot, place],
            device_id=(space, z * 2 + 1 - core), device_id_type=MESH,
        )

    for k in (1, 3, 2, 0):
        spread(1, k).start()

    ones = jnp.ones((3, ncell), f32)
    blank = jnp.zeros((8, ncell), f32)
    c = cc_ref[...] - origin
    c1, c2, c3 = three(c)
    cq = jnp.concatenate(three(jnp.sum(c * c, axis=0, keepdims=True)), axis=0)
    cells_f[...] = jnp.transpose(
        jnp.concatenate([c1, c1, c2, c2, c1, c3, cq, ones, blank], axis=0)
    ).astype(bf16)
    p = flat[0:3, :] - origin
    p1, p2, p3 = three(-2.0 * p)
    pq = jnp.concatenate(three(1.0 + jnp.sum(p * p, axis=0, keepdims=True)), axis=0)
    segs_f[...] = jnp.concatenate(
        [p1, p2, p1, p2, p3, p1, ones, pq, blank], axis=0
    ).astype(bf16)

    region = mine[...]
    for k in range(7):
        pltpu.make_async_copy(parts.at[k], parts.at[k], p_recv.at[k]).wait()
        region = region + parts[k]
    moments[0] = region

    def moment_copy(k):
        return pltpu.make_async_remote_copy(
            src_ref=moments.at[0], dst_ref=moments.at[16 - k],
            send_sem=m_send.at[k], recv_sem=m_recv.at[16 - k],
            device_id=((space + k) % 16, sub), device_id_type=MESH,
        )

    def start_moment(k, c):
        moment_copy(k).start()
        return c

    lax.fori_loop(1, 16, start_moment, 0)

    def split_moments(k):
        m = moments[k]
        hi = m.astype(bf16)
        return jnp.concatenate([hi, (m - hi.astype(f32)).astype(bf16)], axis=0)

    def far_chunk(k, first):
        at = pl.multiple_of((space + k) % 16 * per, 256)
        cells = cells_f[pl.ds(at, per), :]
        m = split_moments(k)
        cell_id = at + lax.broadcasted_iota(jnp.int32, (per, 128), 0)

        def tile(j, carry):
            lanes = pl.ds(pl.multiple_of(j * SEG_TILE, SEG_TILE), SEG_TILE)
            d = jnp.dot(cells, segs_f[:, lanes], preferred_element_type=f32)
            w = pl.reciprocal(d, approx=True)
            if first:
                cols = []
                for q in range(SEG_TILE // 128):
                    block = cell_ref[pl.ds(j * (SEG_TILE // 128) + q, 1), :]
                    cols.append(
                        jnp.where(cell_id == block, 0.0, w[:, q * 128 : q * 128 + 128])
                    )
                w = jnp.concatenate(cols, axis=1)
            hi = w.astype(bf16)
            lo = (w - hi.astype(f32)).astype(bf16)
            g = jnp.dot(m, hi, preferred_element_type=f32)
            g = g + jnp.dot(m, lo, preferred_element_type=f32)
            if first:
                acc[:, lanes] = g
            else:
                acc[:, lanes] += g
            return carry

        lax.fori_loop(0, nblocks * 128 // SEG_TILE, tile, 0)

    def later_chunk(k, carry):
        pltpu.make_async_copy(moments.at[k], moments.at[k], m_recv.at[k]).wait()
        far_chunk(k, False)
        return carry

    far_chunk(0, True)
    lax.fori_loop(1, 3, later_chunk, 0)
    arrived(0, sub)
    arrived(2, sub)
    for slot in (0, 2):
        for k in (1, 3, 2, 0):
            spread(slot, k).start()
    lax.fori_loop(3, 6, later_chunk, 0)
    for k in (1, 3, 2):
        arrived(1, (z + k) % 4 * 2 + core)
        relay(1, k).start()
    lax.fori_loop(6, 13, later_chunk, 0)
    for slot in (0, 2):
        for k in (1, 3, 2):
            arrived(slot, (z + k) % 4 * 2 + core)
            relay(slot, k).start()
    lax.fori_loop(13, 16, later_chunk, 0)

    grid = acc[0:9, :] + acc[16:25, :]
    line = flat[8:11, :]
    for a in range(3):
        row = jnp.sum(grid[3 * a : 3 * a + 3, :] * line, axis=0, keepdims=True)
        for g in range(nblocks):
            far_ref[g, a : a + 1, :] = row[:, g * 128 : g * 128 + 128]

    other = 1 - core
    for slot in range(3):
        for k in range(4):
            arrived(slot, (z + k) % 4 * 2 + other)
    own_copy.wait()
    right.wait_send()
    left.wait_send()
    for slot in range(3):
        for k in range(4):
            spread(slot, k).wait_send()
        for k in range(1, 4):
            relay(slot, k).wait_send()

    def end_part(k, c):
        part_copy(k).wait_send()
        return c

    def end_moment(k, c):
        moment_copy(k).wait_send()
        return c

    lax.fori_loop(1, 8, end_part, 0)
    lax.fori_loop(1, 16, end_moment, 0)


def near_kernel(win_ref, place_ref, far_ref, out_ref, feats, arrange, acc, listed, table, sem):
    space, sub = place_ref[0], place_ref[1]
    nblocks = far_ref.shape[0]
    first_block = ((space * 8 + sub) * nblocks).astype(f32)
    row_of = lambda dev, block: dev * ROWS + 9 * block
    my_row = (8 + sub) * ROWS
    row16 = lax.broadcasted_iota(jnp.int32, (16, 128), 0)

    target = jnp.concatenate(
        [win_ref[d * ROWS + 288 : d * ROWS + 289, :] for d in range(24)]
        + [win_ref[pl.ds(my_row + 288, 1), :]], axis=0
    )
    source = jnp.concatenate(
        [win_ref[d * ROWS + 289 : d * ROWS + 290, :] for d in range(24)]
        + [win_ref[pl.ds(my_row + 289, 1), :]], axis=0
    )
    item_row = lax.broadcasted_iota(jnp.int32, (25, 128), 0)
    is_own = item_row == 24
    mine = jnp.where(is_own, target, source) - first_block
    theirs = jnp.where(is_own, source, target)
    used = (source >= 0) & (mine >= 0) & (mine < nblocks)
    owner = jnp.floor(theirs * (1.0 / 32))
    their_space = jnp.floor(owner * (1.0 / 8))
    ahead = their_space - space.astype(f32) + 1.0
    ahead = jnp.where(ahead < 0, ahead + 16.0, jnp.where(ahead >= 16, ahead - 16.0, ahead))
    dev = ahead * 8.0 + (owner - 8.0 * their_space)
    local = theirs - 32.0 * owner
    usedf = used.astype(f32)
    before = (
        lax.broadcasted_iota(jnp.int32, (128, 128), 0)
        < lax.broadcasted_iota(jnp.int32, (128, 128), 1)
    ).astype(bf16)
    rank = jnp.dot(usedf.astype(bf16), before, preferred_element_type=f32)
    sums = jnp.sum(usedf, axis=1, keepdims=True)
    above = (
        lax.broadcasted_iota(jnp.int32, (25, 25), 1)
        < lax.broadcasted_iota(jnp.int32, (25, 25), 0)
    ).astype(f32)
    starts = jnp.dot(
        above, jnp.broadcast_to(sums, (25, 128)), precision=lax.Precision.HIGHEST,
        preferred_element_type=f32,
    )
    rank = jnp.where(used, rank + starts, -1.0)
    count = jnp.sum(usedf).astype(jnp.int32)
    pad = jnp.full((128 - 25, 128), -1.0, f32)
    rank_t = jnp.transpose(jnp.concatenate([rank, pad], axis=0))
    lane = lax.broadcasted_iota(jnp.int32, (128, 128), 1).astype(f32)
    row8 = lax.broadcasted_iota(jnp.int32, (8, 128), 0)

    def fill(kr, carry):
        got = jnp.zeros((8, 128), f32)
        want = lane + (kr * 128).astype(f32)
        for r in range(25):
            hot = (rank_t[:, r : r + 1] == want).astype(bf16)
            vals = jnp.where(
                row8 == 0, dev[r : r + 1], jnp.where(row8 == 1, local[r : r + 1], mine[r : r + 1])
            )
            vals = jnp.where(row8 < 3, vals, 0.0)
            vals = jnp.where(used[r : r + 1], vals, 0.0)
            got = got + jnp.dot(vals.astype(bf16), hot, preferred_element_type=f32)
        other = got[0:1] * float(ROWS) + got[1:2] * 9.0
        rows = jnp.where(row8 == 0, other, jnp.where(row8 == 1, got[2:3], 0.0))
        listed[...] = rows.astype(jnp.int32)
        copy = pltpu.make_async_copy(listed, table.at[pl.ds(kr * 8, 8)], sem)
        copy.start()
        copy.wait()
        return carry

    lax.fori_loop(0, (count + 127) // 128, fill, 0)

    origin_col = jnp.where(
        lax.broadcasted_iota(jnp.int32, (16, 1), 0) < 3, win_ref[pl.ds(my_row, 16), 0:1], 0.0
    )

    def split_rows(x, plus):
        x = x - origin_col
        a, b, c = three(x)
        sq = jnp.sum(jnp.where(row16 < 3, x * x, 0.0), axis=0, keepdims=True) + plus
        s1, s2, s3 = three(sq)
        ext = jnp.where(
            row16 < 3, 1.0,
            jnp.where(row16 == 3, s1, jnp.where(row16 == 4, s2, jnp.where(row16 == 5, s3, 0.0))),
        )
        return x, a.astype(bf16), b.astype(bf16), c.astype(bf16), ext.astype(bf16)

    r = lax.broadcasted_iota(jnp.int32, (64, 384), 0)
    q = lax.broadcasted_iota(jnp.int32, (64, 384), 1)
    kind, col = q // 128, q % 128
    group, line = col // 16, col % 16
    mate = jnp.where(group < 3, group, jnp.where(group < 5, group - 3, 0))
    dist = (kind == 0) & (group < 6) & (line < 3) & (r == mate * 16 + line)
    extra = (kind == 0) & (group == 6) & (
        ((line < 3) & (r == 48 + 3 + line)) | ((line >= 3) & (line < 6) & (r == 48))
    )
    burg_line = (kind == 1) & (group < 6) & (line >= 3) & (line < 6) & (r == mate * 16 + line + 3)
    line_burg = (kind == 2) & (group < 6) & (line >= 6) & (line < 9) & (r == mate * 16 + line - 3)
    arrange[...] = jnp.where(
        dist, -2.0, jnp.where(extra | burg_line | line_burg, 1.0, 0.0)
    ).astype(bf16)

    def own_features(g, carry):
        _, a, b, c, ext = split_rows(win_ref[pl.ds(my_row + 9 * g, 16), :], 0.25)
        x = jnp.concatenate([a, b, c, ext], axis=0)
        f = lax.dot_general(
            x, arrange[...], (((0,), (0,)), ((), ())), preferred_element_type=f32
        )
        for kind in range(3):
            feats[g, kind * 128 : kind * 128 + 128, :] = f[
                :, kind * 128 : kind * 128 + 128
            ].astype(bf16)
        acc[g] = jnp.zeros((128, 128), f32)
        return carry

    lax.fori_loop(0, nblocks, own_features, 0)

    def items(step, carry):
        work = []
        for u in range(UNROLL):
            k = step * UNROLL + u
            kk = jnp.minimum(k, count - 1)
            alive = (k < count).astype(f32)
            other = table[kk // 128 * 8, kk % 128]
            own = table[kk // 128 * 8 + 1, kk % 128]
            _, a, b, c, ext = split_rows(win_ref[pl.ds(other, 16), :], 0.0)
            rhs = jnp.concatenate([a, a, a, b, b, c, ext, jnp.zeros((16, 128), bf16)], axis=0)
            work.append((own, alive, rhs))
        outs = []
        for own, alive, rhs in work:
            outs.append(jnp.dot(feats[own], rhs, preferred_element_type=f32))
        for (own, alive, rhs), out in zip(work, outs):
            inv = lax.rsqrt(jnp.maximum(out[0:128], 0.25))
            g = (inv * inv) * (inv * alive) * (out[128:256] * out[256:384])
            hi = g.astype(bf16)
            lo = (g - hi.astype(f32)).astype(bf16)
            both = lax.dot_general(
                jnp.concatenate([hi, lo], axis=0), rhs, (((1,), (1,)), ((), ())),
                preferred_element_type=f32,
            )
            acc[own] += both[0:128] + both[128:256]
        return carry

    lax.fori_loop(0, (count + UNROLL - 1) // UNROLL, items, 0)

    def finish(g, carry):
        t = jnp.transpose(acc[g])
        p = win_ref[pl.ds(my_row + 9 * g, 16), :] - origin_col
        gp = t[0:3] + t[48:51] + t[80:83]
        out_ref[g] = far_ref[g] + p[0:3] * t[96:97] - gp
        return carry

    lax.fori_loop(0, nblocks, finish, 0)


def on_device(seg_data, cell_of_block, cell_center, pairs, live_count):
    nblocks, _, width = seg_data.shape
    ncell = cell_center.shape[1]
    slots = pairs.shape[0]
    live = jnp.arange(slots, dtype=jnp.int32)[None, :] < live_count
    pair_rows = jnp.where(live, pairs.T, -1).astype(f32)
    pair_rows = jnp.concatenate([pair_rows, jnp.zeros((6, slots), f32)], axis=0)
    vmem = pl.BlockSpec(memory_space=pltpu.VMEM)
    dma = pltpu.SemaphoreType.DMA
    far, window = pl.pallas_call(
        exchange_and_far,
        out_shape=(
            jax.ShapeDtypeStruct((nblocks, 3, width), f32),
            jax.ShapeDtypeStruct((3, 8, ROWS, width), f32),
        ),
        in_specs=[vmem] * 4,
        out_specs=(vmem, pl.BlockSpec(memory_space=pl.ANY)),
        scratch_shapes=[
            pltpu.VMEM((ROWS, width), f32),
            pltpu.VMEM((16, nblocks * width), f32),
            pltpu.VMEM((16, ncell // 16), f32),
            pltpu.VMEM((7, 16, ncell // 16), f32),
            pltpu.VMEM((16, 16, ncell // 16), f32),
            pltpu.VMEM((ncell, 32), bf16),
            pltpu.VMEM((32, nblocks * width), bf16),
            pltpu.VMEM((32, nblocks * width), f32),
            dma((2,)), dma((3, 4)), dma((3, 3)), dma((3, 8)),
            dma((7,)), dma((7,)), dma((16,)), dma((16,)), dma,
        ],
        compiler_params=pltpu.CompilerParams(
            collective_id=0, has_side_effects=True, vmem_limit_bytes=48 << 20
        ),
    )(seg_data, cell_of_block[:, None], cell_center, pair_rows)
    place = jnp.stack([lax.axis_index("space"), lax.axis_index("sub")]).astype(jnp.int32)
    return pl.pallas_call(
        near_kernel,
        out_shape=jax.ShapeDtypeStruct((nblocks, 3, width), f32),
        in_specs=[vmem, pl.BlockSpec(memory_space=pltpu.SMEM), vmem],
        out_specs=vmem,
        scratch_shapes=[
            pltpu.VMEM((nblocks, 384, width), bf16),
            pltpu.VMEM((64, 384), bf16),
            pltpu.VMEM((nblocks, width, width), f32),
            pltpu.VMEM((8, width), jnp.int32),
            pltpu.SMEM((25 * 8, width), jnp.int32),
            pltpu.SemaphoreType.DMA,
        ],
        compiler_params=pltpu.CompilerParams(vmem_limit_bytes=48 << 20),
    )(window.reshape(24 * ROWS, width), place, far)


def solution(mesh):
    placed = (
        P(("space", "sub"), None, None),
        P(("space", "sub")),
        P(),
        P(("space", "sub"), None),
        P(("space", "sub")),
    )
    return jax.shard_map(
        on_device,
        mesh=mesh,
        in_specs=placed,
        out_specs=P(("space", "sub"), None, None),
        check_vma=False,
    )
```

```python
import functools

import jax
import jax.numpy as jnp
from jax import lax
from jax.experimental import pallas as pl
from jax.experimental.pallas import tpu as pltpu
from jax.sharding import PartitionSpec as P

MESH = pl.DeviceIdType.MESH
f32 = jnp.float32
bf16 = jnp.bfloat16
ROWS = 296
UNROLL = 8
SEG_TILE = 2048


def three(x):
    a = x.astype(bf16).astype(f32)
    r = x - a
    b = r.astype(bf16).astype(f32)
    return a, b, (r - b).astype(bf16).astype(f32)


def exchange_and_far(
    seg_hbm, cell_hbm, cc_hbm, pair_hbm, live_hbm, far_ref, win_ref,
    seg_ref, cell_row, cc_ref, pair_ref, live_ref, cell_ref,
    payload, flat, mine, parts, moments, cells_f, segs_f, acc,
    in_sem, x_send, w_send, r_send, w_recv, p_send, p_recv, m_send, m_recv, own_sem,
):
    space = lax.axis_index("space")
    sub = lax.axis_index("sub")
    z, core = sub // 2, sub % 2
    nblocks = seg_ref.shape[1]
    ncell = cc_ref.shape[1]
    per = ncell // 16

    ins = [
        pltpu.make_async_copy(src, dst, in_sem.at[i])
        for i, (src, dst) in enumerate(
            [
                (cell_hbm, cell_row), (cc_hbm, cc_ref), (seg_hbm, seg_ref),
                (pair_hbm, pair_ref), (live_hbm, live_ref),
            ]
        )
    ]
    for copy in ins:
        copy.start()
    barrier = pltpu.get_barrier_semaphore()

    def greet_sub(k, c):
        pl.semaphore_signal(
            barrier, inc=1, device_id=(space, (sub + k) % 8), device_id_type=MESH
        )
        return c

    def greet_space(k, c):
        pl.semaphore_signal(
            barrier, inc=1, device_id=((space + k) % 16, sub), device_id_type=MESH
        )
        return c

    lax.fori_loop(1, 8, greet_sub, 0)
    lax.fori_loop(1, 16, greet_space, 0)

    for copy in ins:
        copy.wait()

    base = space * per
    own_cc = cc_ref[:, pl.ds(pl.multiple_of(base, 256), per)]
    square = lax.broadcasted_iota(jnp.int32, (nblocks, nblocks), 0)
    lane = lax.broadcasted_iota(jnp.int32, (nblocks, nblocks), 1)
    cell = jnp.sum(
        jnp.where(square == lane, cell_row[...].astype(f32), 0.0), axis=1, keepdims=True
    )
    cell_ref[...] = jnp.broadcast_to(cell, (nblocks, 128)).astype(jnp.int32)
    hot = (
        cell.astype(jnp.int32) - base
        == lax.broadcasted_iota(jnp.int32, (nblocks, per), 1)
    ).astype(f32)
    origin = []
    for a in range(3):
        centre = jnp.sum(hot * own_cc[a : a + 1], axis=1, keepdims=True)
        origin.append(centre[0:1])
        payload[pl.ds(a, nblocks, stride=9), :] = seg_ref[a] + centre
    for a in range(3, 9):
        payload[pl.ds(a, nblocks, stride=9), :] = seg_ref[a]
    alive = lax.broadcasted_iota(jnp.int32, (2, 128), 1) < live_ref[...]
    payload[288:290, :] = jnp.where(alive, pair_ref[...].astype(f32), -1.0)
    payload[290:296, :] = jnp.zeros((6, 128), f32)
    for a in range(3):
        for b in range(3):
            outer = jnp.sum(seg_ref[6 + a] * seg_ref[3 + b], axis=1, keepdims=True)
            mine[3 * a + b : 3 * a + b + 1, :] = jnp.sum(hot * outer, axis=0, keepdims=True)
    mine[9:16, :] = jnp.zeros((7, per), f32)

    pl.semaphore_wait(barrier, 22)

    def part_copy(k):
        to = (sub + k) % 8
        return pltpu.make_async_remote_copy(
            src_ref=mine, dst_ref=parts.at[7 - k],
            send_sem=p_send.at[k - 1], recv_sem=p_recv.at[7 - k],
            device_id=(space, to), device_id_type=MESH,
        )


    def start_part(k, c):
        part_copy(k).start()
        return c

    lax.fori_loop(1, 8, start_part, 0)

    def beside(step, slot, sem):
        return pltpu.make_async_remote_copy(
            src_ref=payload, dst_ref=win_ref.at[slot, sub],
            send_sem=x_send.at[sem], recv_sem=w_recv.at[slot, sub],
            device_id=((space + step) % 16, sub), device_id_type=MESH,
        )

    right, left = beside(1, 0, 0), beside(15, 2, 1)
    right.start()
    left.start()
    own_copy = pltpu.make_async_copy(payload, win_ref.at[1, sub], own_sem)
    own_copy.start()

    def spread(slot, k):
        src = payload if slot == 1 else win_ref.at[slot, sub]
        if k == 0:
            to = z * 2 + 1 - core
        else:
            to = (z + k) % 4 * 2 + core
        return pltpu.make_async_remote_copy(
            src_ref=src, dst_ref=win_ref.at[slot, sub],
            send_sem=w_send.at[slot, k], recv_sem=w_recv.at[slot, sub],
            device_id=(space, to), device_id_type=MESH,
        )

    def arrived(slot, place):
        pltpu.make_async_copy(
            win_ref.at[slot, place], win_ref.at[slot, place], w_recv.at[slot, place]
        ).wait()

    def relay(slot, k):
        place = (z + k) % 4 * 2 + core
        return pltpu.make_async_remote_copy(
            src_ref=win_ref.at[slot, place], dst_ref=win_ref.at[slot, place],
            send_sem=r_send.at[slot, k - 1], recv_sem=w_recv.at[slot, place],
            device_id=(space, z * 2 + 1 - core), device_id_type=MESH,
        )

    for k in (1, 3, 2, 0):
        spread(1, k).start()

    for g in range(nblocks):
        lanes = slice(g * 128, g * 128 + 128)
        flat[0:3, lanes] = payload[9 * g : 9 * g + 3, :]
        flat[8:11, lanes] = payload[9 * g + 3 : 9 * g + 6, :]
    row3 = lax.broadcasted_iota(jnp.int32, (3, 1), 0)
    origin = jnp.where(row3 == 0, origin[0], jnp.where(row3 == 1, origin[1], origin[2]))
    ones = jnp.ones((3, ncell), f32)
    blank = jnp.zeros((8, ncell), f32)
    c = cc_ref[...] - origin
    c1, c2, c3 = three(c)
    cq = jnp.concatenate(three(jnp.sum(c * c, axis=0, keepdims=True)), axis=0)
    cells_f[...] = jnp.transpose(
        jnp.concatenate([c1, c1, c2, c2, c1, c3, cq, ones, blank], axis=0)
    ).astype(bf16)
    p = flat[0:3, :] - origin
    p1, p2, p3 = three(-2.0 * p)
    pq = jnp.concatenate(three(1.0 + jnp.sum(p * p, axis=0, keepdims=True)), axis=0)
    segs_f[...] = jnp.concatenate(
        [p1, p2, p1, p2, p3, p1, ones, pq, blank], axis=0
    ).astype(bf16)

    region = mine[...]
    for k in range(7):
        pltpu.make_async_copy(parts.at[k], parts.at[k], p_recv.at[k]).wait()
        region = region + parts[k]
    moments[0] = region

    def moment_copy(k):
        return pltpu.make_async_remote_copy(
            src_ref=moments.at[0], dst_ref=moments.at[16 - k],
            send_sem=m_send.at[k], recv_sem=m_recv.at[16 - k],
            device_id=((space + k) % 16, sub), device_id_type=MESH,
        )

    def start_moment(k, c):
        moment_copy(k).start()
        return c

    lax.fori_loop(1, 16, start_moment, 0)

    def split_moments(k):
        m = moments[k]
        hi = m.astype(bf16)
        return jnp.concatenate([hi, (m - hi.astype(f32)).astype(bf16)], axis=0)

    def far_chunk(k, first):
        at = pl.multiple_of((space + k) % 16 * per, 256)
        cells = cells_f[pl.ds(at, per), :]
        m = split_moments(k)
        cell_id = at + lax.broadcasted_iota(jnp.int32, (per, 128), 0)

        def tile(j, carry):
            lanes = pl.ds(pl.multiple_of(j * SEG_TILE, SEG_TILE), SEG_TILE)
            d = jnp.dot(cells, segs_f[:, lanes], preferred_element_type=f32)
            w = pl.reciprocal(d, approx=True)
            if first:
                cols = []
                for q in range(SEG_TILE // 128):
                    block = cell_ref[pl.ds(j * (SEG_TILE // 128) + q, 1), :]
                    cols.append(
                        jnp.where(cell_id == block, 0.0, w[:, q * 128 : q * 128 + 128])
                    )
                w = jnp.concatenate(cols, axis=1)
            hi = w.astype(bf16)
            lo = (w - hi.astype(f32)).astype(bf16)
            g = jnp.dot(m, hi, preferred_element_type=f32)
            g = g + jnp.dot(m, lo, preferred_element_type=f32)
            if first:
                acc[:, lanes] = g
            else:
                acc[:, lanes] += g
            return carry

        lax.fori_loop(0, nblocks * 128 // SEG_TILE, tile, 0)

    def later_chunk(k, carry):
        pltpu.make_async_copy(moments.at[k], moments.at[k], m_recv.at[k]).wait()
        far_chunk(k, False)
        return carry

    far_chunk(0, True)
    lax.fori_loop(1, 3, later_chunk, 0)
    arrived(0, sub)
    arrived(2, sub)
    for slot in (0, 2):
        for k in (1, 3, 2, 0):
            spread(slot, k).start()
    lax.fori_loop(3, 6, later_chunk, 0)
    for k in (1, 3, 2):
        arrived(1, (z + k) % 4 * 2 + core)
        relay(1, k).start()
    lax.fori_loop(6, 13, later_chunk, 0)
    for slot in (0, 2):
        for k in (1, 3, 2):
            arrived(slot, (z + k) % 4 * 2 + core)
            relay(slot, k).start()
    lax.fori_loop(13, 16, later_chunk, 0)

    grid = acc[0:9, :] + acc[16:25, :]
    line = flat[8:11, :]
    for a in range(3):
        far_ref[a : a + 1, :] = jnp.sum(
            grid[3 * a : 3 * a + 3, :] * line, axis=0, keepdims=True
        )

    other = 1 - core
    for slot in range(3):
        for k in range(4):
            arrived(slot, (z + k) % 4 * 2 + other)
    own_copy.wait()
    right.wait_send()
    left.wait_send()
    for slot in range(3):
        for k in range(4):
            spread(slot, k).wait_send()
        for k in range(1, 4):
            relay(slot, k).wait_send()

    def end_part(k, c):
        part_copy(k).wait_send()
        return c

    def end_moment(k, c):
        moment_copy(k).wait_send()
        return c

    lax.fori_loop(1, 8, end_part, 0)
    lax.fori_loop(1, 16, end_moment, 0)


def arrangement():
    r = lax.broadcasted_iota(jnp.int32, (64, 384), 0)
    q = lax.broadcasted_iota(jnp.int32, (64, 384), 1)
    kind, col = q // 128, q % 128
    group, line = col // 16, col % 16
    mate = jnp.where(group < 3, group, jnp.where(group < 5, group - 3, 0))
    dist = (kind == 0) & (group < 6) & (line < 3) & (r == mate * 16 + line)
    extra = (kind == 0) & (group == 6) & (
        ((line < 3) & (r == 48 + 3 + line)) | ((line >= 3) & (line < 6) & (r == 48))
    )
    burg_line = (kind == 1) & (group < 6) & (line >= 3) & (line < 6) & (r == mate * 16 + line + 3)
    line_burg = (kind == 2) & (group < 6) & (line >= 6) & (line < 9) & (r == mate * 16 + line - 3)
    return jnp.where(
        dist, -2.0, jnp.where(extra | burg_line | line_burg, 1.0, 0.0)
    ).astype(bf16)


def split_rows(x, plus):
    row16 = lax.broadcasted_iota(jnp.int32, (16, 128), 0)
    a, b, c = three(x)
    sq = jnp.sum(jnp.where(row16 < 3, x * x, 0.0), axis=0, keepdims=True) + plus
    s1, s2, s3 = three(sq)
    ext = jnp.where(
        row16 < 3, 1.0,
        jnp.where(row16 == 3, s1, jnp.where(row16 == 4, s2, jnp.where(row16 == 5, s3, 0.0))),
    )
    return a.astype(bf16), b.astype(bf16), c.astype(bf16), ext.astype(bf16)


def build_list(win_ref, space, sub, nblocks, hots, listed, table, sem):
    my_row = (8 + sub) * ROWS
    first_block = ((space * 8 + sub) * nblocks).astype(f32)
    target = jnp.concatenate(
        [win_ref[d * ROWS + 288 : d * ROWS + 289, :] for d in range(24)]
        + [win_ref[pl.ds(my_row + 288, 1), :]], axis=0
    )
    source = jnp.concatenate(
        [win_ref[d * ROWS + 289 : d * ROWS + 290, :] for d in range(24)]
        + [win_ref[pl.ds(my_row + 289, 1), :]], axis=0
    )
    is_own = lax.broadcasted_iota(jnp.int32, (25, 128), 0) == 24
    mine = jnp.where(is_own, target, source) - first_block
    theirs = jnp.where(is_own, source, target)
    used = (source >= 0) & (mine >= 0) & (mine < nblocks)
    mine = jnp.where(used, mine, -1.0)
    owner = jnp.floor(theirs * (1.0 / 32))
    their_space = jnp.floor(owner * (1.0 / 8))
    ahead = their_space - space.astype(f32) + 1.0
    ahead = jnp.where(ahead < 0, ahead + 16.0, jnp.where(ahead >= 16, ahead - 16.0, ahead))
    dev = ahead * 8.0 + (owner - 8.0 * their_space)
    local = theirs - 32.0 * owner
    before = (
        lax.broadcasted_iota(jnp.int32, (128, 128), 0)
        < lax.broadcasted_iota(jnp.int32, (128, 128), 1)
    ).astype(bf16)
    block_id = lax.broadcasted_iota(jnp.int32, (32, 128), 0).astype(f32)
    run = jnp.zeros((32, 1), f32)
    hots[...] = jnp.concatenate(
        [(mine[r : r + 1] == block_id).astype(f32) for r in range(25)], axis=0
    )
    within = jnp.dot(hots[...].astype(bf16), before, preferred_element_type=f32)
    sums = jnp.sum(hots[...], axis=1, keepdims=True)
    runs = []
    for r in range(25):
        runs.append(run)
        run = run + sums[32 * r : 32 * r + 32]
    even = 2.0 * jnp.floor((run + 1.0) * 0.5)
    above = (
        lax.broadcasted_iota(jnp.int32, (32, 32), 1)
        < lax.broadcasted_iota(jnp.int32, (32, 32), 0)
    ).astype(f32)
    starts = jnp.dot(
        above, jnp.broadcast_to(even, (32, 128)), precision=lax.Precision.HIGHEST,
        preferred_element_type=f32,
    )[:, 0:1]
    count = jnp.sum(even).astype(jnp.int32)
    ranks = []
    for r in range(25):
        h = hots[32 * r : 32 * r + 32, :]
        at = within[32 * r : 32 * r + 32] + (runs[r] + starts)
        ranks.append(jnp.sum(h * at, axis=0, keepdims=True))
    rank = jnp.where(used, jnp.concatenate(ranks, axis=0), -1.0)
    pad = jnp.full((128 - 25, 128), -1.0, f32)
    rank_t = jnp.transpose(jnp.concatenate([rank, pad], axis=0))
    lane = lax.broadcasted_iota(jnp.int32, (128, 128), 1).astype(f32)
    row8 = lax.broadcasted_iota(jnp.int32, (8, 128), 0)
    ends = starts + even

    def fill(kr, carry):
        got = jnp.zeros((8, 128), f32)
        first = (kr * 128).astype(f32)
        want = lane + first
        for r in range(25):
            hot = (rank_t[:, r : r + 1] == want).astype(bf16)
            vals = jnp.where(row8 == 0, dev[r : r + 1], jnp.where(row8 == 1, local[r : r + 1], 1.0))
            vals = jnp.where((row8 < 3) & used[r : r + 1], vals, 0.0)
            got = got + jnp.dot(vals.astype(bf16), hot, preferred_element_type=f32)
        other = got[0:1] * float(ROWS) + got[1:2] * 9.0
        own = jnp.sum((ends <= want[0:32]).astype(f32), axis=0, keepdims=True)
        own = jnp.minimum(own, 31.0)
        rows = jnp.where(
            row8 == 0, other, jnp.where(row8 == 1, own, jnp.where(row8 == 2, got[2:3], 0.0))
        )
        listed[...] = rows.astype(jnp.int32)
        copy = pltpu.make_async_copy(listed, table.at[pl.ds(kr * 8, 8)], sem)
        copy.start()
        copy.wait()
        return carry

    lax.fori_loop(0, (count + 127) // 128, fill, 0)
    return count


def near_kernel(win_ref, far_ref, out_ref, feats, arrange, acc, hots, listed, table, sem):
    space, sub = lax.axis_index("space"), lax.axis_index("sub")
    nblocks = out_ref.shape[1]
    my_row = (8 + sub) * ROWS
    origin = jnp.where(
        lax.broadcasted_iota(jnp.int32, (16, 1), 0) < 3, win_ref[pl.ds(my_row, 16), 0:1], 0.0
    )
    count = build_list(win_ref, space, sub, nblocks, hots, listed, table, sem)

    arrange[...] = arrangement()
    acc[...] = jnp.zeros_like(acc)
    for q in range(0, nblocks, 8):
        x = jnp.concatenate(
            [
                jnp.concatenate(
                    split_rows(win_ref[pl.ds(my_row + 9 * g, 16), :] - origin, 0.25), axis=0
                )
                for g in range(q, q + 8)
            ],
            axis=1,
        )
        f = lax.dot_general(
            x, arrange[...], (((0,), (0,)), ((), ())), preferred_element_type=f32
        )
        feats[q * 128 : q * 128 + 1024, :] = f.astype(bf16)

    half = lax.broadcasted_iota(jnp.int32, (1, 256), 1) < 128
    top = lax.broadcasted_iota(jnp.int32, (16, 128), 0) < 3

    def items(step, carry):
        work = []
        for u in range(UNROLL):
            k = (step * UNROLL + u) * 2
            inside = k < count
            k = jnp.minimum(k, count - 2)
            row = k // 128 * 8
            col = k % 128
            own = table[row + 1, col]
            rhs = []
            alive = []
            for v in range(2):
                other = table[row, col + v]
                alive.append(jnp.where(inside, table[row + 2, col + v], 0).astype(f32))
                a, b, c, ext = split_rows(win_ref[pl.ds(other, 16), :] - origin, 0.0)
                rhs.append(
                    jnp.concatenate(
                        [a, a, a, b, b, c, ext, jnp.zeros((16, 128), bf16)], axis=0
                    )
                )
            f = feats[pl.ds(pl.multiple_of(own * 128, 128), 128), :]
            f = jnp.concatenate([f[:, 0:128], f[:, 128:256], f[:, 256:384]], axis=0)
            work.append((own, jnp.where(half, alive[0], alive[1]), f, jnp.concatenate(rhs, axis=1)))
        outs = [jnp.dot(f, rhs, preferred_element_type=f32) for _, _, f, rhs in work]
        sums = []
        for (own, live, _, rhs), out in zip(work, outs):
            inv = lax.rsqrt(jnp.maximum(out[0:128], 0.25))
            g = (inv * inv) * (inv * live) * (out[128:256] * out[256:384])
            hi = g.astype(bf16)
            lo = (g - hi.astype(f32)).astype(bf16)
            lhs = jnp.concatenate([rhs[0:16], rhs[48:64], rhs[80:112]], axis=0)
            dims = (((1,), (1,)), ((), ()))
            r = lax.dot_general(lhs, hi, dims, preferred_element_type=f32)
            r = r + lax.dot_general(lhs, lo, dims, preferred_element_type=f32)
            sums.append((own, jnp.where(top, r[0:16] + r[16:32] + r[32:48], r[48:49])))
        for own, r in sums:
            acc[own] += r
        return carry

    lax.fori_loop(0, (count // 2 + UNROLL - 1) // UNROLL, items, 0)

    for g in range(nblocks):
        p = win_ref[pl.ds(my_row + 9 * g, 16), :] - origin
        t = acc[g]
        force = far_ref[0:3, g * 128 : g * 128 + 128] + p[0:3] * t[3:4] - t[0:3]
        for a in range(3):
            out_ref[a, g : g + 1, :] = force[a : a + 1]


def on_device(seg_data, cell_of_block, cell_center, pairs, live_count):
    nblocks, _, width = seg_data.shape
    ncell = cell_center.shape[1]
    slots = pairs.shape[0]
    vmem = pl.BlockSpec(memory_space=pltpu.VMEM)
    hbm = pl.BlockSpec(memory_space=pltpu.HBM)
    dma = pltpu.SemaphoreType.DMA
    far, window = pl.pallas_call(
        exchange_and_far,
        out_shape=(
            jax.ShapeDtypeStruct((3, nblocks * width), f32),
            jax.ShapeDtypeStruct((3, 8, ROWS, width), f32),
        ),
        in_specs=[hbm] * 5,
        out_specs=(vmem, vmem),
        scratch_shapes=[
            pltpu.VMEM((9, nblocks, width), f32),
            pltpu.VMEM((1, nblocks), jnp.int32),
            pltpu.VMEM((3, ncell), f32),
            pltpu.VMEM((2, slots), jnp.int32),
            pltpu.VMEM((1, 1), jnp.int32),
            pltpu.VMEM((nblocks, width), jnp.int32),
            pltpu.VMEM((ROWS, width), f32),
            pltpu.VMEM((16, nblocks * width), f32),
            pltpu.VMEM((16, ncell // 16), f32),
            pltpu.VMEM((7, 16, ncell // 16), f32),
            pltpu.VMEM((16, 16, ncell // 16), f32),
            pltpu.VMEM((ncell, 32), bf16),
            pltpu.VMEM((32, nblocks * width), bf16),
            pltpu.VMEM((32, nblocks * width), f32),
            dma((5,)), dma((2,)), dma((3, 4)), dma((3, 3)), dma((3, 8)),
            dma((7,)), dma((7,)), dma((16,)), dma((16,)), dma,
        ],
        compiler_params=pltpu.CompilerParams(
            collective_id=0, has_side_effects=True, vmem_limit_bytes=28 << 20
        ),
    )(
        seg_data.transpose(1, 0, 2), cell_of_block[None, :], cell_center, pairs.T,
        live_count[None, :],
    )
    force = pl.pallas_call(
        near_kernel,
        out_shape=jax.ShapeDtypeStruct((3, nblocks, width), f32),
        in_specs=[vmem, vmem],
        out_specs=vmem,
        scratch_shapes=[
            pltpu.VMEM((nblocks * width, 384), bf16),
            pltpu.VMEM((64, 384), bf16),
            pltpu.VMEM((nblocks, 16, width), f32),
            pltpu.VMEM((25 * 32, width), f32),
            pltpu.VMEM((8, width), jnp.int32),
            pltpu.SMEM((26 * 8, width), jnp.int32),
            pltpu.SemaphoreType.DMA,
        ],
        compiler_params=pltpu.CompilerParams(vmem_limit_bytes=28 << 20),
    )(window.reshape(24 * ROWS, width), far)
    return force.transpose(1, 0, 2)


def solution(mesh):
    placed = (
        P(("space", "sub"), None, None),
        P(("space", "sub")),
        P(),
        P(("space", "sub"), None),
        P(("space", "sub")),
    )
    return jax.shard_map(
        on_device,
        mesh=mesh,
        in_specs=placed,
        out_specs=P(("space", "sub"), None, None),
        check_vma=False,
    )
```

```python
import functools

import jax
import jax.numpy as jnp
from jax import lax
from jax.experimental import pallas as pl
from jax.experimental.pallas import tpu as pltpu
from jax.sharding import PartitionSpec as P

MESH = pl.DeviceIdType.MESH
f32 = jnp.float32
bf16 = jnp.bfloat16
ROWS = 296
UNROLL = 8
EARLY = 3


def three(x):
    a = x.astype(bf16).astype(f32)
    r = x - a
    b = r.astype(bf16).astype(f32)
    return a, b, (r - b).astype(bf16).astype(f32)


def exchange_and_far(
    seg_hbm, cell_hbm, cc_hbm, pair_hbm, live_hbm, far_hbm, win_ref,
    seg_ref, cell_row, cc_ref, pair_ref, live_ref, cell_ref,
    payload, flat, mine, parts, moments, cells_f, segs_f, acc, early, far_ref,
    in_sem, x_send, w_send, r_send, w_recv, p_send, p_recv, m_send, m_recv, own_sem, far_sem,
):
    space = lax.axis_index("space")
    sub = lax.axis_index("sub")
    z, core = sub // 2, sub % 2
    nblocks = seg_ref.shape[1]
    ncell = cc_ref.shape[1]
    per = ncell // 16

    ins = [
        pltpu.make_async_copy(src, dst, in_sem.at[i])
        for i, (src, dst) in enumerate(
            [
                (cell_hbm, cell_row), (cc_hbm, cc_ref), (seg_hbm, seg_ref),
                (pair_hbm, pair_ref), (live_hbm, live_ref),
            ]
        )
    ]
    for copy in ins:
        copy.start()
    barrier = pltpu.get_barrier_semaphore()

    def greet_sub(k, c):
        pl.semaphore_signal(
            barrier, inc=1, device_id=(space, (sub + k) % 8), device_id_type=MESH
        )
        return c

    def greet_space(k, c):
        pl.semaphore_signal(
            barrier, inc=1, device_id=((space + k) % 16, sub), device_id_type=MESH
        )
        return c

    lax.fori_loop(1, 8, greet_sub, 0)
    lax.fori_loop(1, 16, greet_space, 0)

    for copy in ins:
        copy.wait()

    base = space * per
    own_cc = cc_ref[:, pl.ds(pl.multiple_of(base, 256), per)]
    square = lax.broadcasted_iota(jnp.int32, (nblocks, nblocks), 0)
    lane = lax.broadcasted_iota(jnp.int32, (nblocks, nblocks), 1)
    cell = jnp.sum(
        jnp.where(square == lane, cell_row[...].astype(f32), 0.0), axis=1, keepdims=True
    )
    cell_ref[...] = jnp.broadcast_to(cell, (nblocks, 128)).astype(jnp.int32)
    hot = (
        cell.astype(jnp.int32) - base
        == lax.broadcasted_iota(jnp.int32, (nblocks, per), 1)
    ).astype(f32)
    origin = []
    for a in range(3):
        centre = jnp.sum(hot * own_cc[a : a + 1], axis=1, keepdims=True)
        origin.append(centre[0:1])
        payload[pl.ds(a, nblocks, stride=9), :] = seg_ref[a] + centre
    for a in range(3, 9):
        payload[pl.ds(a, nblocks, stride=9), :] = seg_ref[a]
    alive = lax.broadcasted_iota(jnp.int32, (2, 128), 1) < live_ref[...]
    payload[288:290, :] = jnp.where(alive, pair_ref[...].astype(f32), -1.0)
    payload[290:296, :] = jnp.zeros((6, 128), f32)
    for a in range(3):
        for b in range(3):
            outer = jnp.sum(seg_ref[6 + a] * seg_ref[3 + b], axis=1, keepdims=True)
            mine[3 * a + b : 3 * a + b + 1, :] = jnp.sum(hot * outer, axis=0, keepdims=True)
    mine[9:16, :] = jnp.zeros((7, per), f32)

    pl.semaphore_wait(barrier, 22)

    def part_copy(k):
        to = (sub + k) % 8
        return pltpu.make_async_remote_copy(
            src_ref=mine, dst_ref=parts.at[7 - k],
            send_sem=p_send.at[k - 1], recv_sem=p_recv.at[7 - k],
            device_id=(space, to), device_id_type=MESH,
        )


    def start_part(k, c):
        part_copy(k).start()
        return c

    lax.fori_loop(1, 8, start_part, 0)

    def beside(step, slot, sem):
        return pltpu.make_async_remote_copy(
            src_ref=payload, dst_ref=win_ref.at[slot, sub],
            send_sem=x_send.at[sem], recv_sem=w_recv.at[slot, sub],
            device_id=((space + step) % 16, sub), device_id_type=MESH,
        )

    right, left = beside(1, 0, 0), beside(15, 2, 1)
    right.start()
    left.start()
    own_copy = pltpu.make_async_copy(payload, win_ref.at[1, sub], own_sem)
    own_copy.start()

    def spread(slot, k):
        src = payload if slot == 1 else win_ref.at[slot, sub]
        if k == 0:
            to = z * 2 + 1 - core
        else:
            to = (z + k) % 4 * 2 + core
        return pltpu.make_async_remote_copy(
            src_ref=src, dst_ref=win_ref.at[slot, sub],
            send_sem=w_send.at[slot, k], recv_sem=w_recv.at[slot, sub],
            device_id=(space, to), device_id_type=MESH,
        )

    def arrived(slot, place):
        pltpu.make_async_copy(
            win_ref.at[slot, place], win_ref.at[slot, place], w_recv.at[slot, place]
        ).wait()

    def relay(slot, k):
        place = (z + k) % 4 * 2 + core
        return pltpu.make_async_remote_copy(
            src_ref=win_ref.at[slot, place], dst_ref=win_ref.at[slot, place],
            send_sem=r_send.at[slot, k - 1], recv_sem=w_recv.at[slot, place],
            device_id=(space, z * 2 + 1 - core), device_id_type=MESH,
        )

    def forward(slot):
        step = 1 + 2 * core
        place = (z + 4 - step) % 4 * 2 + core
        return pltpu.make_async_remote_copy(
            src_ref=win_ref.at[slot, place], dst_ref=win_ref.at[slot, place],
            send_sem=w_send.at[slot, 2], recv_sem=w_recv.at[slot, place],
            device_id=(space, (z + step) % 4 * 2 + core), device_id_type=MESH,
        )

    for k in (1, 3, 0):
        spread(1, k).start()

    for g in range(nblocks):
        lanes = slice(g * 128, g * 128 + 128)
        flat[0:3, lanes] = payload[9 * g : 9 * g + 3, :]
        flat[8:11, lanes] = payload[9 * g + 3 : 9 * g + 6, :]
    row3 = lax.broadcasted_iota(jnp.int32, (3, 1), 0)
    origin = jnp.where(row3 == 0, origin[0], jnp.where(row3 == 1, origin[1], origin[2]))
    ones = jnp.ones((3, ncell), f32)
    blank = jnp.zeros((8, ncell), f32)
    c = cc_ref[...] - origin
    c1, c2, c3 = three(c)
    cq = jnp.concatenate(three(jnp.sum(c * c, axis=0, keepdims=True)), axis=0)
    cells_f[...] = jnp.transpose(
        jnp.concatenate([c1, c1, c2, c2, c1, c3, cq, ones, blank], axis=0)
    ).astype(bf16)
    p = flat[0:3, :] - origin
    p1, p2, p3 = three(-2.0 * p)
    pq = jnp.concatenate(three(1.0 + jnp.sum(p * p, axis=0, keepdims=True)), axis=0)
    segs_f[...] = jnp.concatenate(
        [p1, p2, p1, p2, p3, p1, ones, pq, blank], axis=0
    ).astype(bf16)

    def split_moments(k):
        m = moments[k]
        hi = m.astype(bf16)
        return jnp.concatenate([hi, (m - hi.astype(f32)).astype(bf16)], axis=0)

    def weights(k, first):
        at = pl.multiple_of((space + k) % 16 * per, 256)
        dist = jnp.dot(cells_f[pl.ds(at, per), :], segs_f[...], preferred_element_type=f32)
        w = pl.reciprocal(dist, approx=True)
        if first:
            cell_id = at + lax.broadcasted_iota(jnp.int32, (per, 128), 0)
            w = jnp.concatenate(
                [
                    jnp.where(
                        cell_id == cell_ref[g : g + 1, :], 0.0, w[:, g * 128 : g * 128 + 128]
                    )
                    for g in range(nblocks)
                ],
                axis=1,
            )
        hi = w.astype(bf16)
        return hi, (w - hi.astype(f32)).astype(bf16)

    def product(k, hi, lo):
        m = split_moments(k)
        return jnp.dot(m, hi, preferred_element_type=f32) + jnp.dot(
            m, lo, preferred_element_type=f32
        )

    early[0, 0], early[0, 1] = weights(0, True)

    region = mine[...]
    for k in range(7):
        pltpu.make_async_copy(parts.at[k], parts.at[k], p_recv.at[k]).wait()
        region = region + parts[k]
    moments[0] = region

    def moment_copy(k):
        return pltpu.make_async_remote_copy(
            src_ref=moments.at[0], dst_ref=moments.at[16 - k],
            send_sem=m_send.at[k], recv_sem=m_recv.at[16 - k],
            device_id=((space + k) % 16, sub), device_id_type=MESH,
        )

    def start_moment(k, c):
        moment_copy(k).start()
        return c

    lax.fori_loop(1, 16, start_moment, 0)

    for k in range(1, EARLY):
        early[k, 0], early[k, 1] = weights(k, False)
    acc[...] = product(0, early[0, 0], early[0, 1])

    def moments_here(k):
        pltpu.make_async_copy(moments.at[k], moments.at[k], m_recv.at[k]).wait()

    def later_chunk(k, carry):
        moments_here(k)
        hi, lo = weights(k, False)
        acc[...] += product(k, hi, lo)
        return carry

    def chip(k):
        return (z + k) % 4 * 2 + core

    for slot in (0, 2):
        arrived(slot, sub)
        for k in (1, 3, 0):
            spread(slot, k).start()
    for k in range(1, EARLY):
        moments_here(k)
        acc[...] += product(k, early[k, 0], early[k, 1])
    for k in (1, 3):
        arrived(1, chip(k))
    forward(1).start()
    for k in (1, 3):
        relay(1, k).start()
    lax.fori_loop(EARLY, 8, later_chunk, 0)
    for slot in (0, 2):
        for k in (1, 3):
            arrived(slot, chip(k))
        forward(slot).start()
        for k in (1, 3):
            relay(slot, k).start()
    lax.fori_loop(8, 11, later_chunk, 0)
    for slot in range(3):
        arrived(slot, chip(2))
        relay(slot, 2).start()
    lax.fori_loop(11, 16, later_chunk, 0)

    grid = acc[0:9, :] + acc[16:25, :]
    line = flat[8:11, :]
    for a in range(3):
        far_ref[a : a + 1, :] = jnp.sum(
            grid[3 * a : 3 * a + 3, :] * line, axis=0, keepdims=True
        )

    far_copy = pltpu.make_async_copy(far_ref, far_hbm, far_sem)
    far_copy.start()

    other = 1 - core
    for slot in range(3):
        for k in range(4):
            arrived(slot, (z + k) % 4 * 2 + other)
    own_copy.wait()
    far_copy.wait()
    right.wait_send()
    left.wait_send()
    for slot in range(3):
        for k in (0, 1, 3):
            spread(slot, k).wait_send()
        forward(slot).wait_send()
        for k in range(1, 4):
            relay(slot, k).wait_send()

    def end_part(k, c):
        part_copy(k).wait_send()
        return c

    def end_moment(k, c):
        moment_copy(k).wait_send()
        return c

    lax.fori_loop(1, 8, end_part, 0)
    lax.fori_loop(1, 16, end_moment, 0)


def arrangement():
    r = lax.broadcasted_iota(jnp.int32, (64, 384), 0)
    q = lax.broadcasted_iota(jnp.int32, (64, 384), 1)
    kind, col = q // 128, q % 128
    group, line = col // 16, col % 16
    mate = jnp.where(group < 3, group, jnp.where(group < 5, group - 3, 0))
    dist = (kind == 0) & (group < 6) & (line < 3) & (r == mate * 16 + line)
    extra = (kind == 0) & (group == 6) & (
        ((line < 3) & (r == 48 + 3 + line)) | ((line >= 3) & (line < 6) & (r == 48))
    )
    burg_line = (kind == 1) & (group < 6) & (line >= 3) & (line < 6) & (r == mate * 16 + line + 3)
    line_burg = (kind == 2) & (group < 6) & (line >= 6) & (line < 9) & (r == mate * 16 + line - 3)
    return jnp.where(
        dist, -2.0, jnp.where(extra | burg_line | line_burg, 1.0, 0.0)
    ).astype(bf16)


def split_rows(x, plus):
    row16 = lax.broadcasted_iota(jnp.int32, (16, 128), 0)
    a, b, c = three(x)
    sq = jnp.sum(jnp.where(row16 < 3, x * x, 0.0), axis=0, keepdims=True) + plus
    s1, s2, s3 = three(sq)
    ext = jnp.where(
        row16 < 3, 1.0,
        jnp.where(row16 == 3, s1, jnp.where(row16 == 4, s2, jnp.where(row16 == 5, s3, 0.0))),
    )
    return a.astype(bf16), b.astype(bf16), c.astype(bf16), ext.astype(bf16)


def build_list(pair_ref, space, sub, nblocks, hots, listed, table, sem):
    first_block = ((space * 8 + sub) * nblocks).astype(f32)
    target = jnp.concatenate(
        [pair_ref[d, 0:1, :] for d in range(24)] + [pair_ref[8 + sub, 0:1, :]],
        axis=0,
    )
    source = jnp.concatenate(
        [pair_ref[d, 1:2, :] for d in range(24)] + [pair_ref[8 + sub, 1:2, :]],
        axis=0,
    )
    is_own = lax.broadcasted_iota(jnp.int32, (25, 128), 0) == 24
    mine = jnp.where(is_own, target, source) - first_block
    theirs = jnp.where(is_own, source, target)
    used = (source >= 0) & (mine >= 0) & (mine < nblocks)
    mine = jnp.where(used, mine, -1.0)
    owner = jnp.floor(theirs * (1.0 / 32))
    their_space = jnp.floor(owner * (1.0 / 8))
    ahead = their_space - space.astype(f32) + 1.0
    ahead = jnp.where(ahead < 0, ahead + 16.0, jnp.where(ahead >= 16, ahead - 16.0, ahead))
    dev = ahead * 8.0 + (owner - 8.0 * their_space)
    local = theirs - 32.0 * owner
    before = (
        lax.broadcasted_iota(jnp.int32, (128, 128), 0)
        < lax.broadcasted_iota(jnp.int32, (128, 128), 1)
    ).astype(bf16)
    block_id = lax.broadcasted_iota(jnp.int32, (32, 128), 0).astype(f32)
    run = jnp.zeros((32, 1), f32)
    hots[...] = jnp.concatenate(
        [(mine[r : r + 1] == block_id).astype(f32) for r in range(25)], axis=0
    )
    within = jnp.dot(hots[...].astype(bf16), before, preferred_element_type=f32)
    sums = jnp.sum(hots[...], axis=1, keepdims=True)
    runs = []
    for r in range(25):
        runs.append(run)
        run = run + sums[32 * r : 32 * r + 32]
    even = 2.0 * jnp.floor((run + 1.0) * 0.5)
    above = (
        lax.broadcasted_iota(jnp.int32, (32, 32), 1)
        < lax.broadcasted_iota(jnp.int32, (32, 32), 0)
    ).astype(f32)
    starts = jnp.dot(
        above, jnp.broadcast_to(even, (32, 128)), precision=lax.Precision.HIGHEST,
        preferred_element_type=f32,
    )[:, 0:1]
    count = jnp.sum(even).astype(jnp.int32)
    ranks = []
    for r in range(25):
        h = hots[32 * r : 32 * r + 32, :]
        at = within[32 * r : 32 * r + 32] + (runs[r] + starts)
        ranks.append(jnp.sum(h * at, axis=0, keepdims=True))
    rank = jnp.where(used, jnp.concatenate(ranks, axis=0), -1.0)
    pad = jnp.full((128 - 25, 128), -1.0, f32)
    rank_t = jnp.transpose(jnp.concatenate([rank, pad], axis=0))
    lane = lax.broadcasted_iota(jnp.int32, (128, 128), 1).astype(f32)
    row8 = lax.broadcasted_iota(jnp.int32, (8, 128), 0)
    ends = starts + even

    def fill(kr, carry):
        got = jnp.zeros((8, 128), f32)
        first = (kr * 128).astype(f32)
        want = lane + first
        for r in range(25):
            hot = (rank_t[:, r : r + 1] == want).astype(bf16)
            vals = jnp.where(row8 == 0, dev[r : r + 1], jnp.where(row8 == 1, local[r : r + 1], 1.0))
            vals = jnp.where((row8 < 3) & used[r : r + 1], vals, 0.0)
            got = got + jnp.dot(vals.astype(bf16), hot, preferred_element_type=f32)
        other = got[0:1] * float(ROWS) + got[1:2] * 9.0
        own = jnp.sum((ends <= want[0:32]).astype(f32), axis=0, keepdims=True)
        own = jnp.minimum(own, 31.0)
        rows = jnp.where(
            row8 == 0, other, jnp.where(row8 == 1, own, jnp.where(row8 == 2, got[2:3], 0.0))
        )
        listed[...] = rows.astype(jnp.int32)
        copy = pltpu.make_async_copy(listed, table.at[pl.ds(kr * 8, 8)], sem)
        copy.start()
        copy.wait()
        return carry

    lax.fori_loop(0, (count + 127) // 128, fill, 0)
    return count


def near_kernel(
    win_hbm, pair_hbm, far_hbm, out_ref,
    win_ref, pair_ref, own_ref, far_ref, feats, arrange, acc, hots, listed, table, sem, in_sem,
):
    space, sub = lax.axis_index("space"), lax.axis_index("sub")
    nblocks = out_ref.shape[1]
    my_row = pl.multiple_of((8 + sub) * ROWS, 8)
    pairs_in = pltpu.make_async_copy(pair_hbm.at[:, 288:296], pair_ref, in_sem.at[0])
    own_in = pltpu.make_async_copy(win_hbm.at[pl.ds(my_row, ROWS)], own_ref, in_sem.at[1])
    win_in = pltpu.make_async_copy(win_hbm, win_ref, in_sem.at[2])
    far_in = pltpu.make_async_copy(far_hbm, far_ref, in_sem.at[3])
    for copy in (pairs_in, own_in, win_in, far_in):
        copy.start()
    pairs_in.wait()
    count = build_list(pair_ref, space, sub, nblocks, hots, listed, table, sem)
    own_in.wait()
    origin = jnp.where(
        lax.broadcasted_iota(jnp.int32, (16, 1), 0) < 3, own_ref[0:16, 0:1], 0.0
    )

    arrange[...] = arrangement()
    acc[...] = jnp.zeros_like(acc)
    for q in range(0, nblocks, 8):
        x = jnp.concatenate(
            [
                jnp.concatenate(
                    split_rows(own_ref[9 * g : 9 * g + 16, :] - origin, 0.25), axis=0
                )
                for g in range(q, q + 8)
            ],
            axis=1,
        )
        f = lax.dot_general(
            x, arrange[...], (((0,), (0,)), ((), ())), preferred_element_type=f32
        )
        feats[q * 128 : q * 128 + 1024, :] = f.astype(bf16)

    win_in.wait()
    half = lax.broadcasted_iota(jnp.int32, (1, 256), 1) < 128
    top = lax.broadcasted_iota(jnp.int32, (16, 128), 0) < 3

    def items(step, carry):
        work = []
        for u in range(UNROLL):
            k = (step * UNROLL + u) * 2
            inside = k < count
            k = jnp.minimum(k, count - 2)
            row = k // 128 * 8
            col = k % 128
            own = table[row + 1, col]
            rhs = []
            alive = []
            for v in range(2):
                other = table[row, col + v]
                alive.append(jnp.where(inside, table[row + 2, col + v], 0).astype(f32))
                a, b, c, ext = split_rows(win_ref[pl.ds(other, 16), :] - origin, 0.0)
                rhs.append(
                    jnp.concatenate(
                        [a, a, a, b, b, c, ext, jnp.zeros((16, 128), bf16)], axis=0
                    )
                )
            f = feats[pl.ds(pl.multiple_of(own * 128, 128), 128), :]
            f = jnp.concatenate([f[:, 0:128], f[:, 128:256], f[:, 256:384]], axis=0)
            work.append((own, jnp.where(half, alive[0], alive[1]), f, jnp.concatenate(rhs, axis=1)))
        outs = [jnp.dot(f, rhs, preferred_element_type=f32) for _, _, f, rhs in work]
        sums = []
        for (own, live, _, rhs), out in zip(work, outs):
            inv = lax.rsqrt(jnp.maximum(out[0:128], 0.25))
            g = (inv * inv) * (inv * live) * (out[128:256] * out[256:384])
            hi = g.astype(bf16)
            lo = (g - hi.astype(f32)).astype(bf16)
            lhs = jnp.concatenate([rhs[0:16], rhs[48:64], rhs[80:112]], axis=0)
            dims = (((1,), (1,)), ((), ()))
            r = lax.dot_general(lhs, hi, dims, preferred_element_type=f32)
            r = r + lax.dot_general(lhs, lo, dims, preferred_element_type=f32)
            sums.append((own, jnp.where(top, r[0:16] + r[16:32] + r[32:48], r[48:49])))
        for own, r in sums:
            acc[own] += r
        return carry

    lax.fori_loop(0, (count // 2 + UNROLL - 1) // UNROLL, items, 0)

    far_in.wait()
    for g in range(nblocks):
        p = own_ref[9 * g : 9 * g + 16, :] - origin
        t = acc[g]
        force = far_ref[0:3, g * 128 : g * 128 + 128] + p[0:3] * t[3:4] - t[0:3]
        for a in range(3):
            out_ref[a, g : g + 1, :] = force[a : a + 1]


def on_device(seg_data, cell_of_block, cell_center, pairs, live_count):
    nblocks, _, width = seg_data.shape
    ncell = cell_center.shape[1]
    slots = pairs.shape[0]
    vmem = pl.BlockSpec(memory_space=pltpu.VMEM)
    hbm = pl.BlockSpec(memory_space=pltpu.HBM)
    dma = pltpu.SemaphoreType.DMA
    far, window = pl.pallas_call(
        exchange_and_far,
        out_shape=(
            jax.ShapeDtypeStruct((3, nblocks * width), f32),
            jax.ShapeDtypeStruct((3, 8, ROWS, width), f32),
        ),
        in_specs=[hbm] * 5,
        out_specs=(hbm, hbm),
        scratch_shapes=[
            pltpu.VMEM((9, nblocks, width), f32),
            pltpu.VMEM((1, nblocks), jnp.int32),
            pltpu.VMEM((3, ncell), f32),
            pltpu.VMEM((2, slots), jnp.int32),
            pltpu.VMEM((1, 1), jnp.int32),
            pltpu.VMEM((nblocks, width), jnp.int32),
            pltpu.VMEM((ROWS, width), f32),
            pltpu.VMEM((16, nblocks * width), f32),
            pltpu.VMEM((16, ncell // 16), f32),
            pltpu.VMEM((7, 16, ncell // 16), f32),
            pltpu.VMEM((16, 16, ncell // 16), f32),
            pltpu.VMEM((ncell, 32), bf16),
            pltpu.VMEM((32, nblocks * width), bf16),
            pltpu.VMEM((32, nblocks * width), f32),
            pltpu.VMEM((EARLY, 2, ncell // 16, nblocks * width), bf16),
            pltpu.VMEM((3, nblocks * width), f32),
            dma((5,)), dma((2,)), dma((3, 4)), dma((3, 3)), dma((3, 8)),
            dma((7,)), dma((7,)), dma((16,)), dma((16,)), dma, dma,
        ],
        compiler_params=pltpu.CompilerParams(
            collective_id=0, has_side_effects=True, vmem_limit_bytes=56 << 20
        ),
    )(
        seg_data.transpose(1, 0, 2), cell_of_block[None, :], cell_center, pairs.T,
        live_count[None, :],
    )
    force = pl.pallas_call(
        near_kernel,
        out_shape=jax.ShapeDtypeStruct((3, nblocks, width), f32),
        in_specs=[hbm] * 3,
        out_specs=vmem,
        scratch_shapes=[
            pltpu.VMEM((24 * ROWS, width), f32),
            pltpu.VMEM((24, 8, width), f32),
            pltpu.VMEM((ROWS, width), f32),
            pltpu.VMEM((3, nblocks * width), f32),
            pltpu.VMEM((nblocks * width, 384), bf16),
            pltpu.VMEM((64, 384), bf16),
            pltpu.VMEM((nblocks, 16, width), f32),
            pltpu.VMEM((25 * 32, width), f32),
            pltpu.VMEM((8, width), jnp.int32),
            pltpu.SMEM((26 * 8, width), jnp.int32),
            dma, dma((4,)),
        ],
        compiler_params=pltpu.CompilerParams(vmem_limit_bytes=56 << 20),
    )(window.reshape(24 * ROWS, width), window.reshape(24, ROWS, width), far)
    return force.transpose(1, 0, 2)


def solution(mesh):
    placed = (
        P(("space", "sub"), None, None),
        P(("space", "sub")),
        P(),
        P(("space", "sub"), None),
        P(("space", "sub")),
    )
    return jax.shard_map(
        on_device,
        mesh=mesh,
        in_specs=placed,
        out_specs=P(("space", "sub"), None, None),
        check_vma=False,
    )
```

```python
import functools

import jax
import jax.numpy as jnp
from jax import lax
from jax.experimental import pallas as pl
from jax.experimental.pallas import tpu as pltpu
from jax.sharding import PartitionSpec as P

MESH = pl.DeviceIdType.MESH
f32 = jnp.float32
bf16 = jnp.bfloat16
ROWS = 296
UNROLL = 8


def three(x):
    a = x.astype(bf16).astype(f32)
    r = x - a
    b = r.astype(bf16).astype(f32)
    return a, b, (r - b).astype(bf16).astype(f32)


def exchange_and_far(
    seg_hbm, cell_hbm, cc_hbm, pair_hbm, live_hbm, far_hbm, win,
    seg_ref, cell_row, cc_ref, pair_ref, live_ref, cell_ref,
    payload, flat, mine, twin, pair_sum, parts, moments, cells_f, segs_f, acc, early, far_ref,
    in_sem, x_send, x_recv, z_send, z_recv, r_send, r_recv,
    twin_send, twin_recv, p_send, p_recv, y_send, y_recv, m_send, m_recv, own_sem, far_sem,
):
    space = lax.axis_index("space")
    sub = lax.axis_index("sub")
    y, x = space // 4, space % 4
    z, core = sub // 2, sub % 2
    nblocks = seg_ref.shape[1]
    ncell = cc_ref.shape[1]
    per = ncell // 16
    other_core = (space, z * 2 + 1 - core)

    def along_z(k):
        return (space, (z + k) % 4 * 2 + core)

    def along_y(k):
        return ((y + k) % 4 * 4 + x, sub)

    def along_x(k):
        return (y * 4 + (x + k) % 4, sub)

    def along_space(k):
        return ((space + k) % 16, sub)

    ins = [
        pltpu.make_async_copy(src, dst, in_sem.at[i])
        for i, (src, dst) in enumerate(
            [
                (cell_hbm, cell_row), (cc_hbm, cc_ref), (seg_hbm, seg_ref),
                (pair_hbm, pair_ref), (live_hbm, live_ref),
            ]
        )
    ]
    for copy in ins:
        copy.start()
    barrier = pltpu.get_barrier_semaphore()
    partners = [other_core, along_space(1), along_space(15)]
    partners += [to(k) for to in (along_z, along_y, along_x) for k in (1, 2, 3)]
    for to in partners:
        pl.semaphore_signal(barrier, inc=1, device_id=to, device_id_type=MESH)

    for copy in ins:
        copy.wait()

    base = space * per
    own_cc = cc_ref[:, pl.ds(pl.multiple_of(base, 256), per)]
    square = lax.broadcasted_iota(jnp.int32, (nblocks, nblocks), 0)
    lane = lax.broadcasted_iota(jnp.int32, (nblocks, nblocks), 1)
    cell = jnp.sum(
        jnp.where(square == lane, cell_row[...].astype(f32), 0.0), axis=1, keepdims=True
    )
    cell_ref[...] = jnp.broadcast_to(cell, (nblocks, 128)).astype(jnp.int32)
    hot = (
        cell.astype(jnp.int32) - base
        == lax.broadcasted_iota(jnp.int32, (nblocks, per), 1)
    ).astype(f32)
    origin = []
    for a in range(3):
        centre = jnp.sum(hot * own_cc[a : a + 1], axis=1, keepdims=True)
        origin.append(centre[0:1])
        payload[pl.ds(a, nblocks, stride=9), :] = seg_ref[a] + centre
    for a in range(3, 9):
        payload[pl.ds(a, nblocks, stride=9), :] = seg_ref[a]
    alive = lax.broadcasted_iota(jnp.int32, (2, 128), 1) < live_ref[...]
    payload[288:290, :] = jnp.where(alive, pair_ref[...].astype(f32), -1.0)
    payload[290:296, :] = jnp.zeros((6, 128), f32)
    for a in range(3):
        for b in range(3):
            outer = jnp.sum(seg_ref[6 + a] * seg_ref[3 + b], axis=1, keepdims=True)
            row = jnp.sum(hot * outer, axis=0, keepdims=True)
            mine[3 * a + b : 3 * a + b + 1, :] = row[:, 0:128]
            mine[9 + 3 * a + b : 10 + 3 * a + b, :] = row[:, 128:256]

    def send(src, dst, send_sem, recv_sem, to):
        return pltpu.make_async_remote_copy(
            src_ref=src, dst_ref=dst, send_sem=send_sem, recv_sem=recv_sem,
            device_id=to, device_id_type=MESH,
        )

    def arrived(ref, sem):
        pltpu.make_async_copy(ref, ref, sem).wait()

    own_copy = pltpu.make_async_copy(payload, win.at[core, 0], own_sem)
    own_copy.start()
    pl.semaphore_wait(barrier, len(partners))

    to_twin = send(mine, twin, twin_send, twin_recv, other_core)
    to_z = [
        send(pair_sum, parts.at[3 - k], p_send.at[k - 1], p_recv.at[3 - k], along_z(k))
        for k in (1, 2, 3)
    ]
    to_y = [
        send(moments.at[0, 0], moments.at[0, 4 - k], y_send.at[k - 1], y_recv.at[3 - k], along_y(k))
        for k in (1, 2, 3)
    ]
    to_x = [
        send(moments.at[0], moments.at[4 - k], m_send.at[k - 1], m_recv.at[3 - k], along_x(k))
        for k in (1, 2, 3)
    ]
    after = send(payload, win.at[core, 4], x_send.at[0], x_recv.at[0], along_space(1))
    before = send(payload, win.at[core, 5], x_send.at[1], x_recv.at[1], along_space(15))
    step = 1 + 2 * core

    def place(group, dz):
        return win.at[core, dz] if group == 0 else win.at[core, pl.ds(4 + 2 * dz, 2)]

    def spread(group, k):
        return send(
            payload if group == 0 else place(1, 0), place(group, 4 - k),
            z_send.at[group, k // 2], z_recv.at[group, 3 - k], along_z(k),
        )

    def forward(group):
        return send(
            place(group, 4 - step), place(group, 2),
            z_send.at[group, 2], z_recv.at[group, 1], along_z(step),
        )

    def relay(group):
        part = win.at[core, 0:4] if group == 0 else win.at[core, 4:12]
        return send(part, part, r_send.at[group], r_recv.at[group], other_core)

    to_twin.start()
    after.start()
    before.start()
    for k in (1, 3):
        spread(0, k).start()

    for g in range(nblocks):
        lanes = slice(g * 128, g * 128 + 128)
        flat[0:3, lanes] = payload[9 * g : 9 * g + 3, :]
        flat[8:11, lanes] = payload[9 * g + 3 : 9 * g + 6, :]
    row3 = lax.broadcasted_iota(jnp.int32, (3, 1), 0)
    origin = jnp.where(row3 == 0, origin[0], jnp.where(row3 == 1, origin[1], origin[2]))
    ones = jnp.ones((3, ncell), f32)
    blank = jnp.zeros((8, ncell), f32)
    c = cc_ref[...] - origin
    c1, c2, c3 = three(c)
    cq = jnp.concatenate(three(jnp.sum(c * c, axis=0, keepdims=True)), axis=0)
    cells_f[...] = jnp.transpose(
        jnp.concatenate([c1, c1, c2, c2, c1, c3, cq, ones, blank], axis=0)
    ).astype(bf16)
    p = flat[0:3, :] - origin
    p1, p2, p3 = three(-2.0 * p)
    pq = jnp.concatenate(three(1.0 + jnp.sum(p * p, axis=0, keepdims=True)), axis=0)
    segs_f[...] = jnp.concatenate(
        [p1, p2, p1, p2, p3, p1, ones, pq, blank], axis=0
    ).astype(bf16)

    def region_of(dx, dy):
        return (y + dy) % 4 * 4 + (x + dx) % 4

    def weights(region, first):
        at = pl.multiple_of(region * per, 256)
        dist = jnp.dot(cells_f[pl.ds(at, per), :], segs_f[...], preferred_element_type=f32)
        w = pl.reciprocal(dist, approx=True)
        if first:
            cell_id = at + lax.broadcasted_iota(jnp.int32, (per, 128), 0)
            w = jnp.concatenate(
                [
                    jnp.where(
                        cell_id == cell_ref[g : g + 1, :], 0.0, w[:, g * 128 : g * 128 + 128]
                    )
                    for g in range(nblocks)
                ],
                axis=1,
            )
        hi = w.astype(bf16)
        return hi, (w - hi.astype(f32)).astype(bf16)

    def product(dx, dy, hi, lo):
        m = moments[dx, dy]
        m = jnp.concatenate([m[0:9], m[9:18]], axis=1)
        m = jnp.concatenate([m, jnp.zeros((7, per), f32)], axis=0)
        m_hi = m.astype(bf16)
        m = jnp.concatenate([m_hi, (m - m_hi.astype(f32)).astype(bf16)], axis=0)
        return jnp.dot(m, hi, preferred_element_type=f32) + jnp.dot(
            m, lo, preferred_element_type=f32
        )

    early[0, 0], early[0, 1] = weights(space, True)

    arrived(twin, twin_recv)
    pair_sum[...] = mine[...] + twin[...]
    for copy in to_z:
        copy.start()
    early[1, 0], early[1, 1] = weights(region_of(0, 1), False)

    region = pair_sum[...]
    for k in range(3):
        arrived(parts.at[k], p_recv.at[k])
        region = region + parts[k]
    moments[0, 0] = region
    for copy in to_y:
        copy.start()
    early[2, 0], early[2, 1] = weights(region_of(0, 2), False)

    for k in range(3):
        arrived(moments.at[0, k + 1], y_recv.at[k])
    for copy in to_x:
        copy.start()
    for k in range(2):
        arrived(win.at[core, 4 + k], x_recv.at[k])
    for k in (1, 3):
        spread(1, k).start()
    early[3, 0], early[3, 1] = weights(region_of(0, 3), False)

    for dz in (1, 3):
        arrived(place(0, dz), z_recv.at[0, dz - 1])
    forward(0).start()
    acc[...] = product(0, 0, early[0, 0], early[0, 1])
    for k in range(1, 4):
        acc[...] += product(0, k, early[k, 0], early[k, 1])

    def later_chunk(k, carry):
        dx, dy = k // 4, k % 4
        hi, lo = weights(region_of(dx, dy), False)
        acc[...] += product(dx, dy, hi, lo)
        return carry

    arrived(moments.at[1], m_recv.at[0])
    lax.fori_loop(4, 6, later_chunk, 0)
    arrived(place(0, 2), z_recv.at[0, 1])
    own_copy.wait()
    relay(0).start()
    lax.fori_loop(6, 8, later_chunk, 0)
    arrived(moments.at[2], m_recv.at[1])
    lax.fori_loop(8, 9, later_chunk, 0)
    for dz in (1, 3):
        arrived(place(1, dz), z_recv.at[1, dz - 1])
    forward(1).start()
    lax.fori_loop(9, 12, later_chunk, 0)
    arrived(place(1, 2), z_recv.at[1, 1])
    relay(1).start()
    arrived(moments.at[3], m_recv.at[2])
    lax.fori_loop(12, 16, later_chunk, 0)

    grid = acc[0:9, :] + acc[16:25, :]
    line = flat[8:11, :]
    for a in range(3):
        far_ref[a : a + 1, :] = jnp.sum(
            grid[3 * a : 3 * a + 3, :] * line, axis=0, keepdims=True
        )

    far_copy = pltpu.make_async_copy(far_ref, far_hbm, far_sem)
    far_copy.start()

    arrived(win.at[1 - core, 0:4], r_recv.at[0])
    arrived(win.at[1 - core, 4:12], r_recv.at[1])
    for copy in [to_twin, after, before] + to_z + to_y + to_x:
        copy.wait_send()
    for group in range(2):
        for k in (1, 3):
            spread(group, k).wait_send()
        forward(group).wait_send()
        relay(group).wait_send()
    far_copy.wait()


def arrangement():
    r = lax.broadcasted_iota(jnp.int32, (64, 384), 0)
    q = lax.broadcasted_iota(jnp.int32, (64, 384), 1)
    kind, col = q // 128, q % 128
    group, line = col // 16, col % 16
    mate = jnp.where(group < 3, group, jnp.where(group < 5, group - 3, 0))
    dist = (kind == 0) & (group < 6) & (line < 3) & (r == mate * 16 + line)
    extra = (kind == 0) & (group == 6) & (
        ((line < 3) & (r == 48 + 3 + line)) | ((line >= 3) & (line < 6) & (r == 48))
    )
    burg_line = (kind == 1) & (group < 6) & (line >= 3) & (line < 6) & (r == mate * 16 + line + 3)
    line_burg = (kind == 2) & (group < 6) & (line >= 6) & (line < 9) & (r == mate * 16 + line - 3)
    return jnp.where(
        dist, -2.0, jnp.where(extra | burg_line | line_burg, 1.0, 0.0)
    ).astype(bf16)


def split_rows(x, plus):
    row16 = lax.broadcasted_iota(jnp.int32, (16, 128), 0)
    a, b, c = three(x)
    sq = jnp.sum(jnp.where(row16 < 3, x * x, 0.0), axis=0, keepdims=True) + plus
    s1, s2, s3 = three(sq)
    ext = jnp.where(
        row16 < 3, 1.0,
        jnp.where(row16 == 3, s1, jnp.where(row16 == 4, s2, jnp.where(row16 == 5, s3, 0.0))),
    )
    return a.astype(bf16), b.astype(bf16), c.astype(bf16), ext.astype(bf16)


def build_list(pair_ref, space, sub, nblocks, hots, listed, table, sem):
    first_block = ((space * 8 + sub) * nblocks).astype(f32)
    target = jnp.concatenate(
        [pair_ref[d, 0:1, :] for d in range(24)] + [pair_ref[sub % 2 * 12, 0:1, :]],
        axis=0,
    )
    source = jnp.concatenate(
        [pair_ref[d, 1:2, :] for d in range(24)] + [pair_ref[sub % 2 * 12, 1:2, :]],
        axis=0,
    )
    is_own = lax.broadcasted_iota(jnp.int32, (25, 128), 0) == 24
    mine = jnp.where(is_own, target, source) - first_block
    theirs = jnp.where(is_own, source, target)
    used = (source >= 0) & (mine >= 0) & (mine < nblocks)
    mine = jnp.where(used, mine, -1.0)
    owner = jnp.floor(theirs * (1.0 / 32))
    their_space = jnp.floor(owner * (1.0 / 8))
    their_sub = owner - 8.0 * their_space
    their_z = jnp.floor(their_sub * 0.5)
    ahead = their_space - space.astype(f32)
    ahead = jnp.where(ahead < -8, ahead + 16.0, jnp.where(ahead > 8, ahead - 16.0, ahead))
    dz = their_z - (sub // 2).astype(f32)
    dz = jnp.where(dz < 0, dz + 4.0, dz)
    dev = (their_sub - 2.0 * their_z) * 12.0 + jnp.where(
        ahead == 0, dz, 4.0 + 2.0 * dz + (ahead > 0).astype(f32)
    )
    local = theirs - 32.0 * owner
    before = (
        lax.broadcasted_iota(jnp.int32, (128, 128), 0)
        < lax.broadcasted_iota(jnp.int32, (128, 128), 1)
    ).astype(bf16)
    block_id = lax.broadcasted_iota(jnp.int32, (32, 128), 0).astype(f32)
    run = jnp.zeros((32, 1), f32)
    hots[...] = jnp.concatenate(
        [(mine[r : r + 1] == block_id).astype(f32) for r in range(25)], axis=0
    )
    within = jnp.dot(hots[...].astype(bf16), before, preferred_element_type=f32)
    sums = jnp.sum(hots[...], axis=1, keepdims=True)
    runs = []
    for r in range(25):
        runs.append(run)
        run = run + sums[32 * r : 32 * r + 32]
    even = 2.0 * jnp.floor((run + 1.0) * 0.5)
    above = (
        lax.broadcasted_iota(jnp.int32, (32, 32), 1)
        < lax.broadcasted_iota(jnp.int32, (32, 32), 0)
    ).astype(f32)
    starts = jnp.dot(
        above, jnp.broadcast_to(even, (32, 128)), precision=lax.Precision.HIGHEST,
        preferred_element_type=f32,
    )[:, 0:1]
    count = jnp.sum(even).astype(jnp.int32)
    ranks = []
    for r in range(25):
        h = hots[32 * r : 32 * r + 32, :]
        at = within[32 * r : 32 * r + 32] + (runs[r] + starts)
        ranks.append(jnp.sum(h * at, axis=0, keepdims=True))
    rank = jnp.where(used, jnp.concatenate(ranks, axis=0), -1.0)
    pad = jnp.full((128 - 25, 128), -1.0, f32)
    rank_t = jnp.transpose(jnp.concatenate([rank, pad], axis=0))
    lane = lax.broadcasted_iota(jnp.int32, (128, 128), 1).astype(f32)
    row8 = lax.broadcasted_iota(jnp.int32, (8, 128), 0)
    ends = starts + even

    def fill(kr, carry):
        got = jnp.zeros((8, 128), f32)
        first = (kr * 128).astype(f32)
        want = lane + first
        for r in range(25):
            hot = (rank_t[:, r : r + 1] == want).astype(bf16)
            vals = jnp.where(row8 == 0, dev[r : r + 1], jnp.where(row8 == 1, local[r : r + 1], 1.0))
            vals = jnp.where((row8 < 3) & used[r : r + 1], vals, 0.0)
            got = got + jnp.dot(vals.astype(bf16), hot, preferred_element_type=f32)
        other = got[0:1] * float(ROWS) + got[1:2] * 9.0
        own = jnp.sum((ends <= want[0:32]).astype(f32), axis=0, keepdims=True)
        own = jnp.minimum(own, 31.0)
        rows = jnp.where(
            row8 == 0, other, jnp.where(row8 == 1, own, jnp.where(row8 == 2, got[2:3], 0.0))
        )
        listed[...] = rows.astype(jnp.int32)
        copy = pltpu.make_async_copy(listed, table.at[pl.ds(kr * 8, 8)], sem)
        copy.start()
        copy.wait()
        return carry

    lax.fori_loop(0, (count + 127) // 128, fill, 0)
    return count


def near_kernel(
    win_hbm, pair_hbm, far_hbm, out_ref,
    win_ref, pair_ref, own_ref, far_ref, feats, arrange, acc, hots, listed, table, sem, in_sem,
):
    space, sub = lax.axis_index("space"), lax.axis_index("sub")
    nblocks = out_ref.shape[1]
    my_row = pl.multiple_of(sub % 2 * 12 * ROWS, 8)
    pairs_in = pltpu.make_async_copy(pair_hbm.at[:, 288:296], pair_ref, in_sem.at[0])
    own_in = pltpu.make_async_copy(win_hbm.at[pl.ds(my_row, ROWS)], own_ref, in_sem.at[1])
    win_in = pltpu.make_async_copy(win_hbm, win_ref, in_sem.at[2])
    far_in = pltpu.make_async_copy(far_hbm, far_ref, in_sem.at[3])
    for copy in (pairs_in, own_in, win_in, far_in):
        copy.start()
    pairs_in.wait()
    count = build_list(pair_ref, space, sub, nblocks, hots, listed, table, sem)
    own_in.wait()
    origin = jnp.where(
        lax.broadcasted_iota(jnp.int32, (16, 1), 0) < 3, own_ref[0:16, 0:1], 0.0
    )

    arrange[...] = arrangement()
    acc[...] = jnp.zeros_like(acc)
    for q in range(0, nblocks, 8):
        x = jnp.concatenate(
            [
                jnp.concatenate(
                    split_rows(own_ref[9 * g : 9 * g + 16, :] - origin, 0.25), axis=0
                )
                for g in range(q, q + 8)
            ],
            axis=1,
        )
        f = lax.dot_general(
            x, arrange[...], (((0,), (0,)), ((), ())), preferred_element_type=f32
        )
        feats[q * 128 : q * 128 + 1024, :] = f.astype(bf16)

    win_in.wait()
    half = lax.broadcasted_iota(jnp.int32, (1, 256), 1) < 128
    top = lax.broadcasted_iota(jnp.int32, (16, 128), 0) < 3

    def items(step, carry):
        work = []
        for u in range(UNROLL):
            k = (step * UNROLL + u) * 2
            inside = k < count
            k = jnp.minimum(k, count - 2)
            row = k // 128 * 8
            col = k % 128
            own = table[row + 1, col]
            rhs = []
            alive = []
            for v in range(2):
                other = table[row, col + v]
                alive.append(jnp.where(inside, table[row + 2, col + v], 0).astype(f32))
                a, b, c, ext = split_rows(win_ref[pl.ds(other, 16), :] - origin, 0.0)
                rhs.append(
                    jnp.concatenate(
                        [a, a, a, b, b, c, ext, jnp.zeros((16, 128), bf16)], axis=0
                    )
                )
            f = feats[pl.ds(pl.multiple_of(own * 128, 128), 128), :]
            f = jnp.concatenate([f[:, 0:128], f[:, 128:256], f[:, 256:384]], axis=0)
            work.append((own, jnp.where(half, alive[0], alive[1]), f, jnp.concatenate(rhs, axis=1)))
        outs = [jnp.dot(f, rhs, preferred_element_type=f32) for _, _, f, rhs in work]
        sums = []
        for (own, live, _, rhs), out in zip(work, outs):
            inv = lax.rsqrt(jnp.maximum(out[0:128], 0.25))
            g = (inv * inv) * (inv * live) * (out[128:256] * out[256:384])
            hi = g.astype(bf16)
            lo = (g - hi.astype(f32)).astype(bf16)
            lhs = jnp.concatenate([rhs[0:16], rhs[48:64], rhs[80:112]], axis=0)
            dims = (((1,), (1,)), ((), ()))
            r = lax.dot_general(lhs, hi, dims, preferred_element_type=f32)
            r = r + lax.dot_general(lhs, lo, dims, preferred_element_type=f32)
            sums.append((own, jnp.where(top, r[0:16] + r[16:32] + r[32:48], r[48:49])))
        for own, r in sums:
            acc[own] += r
        return carry

    lax.fori_loop(0, (count // 2 + UNROLL - 1) // UNROLL, items, 0)

    far_in.wait()
    for g in range(nblocks):
        p = own_ref[9 * g : 9 * g + 16, :] - origin
        t = acc[g]
        force = far_ref[0:3, g * 128 : g * 128 + 128] + p[0:3] * t[3:4] - t[0:3]
        for a in range(3):
            out_ref[a, g : g + 1, :] = force[a : a + 1]


def on_device(seg_data, cell_of_block, cell_center, pairs, live_count):
    nblocks, _, width = seg_data.shape
    ncell = cell_center.shape[1]
    slots = pairs.shape[0]
    vmem = pl.BlockSpec(memory_space=pltpu.VMEM)
    hbm = pl.BlockSpec(memory_space=pltpu.HBM)
    dma = pltpu.SemaphoreType.DMA
    far, window = pl.pallas_call(
        exchange_and_far,
        out_shape=(
            jax.ShapeDtypeStruct((3, nblocks * width), f32),
            jax.ShapeDtypeStruct((2, 12, ROWS, width), f32),
        ),
        in_specs=[hbm] * 5,
        out_specs=(hbm, hbm),
        scratch_shapes=[
            pltpu.VMEM((9, nblocks, width), f32),
            pltpu.VMEM((1, nblocks), jnp.int32),
            pltpu.VMEM((3, ncell), f32),
            pltpu.VMEM((2, slots), jnp.int32),
            pltpu.VMEM((1, 1), jnp.int32),
            pltpu.VMEM((nblocks, width), jnp.int32),
            pltpu.VMEM((ROWS, width), f32),
            pltpu.VMEM((16, nblocks * width), f32),
            pltpu.VMEM((18, 128), f32),
            pltpu.VMEM((18, 128), f32),
            pltpu.VMEM((18, 128), f32),
            pltpu.VMEM((3, 18, 128), f32),
            pltpu.VMEM((4, 4, 18, 128), f32),
            pltpu.VMEM((ncell, 32), bf16),
            pltpu.VMEM((32, nblocks * width), bf16),
            pltpu.VMEM((32, nblocks * width), f32),
            pltpu.VMEM((4, 2, ncell // 16, nblocks * width), bf16),
            pltpu.VMEM((3, nblocks * width), f32),
            dma((5,)), dma((2,)), dma((2,)), dma((2, 3)), dma((2, 3)), dma((2,)), dma((2,)),
            dma, dma, dma((3,)), dma((3,)), dma((3,)), dma((3,)), dma((3,)), dma((3,)), dma, dma,
        ],
        compiler_params=pltpu.CompilerParams(
            collective_id=0, has_side_effects=True, vmem_limit_bytes=56 << 20
        ),
    )(
        seg_data.transpose(1, 0, 2), cell_of_block[None, :], cell_center, pairs.T,
        live_count[None, :],
    )
    force = pl.pallas_call(
        near_kernel,
        out_shape=jax.ShapeDtypeStruct((3, nblocks, width), f32),
        in_specs=[hbm] * 3,
        out_specs=vmem,
        scratch_shapes=[
            pltpu.VMEM((24 * ROWS, width), f32),
            pltpu.VMEM((24, 8, width), f32),
            pltpu.VMEM((ROWS, width), f32),
            pltpu.VMEM((3, nblocks * width), f32),
            pltpu.VMEM((nblocks * width, 384), bf16),
            pltpu.VMEM((64, 384), bf16),
            pltpu.VMEM((nblocks, 16, width), f32),
            pltpu.VMEM((25 * 32, width), f32),
            pltpu.VMEM((8, width), jnp.int32),
            pltpu.SMEM((26 * 8, width), jnp.int32),
            dma, dma((4,)),
        ],
        compiler_params=pltpu.CompilerParams(vmem_limit_bytes=56 << 20),
    )(window.reshape(24 * ROWS, width), window.reshape(24, ROWS, width), far)
    return force.transpose(1, 0, 2)


def solution(mesh):
    placed = (
        P(("space", "sub"), None, None),
        P(("space", "sub")),
        P(),
        P(("space", "sub"), None),
        P(("space", "sub")),
    )
    return jax.shard_map(
        on_device,
        mesh=mesh,
        in_specs=placed,
        out_specs=P(("space", "sub"), None, None),
        check_vma=False,
    )
```

```python
import functools

import jax
import jax.numpy as jnp
from jax import lax
from jax.experimental import pallas as pl
from jax.experimental.pallas import tpu as pltpu
from jax.sharding import PartitionSpec as P

MESH = pl.DeviceIdType.MESH
f32 = jnp.float32
bf16 = jnp.bfloat16
ROWS = 296
UNROLL = 8


def three(x):
    a = x.astype(bf16).astype(f32)
    r = x - a
    b = r.astype(bf16).astype(f32)
    return a, b, (r - b).astype(bf16).astype(f32)


def exchange_and_far(
    seg_hbm, cell_hbm, cc_hbm, pair_hbm, live_hbm, far_hbm, win,
    seg_ref, cell_row, cc_ref, pair_ref, live_ref, cell_ref,
    payload, flat, mine, twin, pair_sum, parts, moments, cells_f, segs_f, acc, early, far_ref,
    in_sem, x_send, x_recv, z_send, z_recv, r_send, r_recv,
    twin_send, twin_recv, p_send, p_recv, y_send, y_recv, m_send, m_recv, own_sem, far_sem,
):
    space = lax.axis_index("space")
    sub = lax.axis_index("sub")
    y, x = space // 4, space % 4
    z, core = sub // 2, sub % 2
    nblocks = seg_ref.shape[1]
    ncell = cc_ref.shape[1]
    per = ncell // 16
    other_core = (space, z * 2 + 1 - core)

    def along_z(k):
        return (space, (z + k) % 4 * 2 + core)

    def along_y(k):
        return ((y + k) % 4 * 4 + x, sub)

    def along_x(k):
        return (y * 4 + (x + k) % 4, sub)

    def along_space(k):
        return ((space + k) % 16, sub)

    ins = [
        pltpu.make_async_copy(src, dst, in_sem.at[i])
        for i, (src, dst) in enumerate(
            [
                (cell_hbm, cell_row), (cc_hbm, cc_ref), (seg_hbm, seg_ref),
                (pair_hbm, pair_ref), (live_hbm, live_ref),
            ]
        )
    ]
    for copy in ins:
        copy.start()
    barrier = pltpu.get_barrier_semaphore()
    partners = [other_core, along_space(1), along_space(15)]
    partners += [to(k) for to in (along_z, along_y, along_x) for k in (1, 2, 3)]
    for to in partners:
        pl.semaphore_signal(barrier, inc=1, device_id=to, device_id_type=MESH)

    for copy in ins:
        copy.wait()

    base = space * per
    own_cc = cc_ref[:, pl.ds(pl.multiple_of(base, 256), per)]
    square = lax.broadcasted_iota(jnp.int32, (nblocks, nblocks), 0)
    lane = lax.broadcasted_iota(jnp.int32, (nblocks, nblocks), 1)
    cell = jnp.sum(
        jnp.where(square == lane, cell_row[...].astype(f32), 0.0), axis=1, keepdims=True
    )
    cell_ref[...] = jnp.broadcast_to(cell, (nblocks, 128)).astype(jnp.int32)
    hot = (
        cell.astype(jnp.int32) - base
        == lax.broadcasted_iota(jnp.int32, (nblocks, per), 1)
    ).astype(f32)
    origin = []
    for a in range(3):
        centre = jnp.sum(hot * own_cc[a : a + 1], axis=1, keepdims=True)
        origin.append(centre[0:1])
        payload[pl.ds(a, nblocks, stride=9), :] = seg_ref[a] + centre
    for a in range(3, 9):
        payload[pl.ds(a, nblocks, stride=9), :] = seg_ref[a]
    alive = lax.broadcasted_iota(jnp.int32, (2, 128), 1) < live_ref[...]
    payload[288:290, :] = jnp.where(alive, pair_ref[...].astype(f32), -1.0)
    payload[290:296, :] = jnp.zeros((6, 128), f32)
    for a in range(3):
        for b in range(3):
            outer = jnp.sum(seg_ref[6 + a] * seg_ref[3 + b], axis=1, keepdims=True)
            row = jnp.sum(hot * outer, axis=0, keepdims=True)
            mine[3 * a + b : 3 * a + b + 1, :] = row[:, 0:128]
            mine[9 + 3 * a + b : 10 + 3 * a + b, :] = row[:, 128:256]

    def send(src, dst, send_sem, recv_sem, to):
        return pltpu.make_async_remote_copy(
            src_ref=src, dst_ref=dst, send_sem=send_sem, recv_sem=recv_sem,
            device_id=to, device_id_type=MESH,
        )

    def arrived(ref, sem):
        pltpu.make_async_copy(ref, ref, sem).wait()

    own_copy = pltpu.make_async_copy(payload, win.at[core, 0], own_sem)
    own_copy.start()
    pl.semaphore_wait(barrier, len(partners))

    to_twin = send(mine, twin, twin_send, twin_recv, other_core)
    to_z = [
        send(pair_sum, parts.at[3 - k], p_send.at[k - 1], p_recv.at[3 - k], along_z(k))
        for k in (1, 2, 3)
    ]
    to_y = [
        send(moments.at[0, 0], moments.at[0, 4 - k], y_send.at[k - 1], y_recv.at[3 - k], along_y(k))
        for k in (1, 2, 3)
    ]
    to_x = [
        send(moments.at[0], moments.at[4 - k], m_send.at[k - 1], m_recv.at[3 - k], along_x(k))
        for k in (1, 2, 3)
    ]
    after = send(payload, win.at[core, 4], x_send.at[0], x_recv.at[0], along_space(1))
    before = send(payload, win.at[core, 5], x_send.at[1], x_recv.at[1], along_space(15))
    step = 1 + 2 * core

    def place(group, dz):
        return win.at[core, dz] if group == 0 else win.at[core, 3 + group + 2 * dz]

    def spread(group, k):
        return send(
            payload if group == 0 else place(group, 0), place(group, 4 - k),
            z_send.at[group, k // 2], z_recv.at[group, 3 - k], along_z(k),
        )

    def forward(group):
        return send(
            place(group, 4 - step), place(group, 2),
            z_send.at[group, 2], z_recv.at[group, 1], along_z(step),
        )

    relayed = [(0, 4), (4, 6), (6, 8), (10, 12), (8, 10)]

    def relay(i):
        part = win.at[core, relayed[i][0] : relayed[i][1]]
        return send(part, part, r_send.at[i], r_recv.at[i], other_core)

    to_twin.start()
    after.start()
    before.start()
    for k in (1, 3):
        spread(0, k).start()

    for g in range(nblocks):
        lanes = slice(g * 128, g * 128 + 128)
        flat[0:3, lanes] = payload[9 * g : 9 * g + 3, :]
        flat[8:11, lanes] = payload[9 * g + 3 : 9 * g + 6, :]
    row3 = lax.broadcasted_iota(jnp.int32, (3, 1), 0)
    origin = jnp.where(row3 == 0, origin[0], jnp.where(row3 == 1, origin[1], origin[2]))
    ones = jnp.ones((3, ncell), f32)
    blank = jnp.zeros((8, ncell), f32)
    c = cc_ref[...] - origin
    c1, c2, c3 = three(c)
    cq = jnp.concatenate(three(jnp.sum(c * c, axis=0, keepdims=True)), axis=0)
    cells_f[...] = jnp.transpose(
        jnp.concatenate([c1, c1, c2, c2, c1, c3, cq, ones, blank], axis=0)
    ).astype(bf16)
    p = flat[0:3, :] - origin
    p1, p2, p3 = three(-2.0 * p)
    pq = jnp.concatenate(three(1.0 + jnp.sum(p * p, axis=0, keepdims=True)), axis=0)
    segs_f[...] = jnp.concatenate(
        [p1, p2, p1, p2, p3, p1, ones, pq, blank], axis=0
    ).astype(bf16)

    def region_of(dx, dy):
        return (y + dy) % 4 * 4 + (x + dx) % 4

    def weights(region, first):
        at = pl.multiple_of(region * per, 256)
        dist = jnp.dot(cells_f[pl.ds(at, per), :], segs_f[...], preferred_element_type=f32)
        w = pl.reciprocal(dist, approx=True)
        if first:
            cell_id = at + lax.broadcasted_iota(jnp.int32, (per, 128), 0)
            w = jnp.concatenate(
                [
                    jnp.where(
                        cell_id == cell_ref[g : g + 1, :], 0.0, w[:, g * 128 : g * 128 + 128]
                    )
                    for g in range(nblocks)
                ],
                axis=1,
            )
        hi = w.astype(bf16)
        return hi, (w - hi.astype(f32)).astype(bf16)

    def product(dx, dy, hi, lo):
        m = moments[dx, dy]
        m = jnp.concatenate([m[0:9], m[9:18]], axis=1)
        m = jnp.concatenate([m, jnp.zeros((7, per), f32)], axis=0)
        m_hi = m.astype(bf16)
        m = jnp.concatenate([m_hi, (m - m_hi.astype(f32)).astype(bf16)], axis=0)
        return jnp.dot(m, hi, preferred_element_type=f32) + jnp.dot(
            m, lo, preferred_element_type=f32
        )

    def make(k, carry):
        early[k, 0], early[k, 1] = weights(region_of(k // 4, k % 4), False)
        return carry

    def use(k, carry):
        acc[...] += product(k // 4, k % 4, early[k, 0], early[k, 1])
        return carry

    def whole(k, carry):
        hi, lo = weights(region_of(k // 4, k % 4), False)
        acc[...] += product(k // 4, k % 4, hi, lo)
        return carry

    early[0, 0], early[0, 1] = weights(space, True)

    arrived(twin, twin_recv)
    pair_sum[...] = mine[...] + twin[...]
    for copy in to_z:
        copy.start()
    lax.fori_loop(1, 3, make, 0)

    region = pair_sum[...]
    for k in range(3):
        arrived(parts.at[k], p_recv.at[k])
        region = region + parts[k]
    moments[0, 0] = region
    for copy in to_y:
        copy.start()
    for group in (1, 2):
        arrived(place(group, 0), x_recv.at[group - 1])
        for k in (1, 3):
            spread(group, k).start()
    relay(1).start()
    lax.fori_loop(3, 5, make, 0)

    for k in range(3):
        arrived(moments.at[0, k + 1], y_recv.at[k])
    for copy in to_x:
        copy.start()
    for dz in (1, 3):
        arrived(place(0, dz), z_recv.at[0, dz - 1])
    forward(0).start()
    lax.fori_loop(5, 7, make, 0)

    for dz in (1, 3):
        arrived(place(1, dz), z_recv.at[1, dz - 1])
    forward(1).start()
    lax.fori_loop(7, 8, make, 0)
    acc[...] = product(0, 0, early[0, 0], early[0, 1])
    lax.fori_loop(1, 4, use, 0)

    for dz in (1, 3):
        arrived(place(2, dz), z_recv.at[2, dz - 1])
    forward(2).start()
    relay(2).start()
    relay(3).start()
    arrived(place(0, 2), z_recv.at[0, 1])
    own_copy.wait()
    relay(0).start()
    arrived(moments.at[1], m_recv.at[0])
    lax.fori_loop(4, 8, use, 0)
    arrived(moments.at[2], m_recv.at[1])
    lax.fori_loop(8, 10, whole, 0)
    for group in (1, 2):
        arrived(place(group, 2), z_recv.at[group, 1])
    relay(4).start()
    arrived(moments.at[3], m_recv.at[2])
    lax.fori_loop(10, 16, whole, 0)

    grid = acc[0:9, :] + acc[16:25, :]
    line = flat[8:11, :]
    for a in range(3):
        far_ref[a : a + 1, :] = jnp.sum(
            grid[3 * a : 3 * a + 3, :] * line, axis=0, keepdims=True
        )

    far_copy = pltpu.make_async_copy(far_ref, far_hbm, far_sem)
    far_copy.start()

    for i, (lo, hi) in enumerate(relayed):
        arrived(win.at[1 - core, lo:hi], r_recv.at[i])
    for copy in [to_twin, after, before] + to_z + to_y + to_x:
        copy.wait_send()
    for group in range(3):
        for k in (1, 3):
            spread(group, k).wait_send()
        forward(group).wait_send()
    for i in range(len(relayed)):
        relay(i).wait_send()
    far_copy.wait()


def arrangement():
    r = lax.broadcasted_iota(jnp.int32, (64, 384), 0)
    q = lax.broadcasted_iota(jnp.int32, (64, 384), 1)
    kind, col = q // 128, q % 128
    group, line = col // 16, col % 16
    mate = jnp.where(group < 3, group, jnp.where(group < 5, group - 3, 0))
    dist = (kind == 0) & (group < 6) & (line < 3) & (r == mate * 16 + line)
    extra = (kind == 0) & (group == 6) & (
        ((line < 3) & (r == 48 + 3 + line)) | ((line >= 3) & (line < 6) & (r == 48))
    )
    burg_line = (kind == 1) & (group < 6) & (line >= 3) & (line < 6) & (r == mate * 16 + line + 3)
    line_burg = (kind == 2) & (group < 6) & (line >= 6) & (line < 9) & (r == mate * 16 + line - 3)
    return jnp.where(
        dist, -2.0, jnp.where(extra | burg_line | line_burg, 1.0, 0.0)
    ).astype(bf16)


def split_rows(x, plus):
    row16 = lax.broadcasted_iota(jnp.int32, (16, 128), 0)
    a, b, c = three(x)
    sq = jnp.sum(jnp.where(row16 < 3, x * x, 0.0), axis=0, keepdims=True) + plus
    s1, s2, s3 = three(sq)
    ext = jnp.where(
        row16 < 3, 1.0,
        jnp.where(row16 == 3, s1, jnp.where(row16 == 4, s2, jnp.where(row16 == 5, s3, 0.0))),
    )
    return a.astype(bf16), b.astype(bf16), c.astype(bf16), ext.astype(bf16)


def build_list(pair_ref, space, sub, nblocks, hots, listed, table, sem):
    first_block = ((space * 8 + sub) * nblocks).astype(f32)
    target = jnp.concatenate(
        [pair_ref[d, 0:1, :] for d in range(24)] + [pair_ref[sub % 2 * 12, 0:1, :]],
        axis=0,
    )
    source = jnp.concatenate(
        [pair_ref[d, 1:2, :] for d in range(24)] + [pair_ref[sub % 2 * 12, 1:2, :]],
        axis=0,
    )
    is_own = lax.broadcasted_iota(jnp.int32, (25, 128), 0) == 24
    mine = jnp.where(is_own, target, source) - first_block
    theirs = jnp.where(is_own, source, target)
    used = (source >= 0) & (mine >= 0) & (mine < nblocks)
    mine = jnp.where(used, mine, -1.0)
    owner = jnp.floor(theirs * (1.0 / 32))
    their_space = jnp.floor(owner * (1.0 / 8))
    their_sub = owner - 8.0 * their_space
    their_z = jnp.floor(their_sub * 0.5)
    ahead = their_space - space.astype(f32)
    ahead = jnp.where(ahead < -8, ahead + 16.0, jnp.where(ahead > 8, ahead - 16.0, ahead))
    dz = their_z - (sub // 2).astype(f32)
    dz = jnp.where(dz < 0, dz + 4.0, dz)
    dev = (their_sub - 2.0 * their_z) * 12.0 + jnp.where(
        ahead == 0, dz, 4.0 + 2.0 * dz + (ahead > 0).astype(f32)
    )
    local = theirs - 32.0 * owner
    before = (
        lax.broadcasted_iota(jnp.int32, (128, 128), 0)
        < lax.broadcasted_iota(jnp.int32, (128, 128), 1)
    ).astype(bf16)
    block_id = lax.broadcasted_iota(jnp.int32, (32, 128), 0).astype(f32)
    run = jnp.zeros((32, 1), f32)
    hots[...] = jnp.concatenate(
        [(mine[r : r + 1] == block_id).astype(f32) for r in range(25)], axis=0
    )
    within = jnp.dot(hots[...].astype(bf16), before, preferred_element_type=f32)
    sums = jnp.sum(hots[...], axis=1, keepdims=True)
    runs = []
    for r in range(25):
        runs.append(run)
        run = run + sums[32 * r : 32 * r + 32]
    even = 2.0 * jnp.floor((run + 1.0) * 0.5)
    above = (
        lax.broadcasted_iota(jnp.int32, (32, 32), 1)
        < lax.broadcasted_iota(jnp.int32, (32, 32), 0)
    ).astype(f32)
    starts = jnp.dot(
        above, jnp.broadcast_to(even, (32, 128)), precision=lax.Precision.HIGHEST,
        preferred_element_type=f32,
    )[:, 0:1]
    count = jnp.sum(even).astype(jnp.int32)
    ranks = []
    for r in range(25):
        h = hots[32 * r : 32 * r + 32, :]
        at = within[32 * r : 32 * r + 32] + (runs[r] + starts)
        ranks.append(jnp.sum(h * at, axis=0, keepdims=True))
    rank = jnp.where(used, jnp.concatenate(ranks, axis=0), -1.0)
    pad = jnp.full((128 - 25, 128), -1.0, f32)
    rank_t = jnp.transpose(jnp.concatenate([rank, pad], axis=0))
    lane = lax.broadcasted_iota(jnp.int32, (128, 128), 1).astype(f32)
    row8 = lax.broadcasted_iota(jnp.int32, (8, 128), 0)
    ends = starts + even

    def fill(kr, carry):
        got = jnp.zeros((8, 128), f32)
        first = (kr * 128).astype(f32)
        want = lane + first
        for r in range(25):
            hot = (rank_t[:, r : r + 1] == want).astype(bf16)
            vals = jnp.where(row8 == 0, dev[r : r + 1], jnp.where(row8 == 1, local[r : r + 1], 1.0))
            vals = jnp.where((row8 < 3) & used[r : r + 1], vals, 0.0)
            got = got + jnp.dot(vals.astype(bf16), hot, preferred_element_type=f32)
        other = got[0:1] * float(ROWS) + got[1:2] * 9.0
        own = jnp.sum((ends <= want[0:32]).astype(f32), axis=0, keepdims=True)
        own = jnp.minimum(own, 31.0)
        rows = jnp.where(
            row8 == 0, other, jnp.where(row8 == 1, own, jnp.where(row8 == 2, got[2:3], 0.0))
        )
        listed[...] = rows.astype(jnp.int32)
        copy = pltpu.make_async_copy(listed, table.at[pl.ds(kr * 8, 8)], sem)
        copy.start()
        copy.wait()
        return carry

    lax.fori_loop(0, (count + 127) // 128, fill, 0)
    return count


def near_kernel(
    win_hbm, pair_hbm, far_hbm, out_ref,
    win_ref, pair_ref, own_ref, far_ref, feats, arrange, acc, hots, listed, table, sem, in_sem,
):
    space, sub = lax.axis_index("space"), lax.axis_index("sub")
    nblocks = out_ref.shape[1]
    my_row = pl.multiple_of(sub % 2 * 12 * ROWS, 8)
    pairs_in = pltpu.make_async_copy(pair_hbm.at[:, 288:296], pair_ref, in_sem.at[0])
    own_in = pltpu.make_async_copy(win_hbm.at[pl.ds(my_row, ROWS)], own_ref, in_sem.at[1])
    win_in = pltpu.make_async_copy(win_hbm, win_ref, in_sem.at[2])
    far_in = pltpu.make_async_copy(far_hbm, far_ref, in_sem.at[3])
    for copy in (pairs_in, own_in, win_in, far_in):
        copy.start()
    pairs_in.wait()
    count = build_list(pair_ref, space, sub, nblocks, hots, listed, table, sem)
    own_in.wait()
    origin = jnp.where(
        lax.broadcasted_iota(jnp.int32, (16, 1), 0) < 3, own_ref[0:16, 0:1], 0.0
    )

    arrange[...] = arrangement()
    acc[...] = jnp.zeros_like(acc)
    for q in range(0, nblocks, 8):
        x = jnp.concatenate(
            [
                jnp.concatenate(
                    split_rows(own_ref[9 * g : 9 * g + 16, :] - origin, 0.25), axis=0
                )
                for g in range(q, q + 8)
            ],
            axis=1,
        )
        f = lax.dot_general(
            x, arrange[...], (((0,), (0,)), ((), ())), preferred_element_type=f32
        )
        feats[q * 128 : q * 128 + 1024, :] = f.astype(bf16)

    win_in.wait()
    half = lax.broadcasted_iota(jnp.int32, (1, 256), 1) < 128
    top = lax.broadcasted_iota(jnp.int32, (16, 128), 0) < 3

    def items(step, carry):
        work = []
        for u in range(UNROLL):
            k = (step * UNROLL + u) * 2
            inside = k < count
            k = jnp.minimum(k, count - 2)
            row = k // 128 * 8
            col = k % 128
            own = table[row + 1, col]
            rhs = []
            alive = []
            for v in range(2):
                other = table[row, col + v]
                alive.append(jnp.where(inside, table[row + 2, col + v], 0).astype(f32))
                a, b, c, ext = split_rows(win_ref[pl.ds(other, 16), :] - origin, 0.0)
                rhs.append(
                    jnp.concatenate(
                        [a, a, a, b, b, c, ext, jnp.zeros((16, 128), bf16)], axis=0
                    )
                )
            f = feats[pl.ds(pl.multiple_of(own * 128, 128), 128), :]
            f = jnp.concatenate([f[:, 0:128], f[:, 128:256], f[:, 256:384]], axis=0)
            work.append((own, jnp.where(half, alive[0], alive[1]), f, jnp.concatenate(rhs, axis=1)))
        outs = [jnp.dot(f, rhs, preferred_element_type=f32) for _, _, f, rhs in work]
        sums = []
        for (own, live, _, rhs), out in zip(work, outs):
            inv = lax.rsqrt(jnp.maximum(out[0:128], 0.25))
            g = (inv * inv) * (inv * live) * (out[128:256] * out[256:384])
            hi = g.astype(bf16)
            lo = (g - hi.astype(f32)).astype(bf16)
            lhs = jnp.concatenate([rhs[0:16], rhs[48:64], rhs[80:112]], axis=0)
            dims = (((1,), (1,)), ((), ()))
            r = lax.dot_general(lhs, hi, dims, preferred_element_type=f32)
            r = r + lax.dot_general(lhs, lo, dims, preferred_element_type=f32)
            sums.append((own, jnp.where(top, r[0:16] + r[16:32] + r[32:48], r[48:49])))
        for own, r in sums:
            acc[own] += r
        return carry

    lax.fori_loop(0, (count // 2 + UNROLL - 1) // UNROLL, items, 0)

    far_in.wait()
    for g in range(nblocks):
        p = own_ref[9 * g : 9 * g + 16, :] - origin
        t = acc[g]
        force = far_ref[0:3, g * 128 : g * 128 + 128] + p[0:3] * t[3:4] - t[0:3]
        for a in range(3):
            out_ref[a, g : g + 1, :] = force[a : a + 1]


def on_device(seg_data, cell_of_block, cell_center, pairs, live_count):
    nblocks, _, width = seg_data.shape
    ncell = cell_center.shape[1]
    slots = pairs.shape[0]
    vmem = pl.BlockSpec(memory_space=pltpu.VMEM)
    hbm = pl.BlockSpec(memory_space=pltpu.HBM)
    dma = pltpu.SemaphoreType.DMA
    far, window = pl.pallas_call(
        exchange_and_far,
        out_shape=(
            jax.ShapeDtypeStruct((3, nblocks * width), f32),
            jax.ShapeDtypeStruct((2, 12, ROWS, width), f32),
        ),
        in_specs=[hbm] * 5,
        out_specs=(hbm, hbm),
        scratch_shapes=[
            pltpu.VMEM((9, nblocks, width), f32),
            pltpu.VMEM((1, nblocks), jnp.int32),
            pltpu.VMEM((3, ncell), f32),
            pltpu.VMEM((2, slots), jnp.int32),
            pltpu.VMEM((1, 1), jnp.int32),
            pltpu.VMEM((nblocks, width), jnp.int32),
            pltpu.VMEM((ROWS, width), f32),
            pltpu.VMEM((16, nblocks * width), f32),
            pltpu.VMEM((18, 128), f32),
            pltpu.VMEM((18, 128), f32),
            pltpu.VMEM((18, 128), f32),
            pltpu.VMEM((3, 18, 128), f32),
            pltpu.VMEM((4, 4, 18, 128), f32),
            pltpu.VMEM((ncell, 32), bf16),
            pltpu.VMEM((32, nblocks * width), bf16),
            pltpu.VMEM((32, nblocks * width), f32),
            pltpu.VMEM((8, 2, ncell // 16, nblocks * width), bf16),
            pltpu.VMEM((3, nblocks * width), f32),
            dma((5,)), dma((2,)), dma((2,)), dma((3, 3)), dma((3, 3)), dma((5,)), dma((5,)),
            dma, dma, dma((3,)), dma((3,)), dma((3,)), dma((3,)), dma((3,)), dma((3,)), dma, dma,
        ],
        compiler_params=pltpu.CompilerParams(
            collective_id=0, has_side_effects=True, vmem_limit_bytes=56 << 20
        ),
    )(
        seg_data.transpose(1, 0, 2), cell_of_block[None, :], cell_center, pairs.T,
        live_count[None, :],
    )
    force = pl.pallas_call(
        near_kernel,
        out_shape=jax.ShapeDtypeStruct((3, nblocks, width), f32),
        in_specs=[hbm] * 3,
        out_specs=vmem,
        scratch_shapes=[
            pltpu.VMEM((24 * ROWS, width), f32),
            pltpu.VMEM((24, 8, width), f32),
            pltpu.VMEM((ROWS, width), f32),
            pltpu.VMEM((3, nblocks * width), f32),
            pltpu.VMEM((nblocks * width, 384), bf16),
            pltpu.VMEM((64, 384), bf16),
            pltpu.VMEM((nblocks, 16, width), f32),
            pltpu.VMEM((25 * 32, width), f32),
            pltpu.VMEM((8, width), jnp.int32),
            pltpu.SMEM((26 * 8, width), jnp.int32),
            dma, dma((4,)),
        ],
        compiler_params=pltpu.CompilerParams(vmem_limit_bytes=56 << 20),
    )(window.reshape(24 * ROWS, width), window.reshape(24, ROWS, width), far)
    return force.transpose(1, 0, 2)


def solution(mesh):
    placed = (
        P(("space", "sub"), None, None),
        P(("space", "sub")),
        P(),
        P(("space", "sub"), None),
        P(("space", "sub")),
    )
    return jax.shard_map(
        on_device,
        mesh=mesh,
        in_specs=placed,
        out_specs=P(("space", "sub"), None, None),
        check_vma=False,
    )
```

```python
import functools

import jax
import jax.numpy as jnp
from jax import lax
from jax.experimental import pallas as pl
from jax.experimental.pallas import tpu as pltpu
from jax.sharding import PartitionSpec as P

MESH = pl.DeviceIdType.MESH
f32 = jnp.float32
bf16 = jnp.bfloat16
ROWS = 296
RING = 6
UNROLL = 8


def three(x):
    a = x.astype(bf16).astype(f32)
    r = x - a
    b = r.astype(bf16).astype(f32)
    return a, b, (r - b).astype(bf16).astype(f32)


def exchange_and_far(
    seg_hbm, cell_hbm, cc_hbm, pair_hbm, live_hbm, far_hbm, win,
    seg_ref, cell_row, cc_ref, pair_ref, live_ref, cell_ref,
    payload, flat, mine, twin, pair_sum, parts, moments, cells_f, segs_f, acc, early, far_ref,
    in_sem, x_send, x_recv, z_send, z_recv, r_send, r_recv,
    twin_send, twin_recv, p_send, p_recv, y_send, y_recv, m_send, m_recv, own_sem, far_sem,
):
    space = lax.axis_index("space")
    sub = lax.axis_index("sub")
    y, x = space // 4, space % 4
    z, core = sub // 2, sub % 2
    nblocks = seg_ref.shape[1]
    ncell = cc_ref.shape[1]
    per = ncell // 16
    other_core = (space, z * 2 + 1 - core)

    def along_z(k):
        return (space, (z + k) % 4 * 2 + core)

    def along_y(k):
        return ((y + k) % 4 * 4 + x, sub)

    def along_x(k):
        return (y * 4 + (x + k) % 4, sub)

    def along_space(k):
        return ((space + k) % 16, sub)

    ins = [
        pltpu.make_async_copy(src, dst, in_sem.at[i])
        for i, (src, dst) in enumerate(
            [
                (cell_hbm, cell_row), (cc_hbm, cc_ref), (seg_hbm, seg_ref),
                (pair_hbm, pair_ref), (live_hbm, live_ref),
            ]
        )
    ]
    for copy in ins:
        copy.start()
    barrier = pltpu.get_barrier_semaphore()
    partners = [other_core, along_space(1), along_space(15)]
    partners += [to(k) for to in (along_z, along_y, along_x) for k in (1, 2, 3)]
    for to in partners:
        pl.semaphore_signal(barrier, inc=1, device_id=to, device_id_type=MESH)

    for copy in ins:
        copy.wait()

    base = space * per
    own_cc = cc_ref[:, pl.ds(pl.multiple_of(base, 256), per)]
    square = lax.broadcasted_iota(jnp.int32, (nblocks, nblocks), 0)
    lane = lax.broadcasted_iota(jnp.int32, (nblocks, nblocks), 1)
    cell = jnp.sum(
        jnp.where(square == lane, cell_row[...].astype(f32), 0.0), axis=1, keepdims=True
    )
    cell_ref[...] = jnp.broadcast_to(cell, (nblocks, 128)).astype(jnp.int32)
    hot = (
        cell.astype(jnp.int32) - base
        == lax.broadcasted_iota(jnp.int32, (nblocks, per), 1)
    ).astype(f32)
    origin = []
    for a in range(3):
        centre = jnp.sum(hot * own_cc[a : a + 1], axis=1, keepdims=True)
        origin.append(centre[0:1])
        payload[pl.ds(a, nblocks, stride=9), :] = seg_ref[a] + centre
    for a in range(3, 9):
        payload[pl.ds(a, nblocks, stride=9), :] = seg_ref[a]
    alive = lax.broadcasted_iota(jnp.int32, (2, 128), 1) < live_ref[...]
    payload[288:290, :] = jnp.where(alive, pair_ref[...].astype(f32), -1.0)
    payload[290:296, :] = jnp.zeros((6, 128), f32)
    for a in range(3):
        for b in range(3):
            outer = jnp.sum(seg_ref[6 + a] * seg_ref[3 + b], axis=1, keepdims=True)
            row = jnp.sum(hot * outer, axis=0, keepdims=True)
            mine[3 * a + b : 3 * a + b + 1, :] = row[:, 0:128]
            mine[9 + 3 * a + b : 10 + 3 * a + b, :] = row[:, 128:256]

    def send(src, dst, send_sem, recv_sem, to):
        return pltpu.make_async_remote_copy(
            src_ref=src, dst_ref=dst, send_sem=send_sem, recv_sem=recv_sem,
            device_id=to, device_id_type=MESH,
        )

    def arrived(ref, sem):
        pltpu.make_async_copy(ref, ref, sem).wait()

    own_copy = pltpu.make_async_copy(payload, win.at[core, 0], own_sem)
    own_copy.start()
    pl.semaphore_wait(barrier, len(partners))

    to_twin = send(mine, twin, twin_send, twin_recv, other_core)
    to_z = [
        send(pair_sum, parts.at[3 - k], p_send.at[k - 1], p_recv.at[3 - k], along_z(k))
        for k in (1, 2, 3)
    ]
    to_y = [
        send(moments.at[0, 0], moments.at[0, 4 - k], y_send.at[k - 1], y_recv.at[3 - k], along_y(k))
        for k in (1, 2, 3)
    ]
    to_x = [
        send(moments.at[0], moments.at[4 - k], m_send.at[k - 1], m_recv.at[3 - k], along_x(k))
        for k in (1, 2, 3)
    ]
    after = send(payload, win.at[core, 4], x_send.at[0], x_recv.at[0], along_space(1))
    before = send(payload, win.at[core, 5], x_send.at[1], x_recv.at[1], along_space(15))
    step = 1 + 2 * core

    def place(group, dz):
        return win.at[core, dz] if group == 0 else win.at[core, 3 + group + 2 * dz]

    def spread(group, k):
        return send(
            payload if group == 0 else place(group, 0), place(group, 4 - k),
            z_send.at[group, k // 2], z_recv.at[group, 3 - k], along_z(k),
        )

    def forward(group):
        return send(
            place(group, 4 - step), place(group, 2),
            z_send.at[group, 2], z_recv.at[group, 1], along_z(step),
        )

    relayed = [(0, 4), (4, 6), (6, 8), (10, 12), (8, 10)]

    def relay(i):
        part = win.at[core, relayed[i][0] : relayed[i][1]]
        return send(part, part, r_send.at[i], r_recv.at[i], other_core)

    to_twin.start()
    after.start()
    before.start()
    for k in (1, 3):
        spread(0, k).start()

    for g in range(nblocks):
        lanes = slice(g * 128, g * 128 + 128)
        flat[0:3, lanes] = payload[9 * g : 9 * g + 3, :]
        flat[8:11, lanes] = payload[9 * g + 3 : 9 * g + 6, :]
    row3 = lax.broadcasted_iota(jnp.int32, (3, 1), 0)
    origin = jnp.where(row3 == 0, origin[0], jnp.where(row3 == 1, origin[1], origin[2]))
    ones = jnp.ones((3, ncell), f32)
    blank = jnp.zeros((8, ncell), f32)
    c = cc_ref[...] - origin
    c1, c2, c3 = three(c)
    cq = jnp.concatenate(three(jnp.sum(c * c, axis=0, keepdims=True)), axis=0)
    cells_f[...] = jnp.transpose(
        jnp.concatenate([c1, c1, c2, c2, c1, c3, cq, ones, blank], axis=0)
    ).astype(bf16)
    p = flat[0:3, :] - origin
    p1, p2, p3 = three(-2.0 * p)
    pq = jnp.concatenate(three(1.0 + jnp.sum(p * p, axis=0, keepdims=True)), axis=0)
    segs_f[...] = jnp.concatenate(
        [p1, p2, p1, p2, p3, p1, ones, pq, blank], axis=0
    ).astype(bf16)

    def region_of(dx, dy):
        return (y + dy) % 4 * 4 + (x + dx) % 4

    def weights(region, first):
        at = pl.multiple_of(region * per, 256)
        dist = jnp.dot(cells_f[pl.ds(at, per), :], segs_f[...], preferred_element_type=f32)
        w = pl.reciprocal(dist, approx=True)
        if first:
            cell_id = at + lax.broadcasted_iota(jnp.int32, (per, 128), 0)
            w = jnp.concatenate(
                [
                    jnp.where(
                        cell_id == cell_ref[g : g + 1, :], 0.0, w[:, g * 128 : g * 128 + 128]
                    )
                    for g in range(nblocks)
                ],
                axis=1,
            )
        hi = w.astype(bf16)
        return hi, (w - hi.astype(f32)).astype(bf16)

    def product(dx, dy, hi, lo):
        m = moments[dx, dy]
        m = jnp.concatenate([m[0:9], m[9:18]], axis=1)
        m = jnp.concatenate([m, jnp.zeros((7, per), f32)], axis=0)
        m_hi = m.astype(bf16)
        m = jnp.concatenate([m_hi, (m - m_hi.astype(f32)).astype(bf16)], axis=0)
        return jnp.dot(m, hi, preferred_element_type=f32) + jnp.dot(
            m, lo, preferred_element_type=f32
        )

    def make(k):
        early[k % RING, 0], early[k % RING, 1] = weights(region_of(k // 4, k % 4), False)

    def use(k):
        acc[...] += product(k // 4, k % 4, early[k % RING, 0], early[k % RING, 1])

    def makes(k, carry):
        make(k)
        return carry

    def one_use(k, behind):
        use(k - behind)
        make(k)
        return behind

    def two_uses(k, ahead):
        use(2 * k - ahead)
        use(2 * k - ahead + 1)
        make(k)
        return ahead

    acc[...] = jnp.zeros_like(acc)
    early[0, 0], early[0, 1] = weights(space, True)

    arrived(twin, twin_recv)
    pair_sum[...] = mine[...] + twin[...]
    for copy in to_z:
        copy.start()
    lax.fori_loop(1, 3, makes, 0)

    region = pair_sum[...]
    for k in range(3):
        arrived(parts.at[k], p_recv.at[k])
        region = region + parts[k]
    moments[0, 0] = region
    for copy in to_y:
        copy.start()
    for group in (1, 2):
        arrived(place(group, 0), x_recv.at[group - 1])
        for k in (1, 3):
            spread(group, k).start()
    relay(1).start()
    lax.fori_loop(3, 5, makes, 0)

    for k in range(3):
        arrived(moments.at[0, k + 1], y_recv.at[k])
    for copy in to_x:
        copy.start()
    for dz in (1, 3):
        arrived(place(0, dz), z_recv.at[0, dz - 1])
    forward(0).start()
    lax.fori_loop(5, 7, one_use, 5)

    for dz in (1, 3):
        arrived(place(1, dz), z_recv.at[1, dz - 1])
    forward(1).start()
    lax.fori_loop(7, 9, one_use, 5)

    for dz in (1, 3):
        arrived(place(2, dz), z_recv.at[2, dz - 1])
    forward(2).start()
    relay(2).start()
    relay(3).start()
    arrived(place(0, 2), z_recv.at[0, 1])
    own_copy.wait()
    relay(0).start()
    arrived(moments.at[1], m_recv.at[0])
    lax.fori_loop(9, 11, two_uses, 14)

    for group in (1, 2):
        arrived(place(group, 2), z_recv.at[group, 1])
    relay(4).start()
    arrived(moments.at[2], m_recv.at[1])
    lax.fori_loop(11, 12, two_uses, 14)
    lax.fori_loop(12, 13, one_use, 2)
    arrived(moments.at[3], m_recv.at[2])
    lax.fori_loop(13, 16, one_use, 2)
    use(14)
    use(15)

    grid = acc[0:9, :] + acc[16:25, :]
    line = flat[8:11, :]
    for a in range(3):
        far_ref[a : a + 1, :] = jnp.sum(
            grid[3 * a : 3 * a + 3, :] * line, axis=0, keepdims=True
        )

    far_copy = pltpu.make_async_copy(far_ref, far_hbm, far_sem)
    far_copy.start()

    for i, (lo, hi) in enumerate(relayed):
        arrived(win.at[1 - core, lo:hi], r_recv.at[i])
    for copy in [to_twin, after, before] + to_z + to_y + to_x:
        copy.wait_send()
    for group in range(3):
        for k in (1, 3):
            spread(group, k).wait_send()
        forward(group).wait_send()
    for i in range(len(relayed)):
        relay(i).wait_send()
    far_copy.wait()


def arrangement():
    r = lax.broadcasted_iota(jnp.int32, (64, 256), 0)
    q = lax.broadcasted_iota(jnp.int32, (64, 256), 1)
    kind, col = q // 128, q % 128
    group, line = col // 16, col % 16
    mate = jnp.where(group < 3, group, jnp.where(group < 5, group - 3, 0))
    same = (group < 6) & (r == mate * 16 + line)
    dist = (kind == 0) & same & (line < 3)
    extra = (kind == 0) & (group == 6) & (
        ((line < 3) & (r == 48 + 3 + line)) | ((line >= 3) & (line < 6) & (r == 48))
    )
    couple = (kind == 1) & same & (line >= 3) & (line < 12)
    return jnp.where(dist, -2.0, jnp.where(extra | couple, 1.0, 0.0)).astype(bf16)


def block_rows(ref, row, origin, first, second):
    row16 = lax.broadcasted_iota(jnp.int32, (16, 128), 0)
    u = [ref[pl.ds(row + first + k, 1), :] for k in range(3)]
    v = [ref[pl.ds(row + second + k, 1), :] for k in range(3)]
    left = jnp.where(row16 < 6, u[0], jnp.where(row16 < 9, u[1], u[2]))
    place = row16 % 3
    right = jnp.where(place == 0, v[0], jnp.where(place == 1, v[1], v[2]))
    both = jnp.where(row16 < 12, left * right, 0.0)
    return jnp.where(row16 < 3, ref[pl.ds(row, 16), :] - origin, both)


def split_rows(x, plus):
    row16 = lax.broadcasted_iota(jnp.int32, (16, 128), 0)
    a, b, c = three(x)
    sq = jnp.sum(jnp.where(row16 < 3, x * x, 0.0), axis=0, keepdims=True) + plus
    s1, s2, s3 = three(sq)
    ext = jnp.where(
        row16 < 3, 1.0,
        jnp.where(row16 == 3, s1, jnp.where(row16 == 4, s2, jnp.where(row16 == 5, s3, 0.0))),
    )
    return a.astype(bf16), b.astype(bf16), c.astype(bf16), ext.astype(bf16)


def build_list(pair_ref, space, sub, nblocks, hots, listed, table, sem):
    first_block = ((space * 8 + sub) * nblocks).astype(f32)
    target = jnp.concatenate(
        [pair_ref[d, 0:1, :] for d in range(24)] + [pair_ref[sub % 2 * 12, 0:1, :]],
        axis=0,
    )
    source = jnp.concatenate(
        [pair_ref[d, 1:2, :] for d in range(24)] + [pair_ref[sub % 2 * 12, 1:2, :]],
        axis=0,
    )
    is_own = lax.broadcasted_iota(jnp.int32, (25, 128), 0) == 24
    mine = jnp.where(is_own, target, source) - first_block
    theirs = jnp.where(is_own, source, target)
    used = (source >= 0) & (mine >= 0) & (mine < nblocks)
    mine = jnp.where(used, mine, -1.0)
    owner = jnp.floor(theirs * (1.0 / 32))
    their_space = jnp.floor(owner * (1.0 / 8))
    their_sub = owner - 8.0 * their_space
    their_z = jnp.floor(their_sub * 0.5)
    ahead = their_space - space.astype(f32)
    ahead = jnp.where(ahead < -8, ahead + 16.0, jnp.where(ahead > 8, ahead - 16.0, ahead))
    dz = their_z - (sub // 2).astype(f32)
    dz = jnp.where(dz < 0, dz + 4.0, dz)
    dev = (their_sub - 2.0 * their_z) * 12.0 + jnp.where(
        ahead == 0, dz, 4.0 + 2.0 * dz + (ahead > 0).astype(f32)
    )
    local = theirs - 32.0 * owner
    before = (
        lax.broadcasted_iota(jnp.int32, (128, 128), 0)
        < lax.broadcasted_iota(jnp.int32, (128, 128), 1)
    ).astype(bf16)
    block_id = lax.broadcasted_iota(jnp.int32, (32, 128), 0).astype(f32)
    run = jnp.zeros((32, 1), f32)
    hots[...] = jnp.concatenate(
        [(mine[r : r + 1] == block_id).astype(f32) for r in range(25)], axis=0
    )
    within = jnp.dot(hots[...].astype(bf16), before, preferred_element_type=f32)
    sums = jnp.sum(hots[...], axis=1, keepdims=True)
    runs = []
    for r in range(25):
        runs.append(run)
        run = run + sums[32 * r : 32 * r + 32]
    even = 2.0 * jnp.floor((run + 1.0) * 0.5)
    above = (
        lax.broadcasted_iota(jnp.int32, (32, 32), 1)
        < lax.broadcasted_iota(jnp.int32, (32, 32), 0)
    ).astype(f32)
    starts = jnp.dot(
        above, jnp.broadcast_to(even, (32, 128)), precision=lax.Precision.HIGHEST,
        preferred_element_type=f32,
    )[:, 0:1]
    count = jnp.sum(even).astype(jnp.int32)
    ranks = []
    for r in range(25):
        h = hots[32 * r : 32 * r + 32, :]
        at = within[32 * r : 32 * r + 32] + (runs[r] + starts)
        ranks.append(jnp.sum(h * at, axis=0, keepdims=True))
    rank = jnp.where(used, jnp.concatenate(ranks, axis=0), -1.0)
    pad = jnp.full((128 - 25, 128), -1.0, f32)
    rank_t = jnp.transpose(jnp.concatenate([rank, pad], axis=0))
    lane = lax.broadcasted_iota(jnp.int32, (128, 128), 1).astype(f32)
    row8 = lax.broadcasted_iota(jnp.int32, (8, 128), 0)
    ends = starts + even

    def fill(kr, carry):
        got = jnp.zeros((8, 128), f32)
        first = (kr * 128).astype(f32)
        want = lane + first
        for r in range(25):
            hot = (rank_t[:, r : r + 1] == want).astype(bf16)
            vals = jnp.where(row8 == 0, dev[r : r + 1], jnp.where(row8 == 1, local[r : r + 1], 1.0))
            vals = jnp.where((row8 < 3) & used[r : r + 1], vals, 0.0)
            got = got + jnp.dot(vals.astype(bf16), hot, preferred_element_type=f32)
        other = got[0:1] * float(ROWS) + got[1:2] * 9.0
        own = jnp.sum((ends <= want[0:32]).astype(f32), axis=0, keepdims=True)
        own = jnp.minimum(own, 31.0)
        rows = jnp.where(
            row8 == 0, other, jnp.where(row8 == 1, own, jnp.where(row8 == 2, got[2:3], 0.0))
        )
        listed[...] = rows.astype(jnp.int32)
        copy = pltpu.make_async_copy(listed, table.at[pl.ds(kr * 8, 8)], sem)
        copy.start()
        copy.wait()
        return carry

    lax.fori_loop(0, (count + 127) // 128, fill, 0)
    return count


def near_kernel(
    win_hbm, pair_hbm, far_hbm, out_ref,
    win_ref, pair_ref, own_ref, far_ref, feats, arrange, unit, acc, hots, listed, table, sem, in_sem,
):
    space, sub = lax.axis_index("space"), lax.axis_index("sub")
    nblocks = out_ref.shape[1]
    my_row = pl.multiple_of(sub % 2 * 12 * ROWS, 8)
    pairs_in = pltpu.make_async_copy(pair_hbm.at[:, 288:296], pair_ref, in_sem.at[0])
    own_in = pltpu.make_async_copy(win_hbm.at[pl.ds(my_row, ROWS)], own_ref, in_sem.at[1])
    win_in = pltpu.make_async_copy(win_hbm, win_ref, in_sem.at[2])
    far_in = pltpu.make_async_copy(far_hbm, far_ref, in_sem.at[3])
    for copy in (pairs_in, own_in, win_in, far_in):
        copy.start()
    pairs_in.wait()
    count = build_list(pair_ref, space, sub, nblocks, hots, listed, table, sem)
    own_in.wait()
    origin = jnp.where(
        lax.broadcasted_iota(jnp.int32, (16, 1), 0) < 3, own_ref[0:16, 0:1], 0.0
    )

    arrange[...] = arrangement()
    acc[...] = jnp.zeros_like(acc)
    row16 = lax.broadcasted_iota(jnp.int32, (16, 128), 0)
    for q in range(0, nblocks, 8):
        parts = []
        for g in range(q, q + 8):
            x = block_rows(own_ref, 9 * g, origin, 6, 3)
            size = jnp.max(jnp.where(row16 < 3, 0.0, jnp.abs(x)), axis=0, keepdims=True)
            size = jnp.maximum(jnp.max(size, axis=1, keepdims=True), 1e-30)
            unit[g : g + 1, :] = jnp.broadcast_to(size, (1, 128))
            x = jnp.where(row16 < 3, x, x * (1.0 / size))
            parts.append(jnp.concatenate(split_rows(x, 0.25), axis=0))
        f = lax.dot_general(
            jnp.concatenate(parts, axis=1), arrange[...], (((0,), (0,)), ((), ())),
            preferred_element_type=f32,
        )
        feats[q * 128 : q * 128 + 1024, :] = f.astype(bf16)

    win_in.wait()
    half = lax.broadcasted_iota(jnp.int32, (1, 256), 1) < 128
    top = lax.broadcasted_iota(jnp.int32, (16, 128), 0) < 3

    def items(step, carry):
        work = []
        for u in range(UNROLL):
            k = (step * UNROLL + u) * 2
            inside = k < count
            k = jnp.minimum(k, count - 2)
            row = k // 128 * 8
            col = k % 128
            own = table[row + 1, col]
            rhs = []
            alive = []
            for v in range(2):
                other = table[row, col + v]
                alive.append(jnp.where(inside, table[row + 2, col + v], 0).astype(f32))
                a, b, c, ext = split_rows(block_rows(win_ref, other, origin, 3, 6), 0.0)
                rhs.append(
                    jnp.concatenate(
                        [a, a, a, b, b, c, ext, jnp.zeros((16, 128), bf16)], axis=0
                    )
                )
            f = feats[pl.ds(pl.multiple_of(own * 128, 128), 128), :]
            f = jnp.concatenate([f[:, 0:128], f[:, 128:256]], axis=0)
            work.append((own, jnp.where(half, alive[0], alive[1]), f, jnp.concatenate(rhs, axis=1)))
        outs = [jnp.dot(f, rhs, preferred_element_type=f32) for _, _, f, rhs in work]
        sums = []
        for (own, live, _, rhs), out in zip(work, outs):
            inv = lax.rsqrt(jnp.maximum(out[0:128], 0.25))
            g = (inv * inv) * (inv * live) * out[128:256]
            hi = g.astype(bf16)
            lo = (g - hi.astype(f32)).astype(bf16)
            lhs = jnp.concatenate([rhs[0:16], rhs[48:64], rhs[80:112]], axis=0)
            dims = (((1,), (1,)), ((), ()))
            r = lax.dot_general(lhs, hi, dims, preferred_element_type=f32)
            r = r + lax.dot_general(lhs, lo, dims, preferred_element_type=f32)
            sums.append((own, jnp.where(top, r[0:16] + r[16:32] + r[32:48], r[48:49])))
        for own, r in sums:
            acc[own] += r
        return carry

    lax.fori_loop(0, (count // 2 + UNROLL - 1) // UNROLL, items, 0)

    far_in.wait()
    for g in range(nblocks):
        p = own_ref[9 * g : 9 * g + 16, :] - origin
        t = acc[g]
        near = (p[0:3] * t[3:4] - t[0:3]) * unit[g : g + 1, :]
        force = far_ref[0:3, g * 128 : g * 128 + 128] + near
        for a in range(3):
            out_ref[a, g : g + 1, :] = force[a : a + 1]


def on_device(seg_data, cell_of_block, cell_center, pairs, live_count):
    nblocks, _, width = seg_data.shape
    ncell = cell_center.shape[1]
    slots = pairs.shape[0]
    vmem = pl.BlockSpec(memory_space=pltpu.VMEM)
    hbm = pl.BlockSpec(memory_space=pltpu.HBM)
    dma = pltpu.SemaphoreType.DMA
    far, window = pl.pallas_call(
        exchange_and_far,
        out_shape=(
            jax.ShapeDtypeStruct((3, nblocks * width), f32),
            jax.ShapeDtypeStruct((2, 12, ROWS, width), f32),
        ),
        in_specs=[hbm] * 5,
        out_specs=(hbm, hbm),
        scratch_shapes=[
            pltpu.VMEM((9, nblocks, width), f32),
            pltpu.VMEM((1, nblocks), jnp.int32),
            pltpu.VMEM((3, ncell), f32),
            pltpu.VMEM((2, slots), jnp.int32),
            pltpu.VMEM((1, 1), jnp.int32),
            pltpu.VMEM((nblocks, width), jnp.int32),
            pltpu.VMEM((ROWS, width), f32),
            pltpu.VMEM((16, nblocks * width), f32),
            pltpu.VMEM((18, 128), f32),
            pltpu.VMEM((18, 128), f32),
            pltpu.VMEM((18, 128), f32),
            pltpu.VMEM((3, 18, 128), f32),
            pltpu.VMEM((4, 4, 18, 128), f32),
            pltpu.VMEM((ncell, 32), bf16),
            pltpu.VMEM((32, nblocks * width), bf16),
            pltpu.VMEM((32, nblocks * width), f32),
            pltpu.VMEM((RING, 2, ncell // 16, nblocks * width), bf16),
            pltpu.VMEM((3, nblocks * width), f32),
            dma((5,)), dma((2,)), dma((2,)), dma((3, 3)), dma((3, 3)), dma((5,)), dma((5,)),
            dma, dma, dma((3,)), dma((3,)), dma((3,)), dma((3,)), dma((3,)), dma((3,)), dma, dma,
        ],
        compiler_params=pltpu.CompilerParams(
            collective_id=0, has_side_effects=True, vmem_limit_bytes=56 << 20
        ),
    )(
        seg_data.transpose(1, 0, 2), cell_of_block[None, :], cell_center, pairs.T,
        live_count[None, :],
    )
    force = pl.pallas_call(
        near_kernel,
        out_shape=jax.ShapeDtypeStruct((3, nblocks, width), f32),
        in_specs=[hbm] * 3,
        out_specs=vmem,
        scratch_shapes=[
            pltpu.VMEM((24 * ROWS, width), f32),
            pltpu.VMEM((24, 8, width), f32),
            pltpu.VMEM((ROWS, width), f32),
            pltpu.VMEM((3, nblocks * width), f32),
            pltpu.VMEM((nblocks * width, 256), bf16),
            pltpu.VMEM((64, 256), bf16),
            pltpu.VMEM((nblocks, width), f32),
            pltpu.VMEM((nblocks, 16, width), f32),
            pltpu.VMEM((25 * 32, width), f32),
            pltpu.VMEM((8, width), jnp.int32),
            pltpu.SMEM((26 * 8, width), jnp.int32),
            dma, dma((4,)),
        ],
        compiler_params=pltpu.CompilerParams(vmem_limit_bytes=56 << 20),
    )(window.reshape(24 * ROWS, width), window.reshape(24, ROWS, width), far)
    return force.transpose(1, 0, 2)


def solution(mesh):
    placed = (
        P(("space", "sub"), None, None),
        P(("space", "sub")),
        P(),
        P(("space", "sub"), None),
        P(("space", "sub")),
    )
    return jax.shard_map(
        on_device,
        mesh=mesh,
        in_specs=placed,
        out_specs=P(("space", "sub"), None, None),
        check_vma=False,
    )
```

```python
import functools

import jax
import jax.numpy as jnp
from jax import lax
from jax.experimental import pallas as pl
from jax.experimental.pallas import tpu as pltpu
from jax.sharding import PartitionSpec as P

MESH = pl.DeviceIdType.MESH
f32 = jnp.float32
bf16 = jnp.bfloat16
ROWS = 296
UNROLL = 12


def three(x):
    a = x.astype(bf16).astype(f32)
    r = x - a
    b = r.astype(bf16).astype(f32)
    return a, b, (r - b).astype(bf16).astype(f32)


def exchange_and_far(
    seg_hbm, cell_hbm, cc_hbm, pair_hbm, live_hbm, far_hbm, win,
    seg_ref, cell_row, cc_ref, pair_ref, live_ref, cell_ref,
    payload, flat, mine, twin, pair_sum, parts, moments, cells_f, segs_f, acc, early, far_ref,
    in_sem, x_send, x_recv, z_send, z_recv, r_send, r_recv,
    twin_send, twin_recv, p_send, p_recv, y_send, y_recv, m_send, m_recv, own_sem, far_sem,
):
    space = lax.axis_index("space")
    sub = lax.axis_index("sub")
    y, x = space // 4, space % 4
    z, core = sub // 2, sub % 2
    nblocks = seg_ref.shape[1]
    ncell = cc_ref.shape[1]
    per = ncell // 16
    other_core = (space, z * 2 + 1 - core)

    def along_z(k):
        return (space, (z + k) % 4 * 2 + core)

    def along_y(k):
        return ((y + k) % 4 * 4 + x, sub)

    def along_x(k):
        return (y * 4 + (x + k) % 4, sub)

    def along_space(k):
        return ((space + k) % 16, sub)

    ins = [
        pltpu.make_async_copy(src, dst, in_sem.at[i])
        for i, (src, dst) in enumerate(
            [
                (cell_hbm, cell_row), (cc_hbm, cc_ref), (seg_hbm, seg_ref),
                (pair_hbm, pair_ref), (live_hbm, live_ref),
            ]
        )
    ]
    for copy in ins:
        copy.start()
    barrier = pltpu.get_barrier_semaphore()
    partners = [other_core, along_space(1), along_space(15)]
    partners += [to(k) for to in (along_z, along_y, along_x) for k in (1, 2, 3)]
    for to in partners:
        pl.semaphore_signal(barrier, inc=1, device_id=to, device_id_type=MESH)

    for copy in ins:
        copy.wait()

    base = space * per
    own_cc = cc_ref[:, pl.ds(pl.multiple_of(base, 256), per)]
    square = lax.broadcasted_iota(jnp.int32, (nblocks, nblocks), 0)
    lane = lax.broadcasted_iota(jnp.int32, (nblocks, nblocks), 1)
    cell = jnp.sum(
        jnp.where(square == lane, cell_row[...].astype(f32), 0.0), axis=1, keepdims=True
    )
    cell_ref[...] = jnp.broadcast_to(cell, (nblocks, 128)).astype(jnp.int32)
    hot = (
        cell.astype(jnp.int32) - base
        == lax.broadcasted_iota(jnp.int32, (nblocks, per), 1)
    ).astype(f32)
    origin = []
    for a in range(3):
        centre = jnp.sum(hot * own_cc[a : a + 1], axis=1, keepdims=True)
        origin.append(centre[0:1])
        payload[pl.ds(a, nblocks, stride=9), :] = seg_ref[a] + centre
    for a in range(3, 9):
        payload[pl.ds(a, nblocks, stride=9), :] = seg_ref[a]
    alive = lax.broadcasted_iota(jnp.int32, (2, 128), 1) < live_ref[...]
    payload[288:290, :] = jnp.where(alive, pair_ref[...].astype(f32), -1.0)
    payload[290:296, :] = jnp.zeros((6, 128), f32)
    for a in range(3):
        for b in range(3):
            outer = jnp.sum(seg_ref[6 + a] * seg_ref[3 + b], axis=1, keepdims=True)
            row = jnp.sum(hot * outer, axis=0, keepdims=True)
            mine[3 * a + b : 3 * a + b + 1, :] = row[:, 0:128]
            mine[9 + 3 * a + b : 10 + 3 * a + b, :] = row[:, 128:256]

    def send(src, dst, send_sem, recv_sem, to):
        return pltpu.make_async_remote_copy(
            src_ref=src, dst_ref=dst, send_sem=send_sem, recv_sem=recv_sem,
            device_id=to, device_id_type=MESH,
        )

    def arrived(ref, sem):
        pltpu.make_async_copy(ref, ref, sem).wait()

    own_copy = pltpu.make_async_copy(payload, win.at[core, 0], own_sem)
    own_copy.start()
    pl.semaphore_wait(barrier, len(partners))

    to_twin = send(mine, twin, twin_send, twin_recv, other_core)
    to_z = [
        send(pair_sum, parts.at[3 - k], p_send.at[k - 1], p_recv.at[3 - k], along_z(k))
        for k in (1, 2, 3)
    ]
    to_y = [
        send(moments.at[0, 0], moments.at[0, 4 - k], y_send.at[k - 1], y_recv.at[3 - k], along_y(k))
        for k in (1, 2, 3)
    ]
    to_x = [
        send(moments.at[0], moments.at[4 - k], m_send.at[k - 1], m_recv.at[3 - k], along_x(k))
        for k in (1, 2, 3)
    ]
    after = send(payload, win.at[core, 4], x_send.at[0], x_recv.at[0], along_space(1))
    before = send(payload, win.at[core, 5], x_send.at[1], x_recv.at[1], along_space(15))
    step = 1 + 2 * core

    def place(group, dz):
        return win.at[core, dz] if group == 0 else win.at[core, 3 + group + 2 * dz]

    def spread(group, k):
        return send(
            payload if group == 0 else place(group, 0), place(group, 4 - k),
            z_send.at[group, k // 2], z_recv.at[group, 3 - k], along_z(k),
        )

    def forward(group):
        return send(
            place(group, 4 - step), place(group, 2),
            z_send.at[group, 2], z_recv.at[group, 1], along_z(step),
        )

    relayed = [(0, 4), (4, 6), (6, 8), (10, 12), (8, 10)]

    def relay(i):
        part = win.at[core, relayed[i][0] : relayed[i][1]]
        return send(part, part, r_send.at[i], r_recv.at[i], other_core)

    to_twin.start()
    after.start()
    before.start()
    for k in (1, 3):
        spread(0, k).start()

    for g in range(nblocks):
        lanes = slice(g * 128, g * 128 + 128)
        flat[0:3, lanes] = payload[9 * g : 9 * g + 3, :]
        flat[8:11, lanes] = payload[9 * g + 3 : 9 * g + 6, :]
    row3 = lax.broadcasted_iota(jnp.int32, (3, 1), 0)
    origin = jnp.where(row3 == 0, origin[0], jnp.where(row3 == 1, origin[1], origin[2]))
    ones = jnp.ones((3, ncell), f32)
    blank = jnp.zeros((8, ncell), f32)
    c = cc_ref[...] - origin
    c1, c2, c3 = three(c)
    cq = jnp.concatenate(three(jnp.sum(c * c, axis=0, keepdims=True)), axis=0)
    cells_f[...] = jnp.transpose(
        jnp.concatenate([c1, c1, c2, c2, c1, c3, cq, ones, blank], axis=0)
    ).astype(bf16)
    p = flat[0:3, :] - origin
    p1, p2, p3 = three(-2.0 * p)
    pq = jnp.concatenate(three(1.0 + jnp.sum(p * p, axis=0, keepdims=True)), axis=0)
    segs_f[...] = jnp.concatenate(
        [p1, p2, p1, p2, p3, p1, ones, pq, blank], axis=0
    ).astype(bf16)

    def region_of(dx, dy):
        return (y + dy) % 4 * 4 + (x + dx) % 4

    def weights(region, first):
        at = pl.multiple_of(region * per, 256)
        dist = jnp.dot(cells_f[pl.ds(at, per), :], segs_f[...], preferred_element_type=f32)
        w = pl.reciprocal(dist, approx=True)
        if first:
            cell_id = at + lax.broadcasted_iota(jnp.int32, (per, 128), 0)
            w = jnp.concatenate(
                [
                    jnp.where(
                        cell_id == cell_ref[g : g + 1, :], 0.0, w[:, g * 128 : g * 128 + 128]
                    )
                    for g in range(nblocks)
                ],
                axis=1,
            )
        hi = w.astype(bf16)
        return hi, (w - hi.astype(f32)).astype(bf16)

    def product(dx, dy, hi, lo):
        m = moments[dx, dy]
        m = jnp.concatenate([m[0:9], m[9:18]], axis=1)
        m = jnp.concatenate([m, jnp.zeros((7, per), f32)], axis=0)
        m_hi = m.astype(bf16)
        m = jnp.concatenate([m_hi, (m - m_hi.astype(f32)).astype(bf16)], axis=0)
        return jnp.dot(m, hi, preferred_element_type=f32) + jnp.dot(
            m, lo, preferred_element_type=f32
        )

    def make(k, carry):
        early[k, 0], early[k, 1] = weights(region_of(0, k), False)
        return carry

    def two(j, carry):
        k = 2 * j
        dx, dy = k // 4, k % 4
        hi, lo = weights(region_of(dx, dy), False)
        hi2, lo2 = weights(region_of(dx, dy + 1), False)
        acc[...] += product(dx, dy, hi, lo) + product(dx, dy + 1, hi2, lo2)
        return carry

    early[0, 0], early[0, 1] = weights(space, True)

    arrived(twin, twin_recv)
    pair_sum[...] = mine[...] + twin[...]
    for copy in to_z:
        copy.start()
    lax.fori_loop(1, 2, make, 0)

    region = pair_sum[...]
    for k in range(3):
        arrived(parts.at[k], p_recv.at[k])
        region = region + parts[k]
    moments[0, 0] = region
    for copy in to_y:
        copy.start()
    lax.fori_loop(2, 4, make, 0)
    for group in (1, 2):
        arrived(place(group, 0), x_recv.at[group - 1])
        for k in (1, 3):
            spread(group, k).start()
    relay(1).start()
    acc[...] = product(0, 0, early[0, 0], early[0, 1])

    for k in range(3):
        arrived(moments.at[0, k + 1], y_recv.at[k])
    for copy in to_x:
        copy.start()
    for dz in (1, 3):
        arrived(place(0, dz), z_recv.at[0, dz - 1])
    forward(0).start()
    acc[...] += (
        product(0, 1, early[1, 0], early[1, 1])
        + product(0, 2, early[2, 0], early[2, 1])
        + product(0, 3, early[3, 0], early[3, 1])
    )

    arrived(moments.at[1], m_recv.at[0])
    lax.fori_loop(2, 3, two, 0)
    for dz in (1, 3):
        arrived(place(1, dz), z_recv.at[1, dz - 1])
    forward(1).start()
    lax.fori_loop(3, 4, two, 0)
    for dz in (1, 3):
        arrived(place(2, dz), z_recv.at[2, dz - 1])
    forward(2).start()
    relay(2).start()
    relay(3).start()
    arrived(place(0, 2), z_recv.at[0, 1])
    own_copy.wait()
    relay(0).start()
    arrived(moments.at[2], m_recv.at[1])
    lax.fori_loop(4, 6, two, 0)
    for group in (1, 2):
        arrived(place(group, 2), z_recv.at[group, 1])
    relay(4).start()
    arrived(moments.at[3], m_recv.at[2])
    lax.fori_loop(6, 8, two, 0)

    grid = acc[0:9, :] + acc[16:25, :]
    line = flat[8:11, :]
    for a in range(3):
        far_ref[a : a + 1, :] = jnp.sum(
            grid[3 * a : 3 * a + 3, :] * line, axis=0, keepdims=True
        )

    far_copy = pltpu.make_async_copy(far_ref, far_hbm, far_sem)
    far_copy.start()

    for i, (lo, hi) in enumerate(relayed):
        arrived(win.at[1 - core, lo:hi], r_recv.at[i])
    for copy in [to_twin, after, before] + to_z + to_y + to_x:
        copy.wait_send()
    for group in range(3):
        for k in (1, 3):
            spread(group, k).wait_send()
        forward(group).wait_send()
    for i in range(len(relayed)):
        relay(i).wait_send()
    far_copy.wait()


def arrangement():
    q = lax.broadcasted_iota(jnp.int32, (256, 64), 0)
    r = lax.broadcasted_iota(jnp.int32, (256, 64), 1)
    kind, col = q // 128, q % 128
    group, line = col // 16, col % 16
    mate = jnp.where(group < 3, group, jnp.where(group < 5, group - 3, 0))
    same = (group < 6) & (r == mate * 16 + line)
    dist = (kind == 0) & same & (line < 3)
    extra = (kind == 0) & (group == 6) & (
        ((line < 3) & (r == 48 + 3 + line)) | ((line >= 3) & (line < 6) & (r == 48))
    )
    couple = (kind == 1) & same & (line >= 3) & (line < 12)
    return jnp.where(dist, -2.0, jnp.where(extra | couple, 1.0, 0.0)).astype(bf16)


def block_rows(ref, row, origin, first, second):
    row16 = lax.broadcasted_iota(jnp.int32, (16, 128), 0)
    u = [ref[pl.ds(row + first + k, 1), :] for k in range(3)]
    v = [ref[pl.ds(row + second + k, 1), :] for k in range(3)]
    left = jnp.where(row16 < 6, u[0], jnp.where(row16 < 9, u[1], u[2]))
    place = row16 % 3
    right = jnp.where(place == 0, v[0], jnp.where(place == 1, v[1], v[2]))
    both = jnp.where(row16 < 12, left * right, 0.0)
    return jnp.where(row16 < 3, ref[pl.ds(row, 16), :] - origin, both)


def split_rows(x, plus):
    row16 = lax.broadcasted_iota(jnp.int32, (16, 128), 0)
    a, b, c = three(x)
    sq = jnp.sum(jnp.where(row16 < 3, x * x, 0.0), axis=0, keepdims=True) + plus
    s1, s2, s3 = three(sq)
    ext = jnp.where(
        row16 < 3, 1.0,
        jnp.where(row16 == 3, s1, jnp.where(row16 == 4, s2, jnp.where(row16 == 5, s3, 0.0))),
    )
    return a.astype(bf16), b.astype(bf16), c.astype(bf16), ext.astype(bf16)


def build_list(pair_ref, space, sub, nblocks, hots, listed, table, sem):
    first_block = ((space * 8 + sub) * nblocks).astype(f32)
    target = jnp.concatenate(
        [pair_ref[d, 0:1, :] for d in range(24)] + [pair_ref[sub % 2 * 12, 0:1, :]],
        axis=0,
    )
    source = jnp.concatenate(
        [pair_ref[d, 1:2, :] for d in range(24)] + [pair_ref[sub % 2 * 12, 1:2, :]],
        axis=0,
    )
    is_own = lax.broadcasted_iota(jnp.int32, (25, 128), 0) == 24
    mine = jnp.where(is_own, target, source) - first_block
    theirs = jnp.where(is_own, source, target)
    used = (source >= 0) & (mine >= 0) & (mine < nblocks)
    mine = jnp.where(used, mine, -1.0)
    owner = jnp.floor(theirs * (1.0 / 32))
    their_space = jnp.floor(owner * (1.0 / 8))
    their_sub = owner - 8.0 * their_space
    their_z = jnp.floor(their_sub * 0.5)
    ahead = their_space - space.astype(f32)
    ahead = jnp.where(ahead < -8, ahead + 16.0, jnp.where(ahead > 8, ahead - 16.0, ahead))
    dz = their_z - (sub // 2).astype(f32)
    dz = jnp.where(dz < 0, dz + 4.0, dz)
    dev = (their_sub - 2.0 * their_z) * 12.0 + jnp.where(
        ahead == 0, dz, 4.0 + 2.0 * dz + (ahead > 0).astype(f32)
    )
    local = theirs - 32.0 * owner
    before = (
        lax.broadcasted_iota(jnp.int32, (128, 128), 0)
        < lax.broadcasted_iota(jnp.int32, (128, 128), 1)
    ).astype(bf16)
    block_id = lax.broadcasted_iota(jnp.int32, (32, 128), 0).astype(f32)
    run = jnp.zeros((32, 1), f32)
    hots[...] = jnp.concatenate(
        [(mine[r : r + 1] == block_id).astype(f32) for r in range(25)], axis=0
    )
    within = jnp.dot(hots[...].astype(bf16), before, preferred_element_type=f32)
    sums = jnp.sum(hots[...], axis=1, keepdims=True)
    runs = []
    for r in range(25):
        runs.append(run)
        run = run + sums[32 * r : 32 * r + 32]
    even = 2.0 * jnp.floor((run + 1.0) * 0.5)
    above = (
        lax.broadcasted_iota(jnp.int32, (32, 32), 1)
        < lax.broadcasted_iota(jnp.int32, (32, 32), 0)
    ).astype(f32)
    starts = jnp.dot(
        above, jnp.broadcast_to(even, (32, 128)), precision=lax.Precision.HIGHEST,
        preferred_element_type=f32,
    )[:, 0:1]
    count = jnp.sum(even).astype(jnp.int32)
    ranks = []
    for r in range(25):
        h = hots[32 * r : 32 * r + 32, :]
        at = within[32 * r : 32 * r + 32] + (runs[r] + starts)
        ranks.append(jnp.sum(h * at, axis=0, keepdims=True))
    rank = jnp.where(used, jnp.concatenate(ranks, axis=0), -1.0)
    pad = jnp.full((128 - 25, 128), -1.0, f32)
    rank_t = jnp.transpose(jnp.concatenate([rank, pad], axis=0))
    lane = lax.broadcasted_iota(jnp.int32, (128, 128), 1).astype(f32)
    row8 = lax.broadcasted_iota(jnp.int32, (8, 128), 0)
    ends = starts + even

    def fill(kr, carry):
        got = jnp.zeros((8, 128), f32)
        first = (kr * 128).astype(f32)
        want = lane + first
        for r in range(25):
            hot = (rank_t[:, r : r + 1] == want).astype(bf16)
            vals = jnp.where(row8 == 0, dev[r : r + 1], jnp.where(row8 == 1, local[r : r + 1], 1.0))
            vals = jnp.where((row8 < 3) & used[r : r + 1], vals, 0.0)
            got = got + jnp.dot(vals.astype(bf16), hot, preferred_element_type=f32)
        other = got[0:1] * float(ROWS) + got[1:2] * 9.0
        own = jnp.sum((ends <= want[0:32]).astype(f32), axis=0, keepdims=True)
        own = jnp.minimum(own, 31.0)
        rows = jnp.where(
            row8 == 0, other, jnp.where(row8 == 1, own, jnp.where(row8 == 2, got[2:3], 0.0))
        )
        listed[...] = rows.astype(jnp.int32)
        copy = pltpu.make_async_copy(listed, table.at[pl.ds(kr * 8, 8)], sem)
        copy.start()
        copy.wait()
        return carry

    lax.fori_loop(0, (count + 127) // 128, fill, 0)
    return count


def near_kernel(
    win_hbm, pair_hbm, far_hbm, out_ref,
    win_ref, pair_ref, own_ref, far_ref, feats, arrange, unit, acc, hots, listed, table, sem, in_sem,
):
    space, sub = lax.axis_index("space"), lax.axis_index("sub")
    nblocks = out_ref.shape[1]
    my_row = pl.multiple_of(sub % 2 * 12 * ROWS, 8)
    pairs_in = pltpu.make_async_copy(pair_hbm.at[:, 288:296], pair_ref, in_sem.at[0])
    own_in = pltpu.make_async_copy(win_hbm.at[pl.ds(my_row, ROWS)], own_ref, in_sem.at[1])
    win_in = pltpu.make_async_copy(win_hbm, win_ref, in_sem.at[2])
    far_in = pltpu.make_async_copy(far_hbm, far_ref, in_sem.at[3])
    for copy in (pairs_in, own_in, win_in, far_in):
        copy.start()
    pairs_in.wait()
    count = build_list(pair_ref, space, sub, nblocks, hots, listed, table, sem)
    own_in.wait()
    origin = jnp.where(
        lax.broadcasted_iota(jnp.int32, (16, 1), 0) < 3, own_ref[0:16, 0:1], 0.0
    )

    arrange[...] = arrangement()
    acc[...] = jnp.zeros_like(acc)
    row16 = lax.broadcasted_iota(jnp.int32, (16, 128), 0)
    for q in range(0, nblocks, 8):
        parts = []
        for g in range(q, q + 8):
            x = block_rows(own_ref, 9 * g, origin, 6, 3)
            size = jnp.max(jnp.where(row16 < 3, 0.0, jnp.abs(x)), axis=0, keepdims=True)
            size = jnp.maximum(jnp.max(size, axis=1, keepdims=True), 1e-30)
            unit[g : g + 1, :] = jnp.broadcast_to(size, (1, 128))
            x = jnp.where(row16 < 3, x, x * (1.0 / size))
            parts.append(jnp.concatenate(split_rows(x, 0.25), axis=0))
        f = jnp.dot(
            arrange[...], jnp.concatenate(parts, axis=1), preferred_element_type=f32
        ).astype(bf16)
        for g in range(8):
            feats[q + g, :, 0:128] = f[0:128, g * 128 : g * 128 + 128]
            feats[q + g, :, 128:256] = f[128:256, g * 128 : g * 128 + 128]

    win_in.wait()
    top = lax.broadcasted_iota(jnp.int32, (16, 128), 0) < 3

    def items(step, carry):
        work = []
        for u in range(UNROLL):
            k = (step * UNROLL + u) * 2
            inside = k < count
            k = jnp.minimum(k, count - 2)
            row = k // 128 * 8
            col = k % 128
            own = table[row + 1, col]
            rhs = []
            alive = []
            for v in range(2):
                other = table[row, col + v]
                alive.append(jnp.where(inside, table[row + 2, col + v], 0).astype(f32))
                a, b, c, ext = split_rows(block_rows(win_ref, other, origin, 3, 6), 0.0)
                rhs.append(
                    jnp.concatenate(
                        [a, a, a, b, b, c, ext, jnp.zeros((16, 128), bf16)], axis=0
                    )
                )
            work.append((own, alive, jnp.concatenate(rhs, axis=1)))
        outs = [
            lax.dot_general(
                rhs, feats[own], (((0,), (0,)), ((), ())), preferred_element_type=f32
            )
            for own, _, rhs in work
        ]
        sums = []
        for (own, alive, rhs), out in zip(work, outs):
            inv = lax.rsqrt(jnp.maximum(out[:, 0:128], 0.25))
            live = jnp.concatenate([inv[0:128] * alive[0], inv[128:256] * alive[1]], axis=0)
            g = (inv * inv) * live * out[:, 128:256]
            hi = g.astype(bf16)
            lo = (g - hi.astype(f32)).astype(bf16)
            lhs = jnp.concatenate([rhs[0:16], rhs[48:64], rhs[80:112]], axis=0)
            r = jnp.dot(lhs, hi, preferred_element_type=f32)
            r = r + jnp.dot(lhs, lo, preferred_element_type=f32)
            sums.append((own, jnp.where(top, r[0:16] + r[16:32] + r[32:48], r[48:49])))
        for own, r in sums:
            acc[own] += r
        return carry

    lax.fori_loop(0, (count // 2 + UNROLL - 1) // UNROLL, items, 0)

    far_in.wait()
    for g in range(nblocks):
        p = own_ref[9 * g : 9 * g + 16, :] - origin
        t = acc[g]
        near = (p[0:3] * t[3:4] - t[0:3]) * unit[g : g + 1, :]
        force = far_ref[0:3, g * 128 : g * 128 + 128] + near
        for a in range(3):
            out_ref[a, g : g + 1, :] = force[a : a + 1]


def on_device(seg_data, cell_of_block, cell_center, pairs, live_count):
    nblocks, _, width = seg_data.shape
    ncell = cell_center.shape[1]
    slots = pairs.shape[0]
    vmem = pl.BlockSpec(memory_space=pltpu.VMEM)
    hbm = pl.BlockSpec(memory_space=pltpu.HBM)
    dma = pltpu.SemaphoreType.DMA
    far, window = pl.pallas_call(
        exchange_and_far,
        out_shape=(
            jax.ShapeDtypeStruct((3, nblocks * width), f32),
            jax.ShapeDtypeStruct((2, 12, ROWS, width), f32),
        ),
        in_specs=[hbm] * 5,
        out_specs=(hbm, hbm),
        scratch_shapes=[
            pltpu.VMEM((9, nblocks, width), f32),
            pltpu.VMEM((1, nblocks), jnp.int32),
            pltpu.VMEM((3, ncell), f32),
            pltpu.VMEM((2, slots), jnp.int32),
            pltpu.VMEM((1, 1), jnp.int32),
            pltpu.VMEM((nblocks, width), jnp.int32),
            pltpu.VMEM((ROWS, width), f32),
            pltpu.VMEM((16, nblocks * width), f32),
            pltpu.VMEM((18, 128), f32),
            pltpu.VMEM((18, 128), f32),
            pltpu.VMEM((18, 128), f32),
            pltpu.VMEM((3, 18, 128), f32),
            pltpu.VMEM((4, 4, 18, 128), f32),
            pltpu.VMEM((ncell, 32), bf16),
            pltpu.VMEM((32, nblocks * width), bf16),
            pltpu.VMEM((32, nblocks * width), f32),
            pltpu.VMEM((4, 2, ncell // 16, nblocks * width), bf16),
            pltpu.VMEM((3, nblocks * width), f32),
            dma((5,)), dma((2,)), dma((2,)), dma((3, 3)), dma((3, 3)), dma((5,)), dma((5,)),
            dma, dma, dma((3,)), dma((3,)), dma((3,)), dma((3,)), dma((3,)), dma((3,)), dma, dma,
        ],
        compiler_params=pltpu.CompilerParams(
            collective_id=0, has_side_effects=True, vmem_limit_bytes=56 << 20
        ),
    )(
        seg_data.transpose(1, 0, 2), cell_of_block[None, :], cell_center, pairs.T,
        live_count[None, :],
    )
    force = pl.pallas_call(
        near_kernel,
        out_shape=jax.ShapeDtypeStruct((3, nblocks, width), f32),
        in_specs=[hbm] * 3,
        out_specs=vmem,
        scratch_shapes=[
            pltpu.VMEM((24 * ROWS, width), f32),
            pltpu.VMEM((24, 8, width), f32),
            pltpu.VMEM((ROWS, width), f32),
            pltpu.VMEM((3, nblocks * width), f32),
            pltpu.VMEM((nblocks, 128, 256), bf16),
            pltpu.VMEM((256, 64), bf16),
            pltpu.VMEM((nblocks, width), f32),
            pltpu.VMEM((nblocks, 16, width), f32),
            pltpu.VMEM((25 * 32, width), f32),
            pltpu.VMEM((8, width), jnp.int32),
            pltpu.SMEM((26 * 8, width), jnp.int32),
            dma, dma((4,)),
        ],
        compiler_params=pltpu.CompilerParams(vmem_limit_bytes=56 << 20),
    )(window.reshape(24 * ROWS, width), window.reshape(24, ROWS, width), far)
    return force.transpose(1, 0, 2)


def solution(mesh):
    placed = (
        P(("space", "sub"), None, None),
        P(("space", "sub")),
        P(),
        P(("space", "sub"), None),
        P(("space", "sub")),
    )
    return jax.shard_map(
        on_device,
        mesh=mesh,
        in_specs=placed,
        out_specs=P(("space", "sub"), None, None),
        check_vma=False,
    )
```

```python
import functools

import jax
import jax.numpy as jnp
from jax import lax
from jax.experimental import pallas as pl
from jax.experimental.pallas import tpu as pltpu
from jax.sharding import PartitionSpec as P

MESH = pl.DeviceIdType.MESH
f32 = jnp.float32
bf16 = jnp.bfloat16
ROWS = 296
UNROLL = 12


def three(x):
    a = x.astype(bf16).astype(f32)
    r = x - a
    b = r.astype(bf16).astype(f32)
    return a, b, (r - b).astype(bf16).astype(f32)


def exchange_and_far(
    seg_hbm, cell_hbm, cc_hbm, pair_hbm, live_hbm, far_hbm, win,
    seg_ref, cell_row, cc_ref, pair_ref, live_ref, cell_ref,
    payload, flat, mine, twin, pair_sum, parts, moments, cells_f, segs_f, acc, early, far_ref,
    in_sem, x_send, x_recv, z_send, z_recv, r_send, r_recv,
    twin_send, twin_recv, p_send, p_recv, y_send, y_recv, m_send, m_recv, own_sem, far_sem,
):
    space = lax.axis_index("space")
    sub = lax.axis_index("sub")
    y, x = lax.div(space, 4), lax.rem(space, 4)
    z, core = lax.div(sub, 2), lax.rem(sub, 2)
    nblocks = seg_ref.shape[1]
    ncell = cc_ref.shape[1]
    per = ncell // 16
    other_core = (space, z * 2 + 1 - core)

    def along_z(k):
        return (space, lax.rem(z + k, 4) * 2 + core)

    def along_y(k):
        return (lax.rem(y + k, 4) * 4 + x, sub)

    def along_x(k):
        return (y * 4 + lax.rem(x + k, 4), sub)

    def along_space(k):
        return (lax.rem(space + k, 16), sub)

    ins = [
        pltpu.make_async_copy(src, dst, in_sem.at[i])
        for i, (src, dst) in enumerate(
            [
                (cell_hbm, cell_row), (cc_hbm, cc_ref), (seg_hbm, seg_ref),
                (pair_hbm, pair_ref), (live_hbm, live_ref),
            ]
        )
    ]
    for copy in ins:
        copy.start()
    barrier = pltpu.get_barrier_semaphore()
    partners = [other_core, along_space(1), along_space(15)]
    partners += [to(k) for to in (along_z, along_y, along_x) for k in (1, 2, 3)]
    for to in partners:
        pl.semaphore_signal(barrier, inc=1, device_id=to, device_id_type=MESH)

    for copy in ins:
        copy.wait()

    base = space * per
    own_cc = cc_ref[:, pl.ds(pl.multiple_of(base, 256), per)]
    square = lax.broadcasted_iota(jnp.int32, (nblocks, nblocks), 0)
    lane = lax.broadcasted_iota(jnp.int32, (nblocks, nblocks), 1)
    cell = jnp.sum(
        jnp.where(square == lane, cell_row[...].astype(f32), 0.0), axis=1, keepdims=True
    )
    cell_ref[...] = jnp.broadcast_to(cell, (nblocks, 128)).astype(jnp.int32)
    hot = (
        cell.astype(jnp.int32) - base
        == lax.broadcasted_iota(jnp.int32, (nblocks, per), 1)
    ).astype(f32)
    origin = []
    for a in range(3):
        centre = jnp.sum(hot * own_cc[a : a + 1], axis=1, keepdims=True)
        origin.append(centre[0:1])
        payload[pl.ds(a, nblocks, stride=9), :] = seg_ref[a] + centre
    for a in range(3, 9):
        payload[pl.ds(a, nblocks, stride=9), :] = seg_ref[a]
    alive = lax.broadcasted_iota(jnp.int32, (2, 128), 1) < live_ref[...]
    payload[288:290, :] = jnp.where(alive, pair_ref[...].astype(f32), -1.0)
    payload[290:296, :] = jnp.zeros((6, 128), f32)
    for a in range(3):
        for b in range(3):
            outer = jnp.sum(seg_ref[6 + a] * seg_ref[3 + b], axis=1, keepdims=True)
            row = jnp.sum(hot * outer, axis=0, keepdims=True)
            mine[3 * a + b : 3 * a + b + 1, :] = row[:, 0:128]
            mine[9 + 3 * a + b : 10 + 3 * a + b, :] = row[:, 128:256]

    def send(src, dst, send_sem, recv_sem, to):
        return pltpu.make_async_remote_copy(
            src_ref=src, dst_ref=dst, send_sem=send_sem, recv_sem=recv_sem,
            device_id=to, device_id_type=MESH,
        )

    def arrived(ref, sem):
        pltpu.make_async_copy(ref, ref, sem).wait()

    own_copy = pltpu.make_async_copy(payload, win.at[core, 0], own_sem)
    own_copy.start()
    pl.semaphore_wait(barrier, len(partners))

    to_twin = send(mine, twin, twin_send, twin_recv, other_core)
    to_z = [
        send(pair_sum, parts.at[3 - k], p_send.at[k - 1], p_recv.at[3 - k], along_z(k))
        for k in (1, 2, 3)
    ]
    to_y = [
        send(moments.at[0, 0], moments.at[0, 4 - k], y_send.at[k - 1], y_recv.at[3 - k], along_y(k))
        for k in (1, 2, 3)
    ]
    to_x = [
        send(moments.at[0], moments.at[4 - k], m_send.at[k - 1], m_recv.at[3 - k], along_x(k))
        for k in (1, 2, 3)
    ]
    after = send(payload, win.at[core, 4], x_send.at[0], x_recv.at[0], along_space(1))
    before = send(payload, win.at[core, 5], x_send.at[1], x_recv.at[1], along_space(15))
    step = 1 + 2 * core

    def place(group, j):
        return win.at[core, j] if group == 0 else win.at[core, pl.ds(4 + 2 * j, 2)]

    def spread(group, j):
        return send(
            payload if group == 0 else place(1, 0), place(group, 2 - j),
            z_send.at[group, j], z_recv.at[group, 1 - j], along_z(1 + 2 * j),
        )

    def forward(group):
        return send(
            place(group, 2 - core), place(group, 3),
            z_send.at[group, 2], z_recv.at[group, 2], along_z(step),
        )

    relayed = [(0, 4), (4, 10), (10, 12)]

    def relay(i):
        part = win.at[core, relayed[i][0] : relayed[i][1]]
        return send(part, part, r_send.at[i], r_recv.at[i], other_core)

    to_twin.start()
    after.start()
    before.start()
    for j in (0, 1):
        spread(0, j).start()

    for g in range(nblocks):
        lanes = slice(g * 128, g * 128 + 128)
        flat[0:3, lanes] = payload[9 * g : 9 * g + 3, :]
        flat[8:11, lanes] = payload[9 * g + 3 : 9 * g + 6, :]
    row3 = lax.broadcasted_iota(jnp.int32, (3, 1), 0)
    origin = jnp.where(row3 == 0, origin[0], jnp.where(row3 == 1, origin[1], origin[2]))
    ones = jnp.ones((3, ncell), f32)
    blank = jnp.zeros((8, ncell), f32)
    c = cc_ref[...] - origin
    c1, c2, c3 = three(c)
    cq = jnp.concatenate(three(jnp.sum(c * c, axis=0, keepdims=True)), axis=0)
    cells_f[...] = jnp.transpose(
        jnp.concatenate([c1, c1, c2, c2, c1, c3, cq, ones, blank], axis=0)
    ).astype(bf16)
    p = flat[0:3, :] - origin
    p1, p2, p3 = three(-2.0 * p)
    pq = jnp.concatenate(three(1.0 + jnp.sum(p * p, axis=0, keepdims=True)), axis=0)
    segs_f[...] = jnp.concatenate(
        [p1, p2, p1, p2, p3, p1, ones, pq, blank], axis=0
    ).astype(bf16)

    def region_of(dx, dy):
        return lax.rem(y + dy, 4) * 4 + lax.rem(x + dx, 4)

    def weights(region, first):
        at = pl.multiple_of(region * per, 256)
        dist = jnp.dot(cells_f[pl.ds(at, per), :], segs_f[...], preferred_element_type=f32)
        w = pl.reciprocal(dist, approx=True)
        if first:
            cell_id = at + lax.broadcasted_iota(jnp.int32, (per, 128), 0)
            w = jnp.concatenate(
                [
                    jnp.where(
                        cell_id == cell_ref[g : g + 1, :], 0.0, w[:, g * 128 : g * 128 + 128]
                    )
                    for g in range(nblocks)
                ],
                axis=1,
            )
        hi = w.astype(bf16)
        return hi, (w - hi.astype(f32)).astype(bf16)

    def product(dx, dy, hi, lo):
        m = moments[dx, dy]
        m = jnp.concatenate([m[0:9], m[9:18]], axis=1)
        m = jnp.concatenate([m, jnp.zeros((7, per), f32)], axis=0)
        m_hi = m.astype(bf16)
        m = jnp.concatenate([m_hi, (m - m_hi.astype(f32)).astype(bf16)], axis=0)
        return jnp.dot(m, hi, preferred_element_type=f32) + jnp.dot(
            m, lo, preferred_element_type=f32
        )

    def make(k, carry):
        early[k, 0], early[k, 1] = weights(region_of(0, k), False)
        return carry

    def two(j, carry):
        k = 2 * j
        dx, dy = lax.div(k, 4), lax.rem(k, 4)
        hi, lo = weights(region_of(dx, dy), False)
        hi2, lo2 = weights(region_of(dx, dy + 1), False)
        acc[...] += product(dx, dy, hi, lo) + product(dx, dy + 1, hi2, lo2)
        return carry

    early[0, 0], early[0, 1] = weights(space, True)

    arrived(twin, twin_recv)
    pair_sum[...] = mine[...] + twin[...]
    for copy in to_z:
        copy.start()
    lax.fori_loop(1, 2, make, 0)

    region = pair_sum[...]
    for k in range(3):
        arrived(parts.at[k], p_recv.at[k])
        region = region + parts[k]
    moments[0, 0] = region
    for copy in to_y:
        copy.start()
    lax.fori_loop(2, 4, make, 0)
    for j in (0, 1):
        arrived(win.at[core, 4 + j], x_recv.at[j])
    for j in (0, 1):
        spread(1, j).start()
    acc[...] = product(0, 0, early[0, 0], early[0, 1])

    for k in range(3):
        arrived(moments.at[0, k + 1], y_recv.at[k])
    for copy in to_x:
        copy.start()
    for j in (0, 1):
        arrived(place(0, j + 1), z_recv.at[0, j])
    forward(0).start()
    acc[...] += (
        product(0, 1, early[1, 0], early[1, 1])
        + product(0, 2, early[2, 0], early[2, 1])
        + product(0, 3, early[3, 0], early[3, 1])
    )

    arrived(moments.at[1], m_recv.at[0])
    lax.fori_loop(2, 4, two, 0)
    for j in (0, 1):
        arrived(place(1, j + 1), z_recv.at[1, j])
    forward(1).start()
    relay(1).start()
    arrived(place(0, 3), z_recv.at[0, 2])
    own_copy.wait()
    relay(0).start()
    arrived(moments.at[2], m_recv.at[1])
    lax.fori_loop(4, 6, two, 0)
    arrived(place(1, 3), z_recv.at[1, 2])
    relay(2).start()
    arrived(moments.at[3], m_recv.at[2])
    lax.fori_loop(6, 8, two, 0)

    grid = acc[0:9, :] + acc[16:25, :]
    line = flat[8:11, :]
    for a in range(3):
        far_ref[a : a + 1, :] = jnp.sum(
            grid[3 * a : 3 * a + 3, :] * line, axis=0, keepdims=True
        )

    far_copy = pltpu.make_async_copy(far_ref, far_hbm, far_sem)
    far_copy.start()

    for i, (lo, hi) in enumerate(relayed):
        arrived(win.at[1 - core, lo:hi], r_recv.at[i])
    for copy in [to_twin, after, before] + to_z + to_y + to_x:
        copy.wait_send()
    for group in range(2):
        for j in (0, 1):
            spread(group, j).wait_send()
        forward(group).wait_send()
    for i in range(len(relayed)):
        relay(i).wait_send()
    far_copy.wait()


def arrangement():
    q = lax.broadcasted_iota(jnp.int32, (256, 64), 0)
    r = lax.broadcasted_iota(jnp.int32, (256, 64), 1)
    kind, col = q // 128, q % 128
    group, line = col // 16, col % 16
    mate = jnp.where(group < 3, group, jnp.where(group < 5, group - 3, 0))
    same = (group < 6) & (r == mate * 16 + line)
    dist = (kind == 0) & same & (line < 3)
    extra = (kind == 0) & (group == 6) & (
        ((line < 3) & (r == 48 + 3 + line)) | ((line >= 3) & (line < 6) & (r == 48))
    )
    couple = (kind == 1) & same & (line >= 3) & (line < 12)
    return jnp.where(dist, -2.0, jnp.where(extra | couple, 1.0, 0.0)).astype(bf16)


def block_rows(ref, row, origin, first, second):
    row16 = lax.broadcasted_iota(jnp.int32, (16, 128), 0)
    u = [ref[pl.ds(row + first + k, 1), :] for k in range(3)]
    v = [ref[pl.ds(row + second + k, 1), :] for k in range(3)]
    left = jnp.where(row16 < 6, u[0], jnp.where(row16 < 9, u[1], u[2]))
    place = row16 % 3
    right = jnp.where(place == 0, v[0], jnp.where(place == 1, v[1], v[2]))
    both = jnp.where(row16 < 12, left * right, 0.0)
    return jnp.where(row16 < 3, ref[pl.ds(row, 16), :] - origin, both)


def split_rows(x, plus):
    row16 = lax.broadcasted_iota(jnp.int32, (16, 128), 0)
    a, b, c = three(x)
    sq = jnp.sum(jnp.where(row16 < 3, x * x, 0.0), axis=0, keepdims=True) + plus
    s1, s2, s3 = three(sq)
    ext = jnp.where(
        row16 < 3, 1.0,
        jnp.where(row16 == 3, s1, jnp.where(row16 == 4, s2, jnp.where(row16 == 5, s3, 0.0))),
    )
    return a.astype(bf16), b.astype(bf16), c.astype(bf16), ext.astype(bf16)


def build_list(pair_ref, space, sub, nblocks, hots, listed, table, sem):
    first_block = ((space * 8 + sub) * nblocks).astype(f32)
    target = jnp.concatenate(
        [pair_ref[d, 0:1, :] for d in range(24)] + [pair_ref[sub % 2 * 12, 0:1, :]],
        axis=0,
    )
    source = jnp.concatenate(
        [pair_ref[d, 1:2, :] for d in range(24)] + [pair_ref[sub % 2 * 12, 1:2, :]],
        axis=0,
    )
    is_own = lax.broadcasted_iota(jnp.int32, (25, 128), 0) == 24
    mine = jnp.where(is_own, target, source) - first_block
    theirs = jnp.where(is_own, source, target)
    used = (source >= 0) & (mine >= 0) & (mine < nblocks)
    mine = jnp.where(used, mine, -1.0)
    owner = jnp.floor(theirs * (1.0 / 32))
    their_space = jnp.floor(owner * (1.0 / 8))
    their_sub = owner - 8.0 * their_space
    their_z = jnp.floor(their_sub * 0.5)
    ahead = their_space - space.astype(f32)
    ahead = jnp.where(ahead < -8, ahead + 16.0, jnp.where(ahead > 8, ahead - 16.0, ahead))
    dz = their_z - (sub // 2).astype(f32)
    dz = jnp.where(dz < 0, dz + 4.0, dz)
    dz = jnp.where(dz == 3, 2.0, jnp.where(dz == 2, 3.0, dz))
    dev = (their_sub - 2.0 * their_z) * 12.0 + jnp.where(
        ahead == 0, dz, 4.0 + 2.0 * dz + (ahead > 0).astype(f32)
    )
    local = theirs - 32.0 * owner
    before = (
        lax.broadcasted_iota(jnp.int32, (128, 128), 0)
        < lax.broadcasted_iota(jnp.int32, (128, 128), 1)
    ).astype(bf16)
    block_id = lax.broadcasted_iota(jnp.int32, (32, 128), 0).astype(f32)
    run = jnp.zeros((32, 1), f32)
    hots[...] = jnp.concatenate(
        [(mine[r : r + 1] == block_id).astype(f32) for r in range(25)], axis=0
    )
    within = jnp.dot(hots[...].astype(bf16), before, preferred_element_type=f32)
    sums = jnp.sum(hots[...], axis=1, keepdims=True)
    runs = []
    for r in range(25):
        runs.append(run)
        run = run + sums[32 * r : 32 * r + 32]
    even = 2.0 * jnp.floor((run + 1.0) * 0.5)
    above = (
        lax.broadcasted_iota(jnp.int32, (32, 32), 1)
        < lax.broadcasted_iota(jnp.int32, (32, 32), 0)
    ).astype(f32)
    starts = jnp.dot(
        above, jnp.broadcast_to(even, (32, 128)), precision=lax.Precision.HIGHEST,
        preferred_element_type=f32,
    )[:, 0:1]
    count = jnp.sum(even).astype(jnp.int32)
    ranks = []
    for r in range(25):
        h = hots[32 * r : 32 * r + 32, :]
        at = within[32 * r : 32 * r + 32] + (runs[r] + starts)
        ranks.append(jnp.sum(h * at, axis=0, keepdims=True))
    rank = jnp.where(used, jnp.concatenate(ranks, axis=0), -1.0)
    pad = jnp.full((128 - 25, 128), -1.0, f32)
    rank_t = jnp.transpose(jnp.concatenate([rank, pad], axis=0))
    lane = lax.broadcasted_iota(jnp.int32, (128, 128), 1).astype(f32)
    row8 = lax.broadcasted_iota(jnp.int32, (8, 128), 0)
    ends = starts + even

    def fill(kr, carry):
        got = jnp.zeros((8, 128), f32)
        first = (kr * 128).astype(f32)
        want = lane + first
        for r in range(25):
            hot = (rank_t[:, r : r + 1] == want).astype(bf16)
            vals = jnp.where(row8 == 0, dev[r : r + 1], jnp.where(row8 == 1, local[r : r + 1], 1.0))
            vals = jnp.where((row8 < 3) & used[r : r + 1], vals, 0.0)
            got = got + jnp.dot(vals.astype(bf16), hot, preferred_element_type=f32)
        other = got[0:1] * float(ROWS) + got[1:2] * 9.0
        own = jnp.sum((ends <= want[0:32]).astype(f32), axis=0, keepdims=True)
        own = jnp.minimum(own, 31.0)
        rows = jnp.where(
            row8 == 0, other, jnp.where(row8 == 1, own, jnp.where(row8 == 2, got[2:3], 0.0))
        )
        listed[...] = rows.astype(jnp.int32)
        copy = pltpu.make_async_copy(listed, table.at[pl.ds(kr * 8, 8)], sem)
        copy.start()
        copy.wait()
        return carry

    lax.fori_loop(0, (count + 127) // 128, fill, 0)
    return count


def near_kernel(
    win_hbm, pair_hbm, far_hbm, out_ref,
    win_ref, pair_ref, own_ref, far_ref, feats, arrange, unit, acc, hots, listed, table, sem, in_sem,
):
    space, sub = lax.axis_index("space"), lax.axis_index("sub")
    nblocks = out_ref.shape[1]
    my_row = pl.multiple_of(sub % 2 * 12 * ROWS, 8)
    pairs_in = pltpu.make_async_copy(pair_hbm.at[:, 288:296], pair_ref, in_sem.at[0])
    own_in = pltpu.make_async_copy(win_hbm.at[pl.ds(my_row, ROWS)], own_ref, in_sem.at[1])
    win_in = pltpu.make_async_copy(win_hbm, win_ref, in_sem.at[2])
    far_in = pltpu.make_async_copy(far_hbm, far_ref, in_sem.at[3])
    for copy in (pairs_in, own_in, win_in, far_in):
        copy.start()
    pairs_in.wait()
    count = build_list(pair_ref, space, sub, nblocks, hots, listed, table, sem)
    own_in.wait()
    origin = jnp.where(
        lax.broadcasted_iota(jnp.int32, (16, 1), 0) < 3, own_ref[0:16, 0:1], 0.0
    )

    arrange[...] = arrangement()
    acc[...] = jnp.zeros_like(acc)
    row16 = lax.broadcasted_iota(jnp.int32, (16, 128), 0)
    for q in range(0, nblocks, 8):
        parts = []
        for g in range(q, q + 8):
            x = block_rows(own_ref, 9 * g, origin, 6, 3)
            size = jnp.max(jnp.where(row16 < 3, 0.0, jnp.abs(x)), axis=0, keepdims=True)
            size = jnp.maximum(jnp.max(size, axis=1, keepdims=True), 1e-30)
            unit[g : g + 1, :] = jnp.broadcast_to(size, (1, 128))
            x = jnp.where(row16 < 3, x, x * (1.0 / size))
            parts.append(jnp.concatenate(split_rows(x, 0.25), axis=0))
        f = jnp.dot(
            arrange[...], jnp.concatenate(parts, axis=1), preferred_element_type=f32
        ).astype(bf16)
        for g in range(8):
            feats[q + g, :, 0:128] = f[0:128, g * 128 : g * 128 + 128]
            feats[q + g, :, 128:256] = f[128:256, g * 128 : g * 128 + 128]

    win_in.wait()
    top = lax.broadcasted_iota(jnp.int32, (16, 128), 0) < 3

    def items(step, carry):
        work = []
        for u in range(UNROLL):
            k = (step * UNROLL + u) * 2
            inside = k < count
            k = jnp.minimum(k, count - 2)
            row = lax.div(k, 128) * 8
            col = lax.rem(k, 128)
            own = table[row + 1, col]
            rhs = []
            alive = []
            for v in range(2):
                other = table[row, col + v]
                alive.append(jnp.where(inside, table[row + 2, col + v], 0).astype(f32))
                a, b, c, ext = split_rows(block_rows(win_ref, other, origin, 3, 6), 0.0)
                rhs.append(
                    jnp.concatenate(
                        [a, a, a, b, b, c, ext, jnp.zeros((16, 128), bf16)], axis=0
                    )
                )
            work.append((own, alive, jnp.concatenate(rhs, axis=1)))
        outs = [
            lax.dot_general(
                rhs, feats[own], (((0,), (0,)), ((), ())), preferred_element_type=f32
            )
            for own, _, rhs in work
        ]
        sums = []
        for (own, alive, rhs), out in zip(work, outs):
            inv = lax.rsqrt(jnp.maximum(out[:, 0:128], 0.25))
            live = jnp.concatenate([inv[0:128] * alive[0], inv[128:256] * alive[1]], axis=0)
            g = (inv * inv) * live * out[:, 128:256]
            hi = g.astype(bf16)
            lo = (g - hi.astype(f32)).astype(bf16)
            lhs = jnp.concatenate([rhs[0:16], rhs[48:64], rhs[80:112]], axis=0)
            r = jnp.dot(lhs, hi, preferred_element_type=f32)
            r = r + jnp.dot(lhs, lo, preferred_element_type=f32)
            sums.append((own, jnp.where(top, r[0:16] + r[16:32] + r[32:48], r[48:49])))
        for own, r in sums:
            acc[own] += r
        return carry

    lax.fori_loop(0, (count // 2 + UNROLL - 1) // UNROLL, items, 0)

    far_in.wait()
    for g in range(nblocks):
        p = own_ref[9 * g : 9 * g + 16, :] - origin
        t = acc[g]
        near = (p[0:3] * t[3:4] - t[0:3]) * unit[g : g + 1, :]
        force = far_ref[0:3, g * 128 : g * 128 + 128] + near
        for a in range(3):
            out_ref[a, g : g + 1, :] = force[a : a + 1]


def on_device(seg_data, cell_of_block, cell_center, pairs, live_count):
    nblocks, _, width = seg_data.shape
    ncell = cell_center.shape[1]
    slots = pairs.shape[0]
    vmem = pl.BlockSpec(memory_space=pltpu.VMEM)
    hbm = pl.BlockSpec(memory_space=pltpu.HBM)
    dma = pltpu.SemaphoreType.DMA
    far, window = pl.pallas_call(
        exchange_and_far,
        out_shape=(
            jax.ShapeDtypeStruct((3, nblocks * width), f32),
            jax.ShapeDtypeStruct((2, 12, ROWS, width), f32),
        ),
        in_specs=[hbm] * 5,
        out_specs=(hbm, hbm),
        scratch_shapes=[
            pltpu.VMEM((9, nblocks, width), f32),
            pltpu.VMEM((1, nblocks), jnp.int32),
            pltpu.VMEM((3, ncell), f32),
            pltpu.VMEM((2, slots), jnp.int32),
            pltpu.VMEM((1, 1), jnp.int32),
            pltpu.VMEM((nblocks, width), jnp.int32),
            pltpu.VMEM((ROWS, width), f32),
            pltpu.VMEM((16, nblocks * width), f32),
            pltpu.VMEM((18, 128), f32),
            pltpu.VMEM((18, 128), f32),
            pltpu.VMEM((18, 128), f32),
            pltpu.VMEM((3, 18, 128), f32),
            pltpu.VMEM((4, 4, 18, 128), f32),
            pltpu.VMEM((ncell, 32), bf16),
            pltpu.VMEM((32, nblocks * width), bf16),
            pltpu.VMEM((32, nblocks * width), f32),
            pltpu.VMEM((4, 2, ncell // 16, nblocks * width), bf16),
            pltpu.VMEM((3, nblocks * width), f32),
            dma((5,)), dma((2,)), dma((2,)), dma((2, 3)), dma((2, 3)), dma((3,)), dma((3,)),
            dma, dma, dma((3,)), dma((3,)), dma((3,)), dma((3,)), dma((3,)), dma((3,)), dma, dma,
        ],
        compiler_params=pltpu.CompilerParams(
            collective_id=0, has_side_effects=True, vmem_limit_bytes=56 << 20
        ),
    )(
        seg_data.transpose(1, 0, 2), cell_of_block[None, :], cell_center, pairs.T,
        live_count[None, :],
    )
    force = pl.pallas_call(
        near_kernel,
        out_shape=jax.ShapeDtypeStruct((3, nblocks, width), f32),
        in_specs=[hbm] * 3,
        out_specs=vmem,
        scratch_shapes=[
            pltpu.VMEM((24 * ROWS, width), f32),
            pltpu.VMEM((24, 8, width), f32),
            pltpu.VMEM((ROWS, width), f32),
            pltpu.VMEM((3, nblocks * width), f32),
            pltpu.VMEM((nblocks, 128, 256), bf16),
            pltpu.VMEM((256, 64), bf16),
            pltpu.VMEM((nblocks, width), f32),
            pltpu.VMEM((nblocks, 16, width), f32),
            pltpu.VMEM((25 * 32, width), f32),
            pltpu.VMEM((8, width), jnp.int32),
            pltpu.SMEM((26 * 8, width), jnp.int32),
            dma, dma((4,)),
        ],
        compiler_params=pltpu.CompilerParams(vmem_limit_bytes=56 << 20),
    )(window.reshape(24 * ROWS, width), window.reshape(24, ROWS, width), far)
    return force.transpose(1, 0, 2)


def solution(mesh):
    placed = (
        P(("space", "sub"), None, None),
        P(("space", "sub")),
        P(),
        P(("space", "sub"), None),
        P(("space", "sub")),
    )
    return jax.shard_map(
        on_device,
        mesh=mesh,
        in_specs=placed,
        out_specs=P(("space", "sub"), None, None),
        check_vma=False,
    )
```

```python
import functools

import jax
import jax.numpy as jnp
from jax import lax
from jax.experimental import pallas as pl
from jax.experimental.pallas import tpu as pltpu
from jax.sharding import PartitionSpec as P

MESH = pl.DeviceIdType.MESH
f32 = jnp.float32
bf16 = jnp.bfloat16
ROWS = 296
UNROLL = 12


def three(x):
    a = x.astype(bf16).astype(f32)
    r = x - a
    b = r.astype(bf16).astype(f32)
    return a, b, (r - b).astype(bf16).astype(f32)


def exchange_and_far(
    seg_hbm, cell_hbm, cc_hbm, pair_hbm, live_hbm, far_hbm, win,
    seg_ref, cell_row, cc_ref, pair_ref, live_ref, cell_ref,
    payload, flat, mine, twin, pair_sum, parts, moments, cells_f, segs_f, acc, early, far_ref,
    in_sem, x_send, x_recv, z_send, z_recv, r_send, r_recv,
    twin_send, twin_recv, p_send, p_recv, y_send, y_recv, m_send, m_recv, own_sem, far_sem,
):
    space = lax.axis_index("space")
    sub = lax.axis_index("sub")
    y, x = lax.div(space, 4), lax.rem(space, 4)
    z, core = lax.div(sub, 2), lax.rem(sub, 2)
    nblocks = seg_ref.shape[1]
    ncell = cc_ref.shape[1]
    per = ncell // 16
    other_core = (space, z * 2 + 1 - core)

    def along_z(k):
        return (space, lax.rem(z + k, 4) * 2 + core)

    def along_y(k):
        return (lax.rem(y + k, 4) * 4 + x, sub)

    def along_x(k):
        return (y * 4 + lax.rem(x + k, 4), sub)

    def along_space(k):
        return (lax.rem(space + k, 16), sub)

    ins = [
        pltpu.make_async_copy(src, dst, in_sem.at[i])
        for i, (src, dst) in enumerate(
            [
                (cell_hbm, cell_row), (cc_hbm, cc_ref), (seg_hbm, seg_ref),
                (pair_hbm, pair_ref), (live_hbm, live_ref),
            ]
        )
    ]
    for copy in ins:
        copy.start()
    barrier = pltpu.get_barrier_semaphore()
    partners = [other_core, along_space(1), along_space(15)]
    partners += [to(k) for to in (along_z, along_y, along_x) for k in (1, 2, 3)]
    for to in partners:
        pl.semaphore_signal(barrier, inc=1, device_id=to, device_id_type=MESH)

    for copy in ins:
        copy.wait()

    base = space * per
    own_cc = cc_ref[:, pl.ds(pl.multiple_of(base, 256), per)]
    square = lax.broadcasted_iota(jnp.int32, (nblocks, nblocks), 0)
    lane = lax.broadcasted_iota(jnp.int32, (nblocks, nblocks), 1)
    cell = jnp.sum(
        jnp.where(square == lane, cell_row[...].astype(f32), 0.0), axis=1, keepdims=True
    )
    cell_ref[...] = jnp.broadcast_to(cell, (nblocks, 128)).astype(jnp.int32)
    hot = (
        cell.astype(jnp.int32) - base
        == lax.broadcasted_iota(jnp.int32, (nblocks, per), 1)
    ).astype(f32)
    origin = []
    for a in range(3):
        centre = jnp.sum(hot * own_cc[a : a + 1], axis=1, keepdims=True)
        origin.append(centre[0:1])
        payload[pl.ds(a, nblocks, stride=9), :] = seg_ref[a] + centre
    for a in range(3, 9):
        payload[pl.ds(a, nblocks, stride=9), :] = seg_ref[a]
    alive = lax.broadcasted_iota(jnp.int32, (2, 128), 1) < live_ref[...]
    payload[288:290, :] = jnp.where(alive, pair_ref[...].astype(f32), -1.0)
    payload[290:296, :] = jnp.zeros((6, 128), f32)
    for a in range(3):
        for b in range(3):
            outer = jnp.sum(seg_ref[6 + a] * seg_ref[3 + b], axis=1, keepdims=True)
            row = jnp.sum(hot * outer, axis=0, keepdims=True)
            mine[3 * a + b : 3 * a + b + 1, :] = row[:, 0:128]
            mine[9 + 3 * a + b : 10 + 3 * a + b, :] = row[:, 128:256]

    def send(src, dst, send_sem, recv_sem, to):
        return pltpu.make_async_remote_copy(
            src_ref=src, dst_ref=dst, send_sem=send_sem, recv_sem=recv_sem,
            device_id=to, device_id_type=MESH,
        )

    def arrived(ref, sem):
        pltpu.make_async_copy(ref, ref, sem).wait()

    own_copy = pltpu.make_async_copy(payload, win.at[core, 0], own_sem)
    own_copy.start()
    pl.semaphore_wait(barrier, len(partners))

    to_twin = send(mine, twin, twin_send, twin_recv, other_core)
    to_z = [
        send(pair_sum, parts.at[3 - k], p_send.at[k - 1], p_recv.at[3 - k], along_z(k))
        for k in (1, 2, 3)
    ]
    to_y = [
        send(moments.at[0, 0], moments.at[0, 4 - k], y_send.at[k - 1], y_recv.at[3 - k], along_y(k))
        for k in (1, 2, 3)
    ]
    to_x = [
        send(moments.at[0], moments.at[4 - k], m_send.at[k - 1], m_recv.at[3 - k], along_x(k))
        for k in (1, 2, 3)
    ]
    after = send(payload, win.at[core, 4], x_send.at[0], x_recv.at[0], along_space(1))
    before = send(payload, win.at[core, 5], x_send.at[1], x_recv.at[1], along_space(15))
    step = 1 + 2 * core

    def place(group, j):
        return win.at[core, j if group == 0 else 3 + group + 2 * j]

    def spread(group, j):
        return send(
            payload if group == 0 else place(group, 0), place(group, 2 - j),
            z_send.at[group, j], z_recv.at[group, 1 - j], along_z(1 + 2 * j),
        )

    def forward(group):
        return send(
            place(group, 2 - core), place(group, 3),
            z_send.at[group, 2], z_recv.at[group, 2], along_z(step),
        )

    relayed = [(0, 4), (4, 10), (10, 12)]

    def relay(i):
        part = win.at[core, relayed[i][0] : relayed[i][1]]
        return send(part, part, r_send.at[i], r_recv.at[i], other_core)

    to_twin.start()
    after.start()
    before.start()

    for g in range(nblocks):
        lanes = slice(g * 128, g * 128 + 128)
        flat[0:3, lanes] = payload[9 * g : 9 * g + 3, :]
        flat[8:11, lanes] = payload[9 * g + 3 : 9 * g + 6, :]
    row3 = lax.broadcasted_iota(jnp.int32, (3, 1), 0)
    origin = jnp.where(row3 == 0, origin[0], jnp.where(row3 == 1, origin[1], origin[2]))
    ones = jnp.ones((3, ncell), f32)
    blank = jnp.zeros((8, ncell), f32)
    c = cc_ref[...] - origin
    c1, c2, c3 = three(c)
    cq = jnp.concatenate(three(jnp.sum(c * c, axis=0, keepdims=True)), axis=0)
    cells_f[...] = jnp.transpose(
        jnp.concatenate([c1, c1, c2, c2, c1, c3, cq, ones, blank], axis=0)
    ).astype(bf16)
    p = flat[0:3, :] - origin
    p1, p2, p3 = three(-2.0 * p)
    pq = jnp.concatenate(three(1.0 + jnp.sum(p * p, axis=0, keepdims=True)), axis=0)
    segs_f[...] = jnp.concatenate(
        [p1, p2, p1, p2, p3, p1, ones, pq, blank], axis=0
    ).astype(bf16)

    def region_of(dx, dy):
        return lax.rem(y + dy, 4) * 4 + lax.rem(x + dx, 4)

    def weights(region, first):
        at = pl.multiple_of(region * per, 256)
        dist = jnp.dot(cells_f[pl.ds(at, per), :], segs_f[...], preferred_element_type=f32)
        w = pl.reciprocal(dist, approx=True)
        if first:
            cell_id = at + lax.broadcasted_iota(jnp.int32, (per, 128), 0)
            w = jnp.concatenate(
                [
                    jnp.where(
                        cell_id == cell_ref[g : g + 1, :], 0.0, w[:, g * 128 : g * 128 + 128]
                    )
                    for g in range(nblocks)
                ],
                axis=1,
            )
        hi = w.astype(bf16)
        return hi, (w - hi.astype(f32)).astype(bf16)

    def product(dx, dy, hi, lo):
        m = moments[dx, dy]
        m = jnp.concatenate([m[0:9], m[9:18]], axis=1)
        m = jnp.concatenate([m, jnp.zeros((7, per), f32)], axis=0)
        m_hi = m.astype(bf16)
        m = jnp.concatenate([m_hi, (m - m_hi.astype(f32)).astype(bf16)], axis=0)
        return jnp.dot(m, hi, preferred_element_type=f32) + jnp.dot(
            m, lo, preferred_element_type=f32
        )

    def make(k, carry):
        early[k, 0], early[k, 1] = weights(region_of(lax.div(k, 4), lax.rem(k, 4)), False)
        return carry

    def two(j, carry):
        k = 2 * j
        dx, dy = lax.div(k, 4), lax.rem(k, 4)
        hi, lo = weights(region_of(dx, dy), False)
        hi2, lo2 = weights(region_of(dx, dy + 1), False)
        acc[...] += product(dx, dy, hi, lo) + product(dx, dy + 1, hi2, lo2)
        return carry

    early[0, 0], early[0, 1] = weights(space, True)

    arrived(twin, twin_recv)
    pair_sum[...] = mine[...] + twin[...]
    for copy in to_z:
        copy.start()
    for j in (0, 1):
        spread(0, j).start()
    lax.fori_loop(1, 4, make, 0)

    region = pair_sum[...]
    for k in range(3):
        arrived(parts.at[k], p_recv.at[k])
        region = region + parts[k]
    moments[0, 0] = region
    for copy in to_y:
        copy.start()
    for group in (1, 2):
        arrived(place(group, 0), x_recv.at[group - 1])
        for j in (0, 1):
            spread(group, j).start()
    lax.fori_loop(4, 6, make, 0)
    acc[...] = product(0, 0, early[0, 0], early[0, 1])

    for k in range(3):
        arrived(moments.at[0, k + 1], y_recv.at[k])
    for copy in to_x:
        copy.start()
    for j in (0, 1):
        arrived(place(0, j + 1), z_recv.at[0, j])
    forward(0).start()
    acc[...] += (
        product(0, 1, early[1, 0], early[1, 1])
        + product(0, 2, early[2, 0], early[2, 1])
        + product(0, 3, early[3, 0], early[3, 1])
    )

    arrived(moments.at[1], m_recv.at[0])
    acc[...] += product(1, 0, early[4, 0], early[4, 1]) + product(1, 1, early[5, 0], early[5, 1])
    for j in (0, 1):
        arrived(place(1, j + 1), z_recv.at[1, j])
    forward(1).start()
    lax.fori_loop(3, 4, two, 0)
    arrived(moments.at[2], m_recv.at[1])
    lax.fori_loop(4, 5, two, 0)
    for j in (0, 1):
        arrived(place(2, j + 1), z_recv.at[2, j])
    forward(2).start()
    relay(1).start()
    arrived(place(0, 3), z_recv.at[0, 2])
    own_copy.wait()
    relay(0).start()
    lax.fori_loop(5, 6, two, 0)
    arrived(moments.at[3], m_recv.at[2])
    lax.fori_loop(6, 7, two, 0)
    for group in (1, 2):
        arrived(place(group, 3), z_recv.at[group, 2])
    relay(2).start()
    lax.fori_loop(7, 8, two, 0)

    grid = acc[0:9, :] + acc[16:25, :]
    line = flat[8:11, :]
    for a in range(3):
        far_ref[a : a + 1, :] = jnp.sum(
            grid[3 * a : 3 * a + 3, :] * line, axis=0, keepdims=True
        )

    far_copy = pltpu.make_async_copy(far_ref, far_hbm, far_sem)
    far_copy.start()

    for i, (lo, hi) in enumerate(relayed):
        arrived(win.at[1 - core, lo:hi], r_recv.at[i])
    for copy in [to_twin, after, before] + to_z + to_y + to_x:
        copy.wait_send()
    for group in range(3):
        for j in (0, 1):
            spread(group, j).wait_send()
        forward(group).wait_send()
    for i in range(len(relayed)):
        relay(i).wait_send()
    far_copy.wait()


def arrangement():
    q = lax.broadcasted_iota(jnp.int32, (256, 64), 0)
    r = lax.broadcasted_iota(jnp.int32, (256, 64), 1)
    kind, col = q // 128, q % 128
    group, line = col // 16, col % 16
    mate = jnp.where(group < 3, group, jnp.where(group < 5, group - 3, 0))
    same = (group < 6) & (r == mate * 16 + line)
    dist = (kind == 0) & same & (line < 3)
    extra = (kind == 0) & (group == 6) & (
        ((line < 3) & (r == 48 + 3 + line)) | ((line >= 3) & (line < 6) & (r == 48))
    )
    couple = (kind == 1) & same & (line >= 3) & (line < 12)
    return jnp.where(dist, -2.0, jnp.where(extra | couple, 1.0, 0.0)).astype(bf16)


def block_rows(ref, row, origin, first, second):
    row16 = lax.broadcasted_iota(jnp.int32, (16, 128), 0)
    u = [ref[pl.ds(row + first + k, 1), :] for k in range(3)]
    v = [ref[pl.ds(row + second + k, 1), :] for k in range(3)]
    left = jnp.where(row16 < 6, u[0], jnp.where(row16 < 9, u[1], u[2]))
    place = row16 % 3
    right = jnp.where(place == 0, v[0], jnp.where(place == 1, v[1], v[2]))
    both = jnp.where(row16 < 12, left * right, 0.0)
    return jnp.where(row16 < 3, ref[pl.ds(row, 16), :] - origin, both)


def split_rows(x, plus):
    row16 = lax.broadcasted_iota(jnp.int32, (16, 128), 0)
    a, b, c = three(x)
    sq = jnp.sum(jnp.where(row16 < 3, x * x, 0.0), axis=0, keepdims=True) + plus
    s1, s2, s3 = three(sq)
    ext = jnp.where(
        row16 < 3, 1.0,
        jnp.where(row16 == 3, s1, jnp.where(row16 == 4, s2, jnp.where(row16 == 5, s3, 0.0))),
    )
    return a.astype(bf16), b.astype(bf16), c.astype(bf16), ext.astype(bf16)


def build_list(pair_ref, space, sub, nblocks, hots, listed, table, sem):
    first_block = ((space * 8 + sub) * nblocks).astype(f32)
    target = jnp.concatenate(
        [pair_ref[d, 0:1, :] for d in range(24)] + [pair_ref[sub % 2 * 12, 0:1, :]],
        axis=0,
    )
    source = jnp.concatenate(
        [pair_ref[d, 1:2, :] for d in range(24)] + [pair_ref[sub % 2 * 12, 1:2, :]],
        axis=0,
    )
    is_own = lax.broadcasted_iota(jnp.int32, (25, 128), 0) == 24
    mine = jnp.where(is_own, target, source) - first_block
    theirs = jnp.where(is_own, source, target)
    used = (source >= 0) & (mine >= 0) & (mine < nblocks)
    mine = jnp.where(used, mine, -1.0)
    owner = jnp.floor(theirs * (1.0 / 32))
    their_space = jnp.floor(owner * (1.0 / 8))
    their_sub = owner - 8.0 * their_space
    their_z = jnp.floor(their_sub * 0.5)
    ahead = their_space - space.astype(f32)
    ahead = jnp.where(ahead < -8, ahead + 16.0, jnp.where(ahead > 8, ahead - 16.0, ahead))
    dz = their_z - (sub // 2).astype(f32)
    dz = jnp.where(dz < 0, dz + 4.0, dz)
    dz = jnp.where(dz == 3, 2.0, jnp.where(dz == 2, 3.0, dz))
    dev = (their_sub - 2.0 * their_z) * 12.0 + jnp.where(
        ahead == 0, dz, 4.0 + 2.0 * dz + (ahead > 0).astype(f32)
    )
    local = theirs - 32.0 * owner
    before = (
        lax.broadcasted_iota(jnp.int32, (128, 128), 0)
        < lax.broadcasted_iota(jnp.int32, (128, 128), 1)
    ).astype(bf16)
    block_id = lax.broadcasted_iota(jnp.int32, (32, 128), 0).astype(f32)
    run = jnp.zeros((32, 1), f32)
    hots[...] = jnp.concatenate(
        [(mine[r : r + 1] == block_id).astype(f32) for r in range(25)], axis=0
    )
    within = jnp.dot(hots[...].astype(bf16), before, preferred_element_type=f32)
    sums = jnp.sum(hots[...], axis=1, keepdims=True)
    runs = []
    for r in range(25):
        runs.append(run)
        run = run + sums[32 * r : 32 * r + 32]
    even = 2.0 * jnp.floor((run + 1.0) * 0.5)
    above = (
        lax.broadcasted_iota(jnp.int32, (32, 32), 1)
        < lax.broadcasted_iota(jnp.int32, (32, 32), 0)
    ).astype(f32)
    starts = jnp.dot(
        above, jnp.broadcast_to(even, (32, 128)), precision=lax.Precision.HIGHEST,
        preferred_element_type=f32,
    )[:, 0:1]
    count = jnp.sum(even).astype(jnp.int32)
    ranks = []
    for r in range(25):
        h = hots[32 * r : 32 * r + 32, :]
        at = within[32 * r : 32 * r + 32] + (runs[r] + starts)
        ranks.append(jnp.sum(h * at, axis=0, keepdims=True))
    rank = jnp.where(used, jnp.concatenate(ranks, axis=0), -1.0)
    pad = jnp.full((128 - 25, 128), -1.0, f32)
    rank_t = jnp.transpose(jnp.concatenate([rank, pad], axis=0))
    lane = lax.broadcasted_iota(jnp.int32, (128, 128), 1).astype(f32)
    row8 = lax.broadcasted_iota(jnp.int32, (8, 128), 0)
    ends = starts + even

    def fill(kr, carry):
        got = jnp.zeros((8, 128), f32)
        first = (kr * 128).astype(f32)
        want = lane + first
        for r in range(25):
            hot = (rank_t[:, r : r + 1] == want).astype(bf16)
            vals = jnp.where(row8 == 0, dev[r : r + 1], jnp.where(row8 == 1, local[r : r + 1], 1.0))
            vals = jnp.where((row8 < 3) & used[r : r + 1], vals, 0.0)
            got = got + jnp.dot(vals.astype(bf16), hot, preferred_element_type=f32)
        other = got[0:1] * float(ROWS) + got[1:2] * 9.0
        own = jnp.sum((ends <= want[0:32]).astype(f32), axis=0, keepdims=True)
        own = jnp.minimum(own, 31.0)
        rows = jnp.where(
            row8 == 0, other, jnp.where(row8 == 1, own, jnp.where(row8 == 2, got[2:3], 0.0))
        )
        listed[...] = rows.astype(jnp.int32)
        copy = pltpu.make_async_copy(listed, table.at[pl.ds(kr * 8, 8)], sem)
        copy.start()
        copy.wait()
        return carry

    lax.fori_loop(0, (count + 127) // 128, fill, 0)
    return count


def near_kernel(
    win_hbm, pair_hbm, far_hbm, out_ref,
    win_ref, pair_ref, own_ref, far_ref, feats, arrange, unit, acc, hots, listed, table, sem, in_sem,
):
    space, sub = lax.axis_index("space"), lax.axis_index("sub")
    nblocks = out_ref.shape[1]
    my_row = pl.multiple_of(sub % 2 * 12 * ROWS, 8)
    pairs_in = pltpu.make_async_copy(pair_hbm.at[:, 288:296], pair_ref, in_sem.at[0])
    own_in = pltpu.make_async_copy(win_hbm.at[pl.ds(my_row, ROWS)], own_ref, in_sem.at[1])
    win_in = pltpu.make_async_copy(win_hbm, win_ref, in_sem.at[2])
    far_in = pltpu.make_async_copy(far_hbm, far_ref, in_sem.at[3])
    for copy in (pairs_in, own_in, win_in, far_in):
        copy.start()
    pairs_in.wait()
    count = build_list(pair_ref, space, sub, nblocks, hots, listed, table, sem)
    own_in.wait()
    origin = jnp.where(
        lax.broadcasted_iota(jnp.int32, (16, 1), 0) < 3, own_ref[0:16, 0:1], 0.0
    )

    arrange[...] = arrangement()
    acc[...] = jnp.zeros_like(acc)
    row16 = lax.broadcasted_iota(jnp.int32, (16, 128), 0)
    for q in range(0, nblocks, 8):
        parts = []
        for g in range(q, q + 8):
            x = block_rows(own_ref, 9 * g, origin, 6, 3)
            size = jnp.max(jnp.where(row16 < 3, 0.0, jnp.abs(x)), axis=0, keepdims=True)
            size = jnp.maximum(jnp.max(size, axis=1, keepdims=True), 1e-30)
            unit[g : g + 1, :] = jnp.broadcast_to(size, (1, 128))
            x = jnp.where(row16 < 3, x, x * (1.0 / size))
            parts.append(jnp.concatenate(split_rows(x, 0.25), axis=0))
        f = jnp.dot(
            arrange[...], jnp.concatenate(parts, axis=1), preferred_element_type=f32
        ).astype(bf16)
        for g in range(8):
            feats[q + g, :, 0:128] = f[0:128, g * 128 : g * 128 + 128]
            feats[q + g, :, 128:256] = f[128:256, g * 128 : g * 128 + 128]

    win_in.wait()
    top = lax.broadcasted_iota(jnp.int32, (16, 128), 0) < 3

    def items(step, carry):
        work = []
        for u in range(UNROLL):
            k = (step * UNROLL + u) * 2
            inside = k < count
            k = jnp.minimum(k, count - 2)
            row = lax.div(k, 128) * 8
            col = lax.rem(k, 128)
            own = table[row + 1, col]
            rhs = []
            alive = []
            for v in range(2):
                other = table[row, col + v]
                alive.append(jnp.where(inside, table[row + 2, col + v], 0).astype(f32))
                a, b, c, ext = split_rows(block_rows(win_ref, other, origin, 3, 6), 0.0)
                rhs.append(
                    jnp.concatenate(
                        [a, a, a, b, b, c, ext, jnp.zeros((16, 128), bf16)], axis=0
                    )
                )
            work.append((own, alive, jnp.concatenate(rhs, axis=1)))
        outs = [
            lax.dot_general(
                rhs, feats[own], (((0,), (0,)), ((), ())), preferred_element_type=f32
            )
            for own, _, rhs in work
        ]
        sums = []
        for (own, alive, rhs), out in zip(work, outs):
            inv = lax.rsqrt(jnp.maximum(out[:, 0:128], 0.25))
            live = jnp.concatenate([inv[0:128] * alive[0], inv[128:256] * alive[1]], axis=0)
            g = (inv * inv) * live * out[:, 128:256]
            hi = g.astype(bf16)
            lo = (g - hi.astype(f32)).astype(bf16)
            lhs = jnp.concatenate([rhs[0:16], rhs[48:64], rhs[80:112]], axis=0)
            r = jnp.dot(lhs, hi, preferred_element_type=f32)
            r = r + jnp.dot(lhs, lo, preferred_element_type=f32)
            sums.append((own, jnp.where(top, r[0:16] + r[16:32] + r[32:48], r[48:49])))
        for own, r in sums:
            acc[own] += r
        return carry

    lax.fori_loop(0, (count // 2 + UNROLL - 1) // UNROLL, items, 0)

    far_in.wait()
    for g in range(nblocks):
        p = own_ref[9 * g : 9 * g + 16, :] - origin
        t = acc[g]
        near = (p[0:3] * t[3:4] - t[0:3]) * unit[g : g + 1, :]
        force = far_ref[0:3, g * 128 : g * 128 + 128] + near
        for a in range(3):
            out_ref[a, g : g + 1, :] = force[a : a + 1]


def on_device(seg_data, cell_of_block, cell_center, pairs, live_count):
    nblocks, _, width = seg_data.shape
    ncell = cell_center.shape[1]
    slots = pairs.shape[0]
    vmem = pl.BlockSpec(memory_space=pltpu.VMEM)
    hbm = pl.BlockSpec(memory_space=pltpu.HBM)
    dma = pltpu.SemaphoreType.DMA
    far, window = pl.pallas_call(
        exchange_and_far,
        out_shape=(
            jax.ShapeDtypeStruct((3, nblocks * width), f32),
            jax.ShapeDtypeStruct((2, 12, ROWS, width), f32),
        ),
        in_specs=[hbm] * 5,
        out_specs=(hbm, hbm),
        scratch_shapes=[
            pltpu.VMEM((9, nblocks, width), f32),
            pltpu.VMEM((1, nblocks), jnp.int32),
            pltpu.VMEM((3, ncell), f32),
            pltpu.VMEM((2, slots), jnp.int32),
            pltpu.VMEM((1, 1), jnp.int32),
            pltpu.VMEM((nblocks, width), jnp.int32),
            pltpu.VMEM((ROWS, width), f32),
            pltpu.VMEM((16, nblocks * width), f32),
            pltpu.VMEM((18, 128), f32),
            pltpu.VMEM((18, 128), f32),
            pltpu.VMEM((18, 128), f32),
            pltpu.VMEM((3, 18, 128), f32),
            pltpu.VMEM((4, 4, 18, 128), f32),
            pltpu.VMEM((ncell, 32), bf16),
            pltpu.VMEM((32, nblocks * width), bf16),
            pltpu.VMEM((32, nblocks * width), f32),
            pltpu.VMEM((6, 2, ncell // 16, nblocks * width), bf16),
            pltpu.VMEM((3, nblocks * width), f32),
            dma((5,)), dma((2,)), dma((2,)), dma((3, 3)), dma((3, 3)), dma((3,)), dma((3,)),
            dma, dma, dma((3,)), dma((3,)), dma((3,)), dma((3,)), dma((3,)), dma((3,)), dma, dma,
        ],
        compiler_params=pltpu.CompilerParams(
            collective_id=0, has_side_effects=True, vmem_limit_bytes=56 << 20
        ),
    )(
        seg_data.transpose(1, 0, 2), cell_of_block[None, :], cell_center, pairs.T,
        live_count[None, :],
    )
    force = pl.pallas_call(
        near_kernel,
        out_shape=jax.ShapeDtypeStruct((3, nblocks, width), f32),
        in_specs=[hbm] * 3,
        out_specs=vmem,
        scratch_shapes=[
            pltpu.VMEM((24 * ROWS, width), f32),
            pltpu.VMEM((24, 8, width), f32),
            pltpu.VMEM((ROWS, width), f32),
            pltpu.VMEM((3, nblocks * width), f32),
            pltpu.VMEM((nblocks, 128, 256), bf16),
            pltpu.VMEM((256, 64), bf16),
            pltpu.VMEM((nblocks, width), f32),
            pltpu.VMEM((nblocks, 16, width), f32),
            pltpu.VMEM((25 * 32, width), f32),
            pltpu.VMEM((8, width), jnp.int32),
            pltpu.SMEM((26 * 8, width), jnp.int32),
            dma, dma((4,)),
        ],
        compiler_params=pltpu.CompilerParams(vmem_limit_bytes=56 << 20),
    )(window.reshape(24 * ROWS, width), window.reshape(24, ROWS, width), far)
    return force.transpose(1, 0, 2)


def solution(mesh):
    placed = (
        P(("space", "sub"), None, None),
        P(("space", "sub")),
        P(),
        P(("space", "sub"), None),
        P(("space", "sub")),
    )
    return jax.shard_map(
        on_device,
        mesh=mesh,
        in_specs=placed,
        out_specs=P(("space", "sub"), None, None),
        check_vma=False,
    )
```

```python
import functools

import jax
import jax.numpy as jnp
from jax import lax
from jax.experimental import pallas as pl
from jax.experimental.pallas import tpu as pltpu
from jax.sharding import PartitionSpec as P

MESH = pl.DeviceIdType.MESH
f32 = jnp.float32
bf16 = jnp.bfloat16
ROWS = 296
UNROLL = 12


def three(x):
    a = x.astype(bf16).astype(f32)
    r = x - a
    b = r.astype(bf16).astype(f32)
    return a, b, (r - b).astype(bf16).astype(f32)


def exchange_and_far(
    seg_hbm, cell_hbm, cc_hbm, pair_hbm, live_hbm, far_hbm, win,
    seg_ref, cell_row, cc_ref, pair_ref, live_ref, cell_ref,
    payload, flat, mine, twin, pair_sum, parts, moments, cells_f, segs_f, acc, early, far_ref,
    in_sem, x_send, x_recv, z_send, z_recv, r_send, r_recv,
    twin_send, twin_recv, p_send, p_recv, y_send, y_recv, m_send, m_recv, own_sem, far_sem,
):
    space = lax.axis_index("space")
    sub = lax.axis_index("sub")
    y, x = lax.div(space, 4), lax.rem(space, 4)
    z, core = lax.div(sub, 2), lax.rem(sub, 2)
    nblocks = seg_ref.shape[1]
    ncell = cc_ref.shape[1]
    per = ncell // 16
    other_core = (space, z * 2 + 1 - core)

    def along_z(k):
        return (space, lax.rem(z + k, 4) * 2 + core)

    def along_y(k):
        return (lax.rem(y + k, 4) * 4 + x, sub)

    def along_x(k):
        return (y * 4 + lax.rem(x + k, 4), sub)

    def along_space(k):
        return (lax.rem(space + k, 16), sub)

    ins = [
        pltpu.make_async_copy(src, dst, in_sem.at[i])
        for i, (src, dst) in enumerate(
            [
                (cell_hbm, cell_row), (cc_hbm, cc_ref), (seg_hbm, seg_ref),
                (pair_hbm, pair_ref), (live_hbm, live_ref),
            ]
        )
    ]
    for copy in ins:
        copy.start()
    barrier = pltpu.get_barrier_semaphore()
    partners = [other_core, along_space(1), along_space(15)]
    partners += [to(k) for to in (along_z, along_y, along_x) for k in (1, 2, 3)]
    for to in partners:
        pl.semaphore_signal(barrier, inc=1, device_id=to, device_id_type=MESH)

    for copy in ins:
        copy.wait()

    base = space * per
    own_cc = cc_ref[:, pl.ds(pl.multiple_of(base, 256), per)]
    square = lax.broadcasted_iota(jnp.int32, (nblocks, nblocks), 0)
    lane = lax.broadcasted_iota(jnp.int32, (nblocks, nblocks), 1)
    cell = jnp.sum(
        jnp.where(square == lane, cell_row[...].astype(f32), 0.0), axis=1, keepdims=True
    )
    cell_ref[...] = jnp.broadcast_to(cell, (nblocks, 128)).astype(jnp.int32)
    hot = (
        cell.astype(jnp.int32) - base
        == lax.broadcasted_iota(jnp.int32, (nblocks, per), 1)
    ).astype(f32)
    origin = []
    for a in range(3):
        centre = jnp.sum(hot * own_cc[a : a + 1], axis=1, keepdims=True)
        origin.append(centre[0:1])
        payload[pl.ds(a, nblocks, stride=9), :] = seg_ref[a] + centre
    for a in range(3, 9):
        payload[pl.ds(a, nblocks, stride=9), :] = seg_ref[a]
    alive = lax.broadcasted_iota(jnp.int32, (2, 128), 1) < live_ref[...]
    payload[288:290, :] = jnp.where(alive, pair_ref[...].astype(f32), -1.0)
    payload[290:296, :] = jnp.zeros((6, 128), f32)
    for a in range(3):
        for b in range(3):
            outer = jnp.sum(seg_ref[6 + a] * seg_ref[3 + b], axis=1, keepdims=True)
            row = jnp.sum(hot * outer, axis=0, keepdims=True)
            mine[3 * a + b : 3 * a + b + 1, :] = row[:, 0:128]
            mine[9 + 3 * a + b : 10 + 3 * a + b, :] = row[:, 128:256]

    def send(src, dst, send_sem, recv_sem, to):
        return pltpu.make_async_remote_copy(
            src_ref=src, dst_ref=dst, send_sem=send_sem, recv_sem=recv_sem,
            device_id=to, device_id_type=MESH,
        )

    def arrived(ref, sem):
        pltpu.make_async_copy(ref, ref, sem).wait()

    own_copy = pltpu.make_async_copy(payload, win.at[core, 0], own_sem)
    own_copy.start()
    pl.semaphore_wait(barrier, len(partners))

    to_twin = send(mine, twin, twin_send, twin_recv, other_core)
    to_z = [
        send(pair_sum, parts.at[3 - k], p_send.at[k - 1], p_recv.at[3 - k], along_z(k))
        for k in (1, 2, 3)
    ]
    to_y = [
        send(moments.at[0, 0], moments.at[0, 4 - k], y_send.at[k - 1], y_recv.at[3 - k], along_y(k))
        for k in (1, 2, 3)
    ]
    to_x = [
        send(moments.at[0], moments.at[4 - k], m_send.at[k - 1], m_recv.at[3 - k], along_x(k))
        for k in (1, 2, 3)
    ]
    after = send(payload, win.at[core, 4], x_send.at[0], x_recv.at[0], along_space(1))
    before = send(payload, win.at[core, 5], x_send.at[1], x_recv.at[1], along_space(15))
    step = 1 + 2 * core

    def place(group, j):
        return win.at[core, j if group == 0 else 3 + group + 2 * j]

    def spread(group, j):
        return send(
            payload if group == 0 else place(group, 0), place(group, 2 - j),
            z_send.at[group, j], z_recv.at[group, 1 - j], along_z(1 + 2 * j),
        )

    def forward(group):
        return send(
            place(group, 2 - core), place(group, 3),
            z_send.at[group, 2], z_recv.at[group, 2], along_z(step),
        )

    relayed = [(0, 4), (4, 10), (10, 12)]

    def relay(i):
        part = win.at[core, relayed[i][0] : relayed[i][1]]
        return send(part, part, r_send.at[i], r_recv.at[i], other_core)

    to_twin.start()
    after.start()
    before.start()

    for g in range(nblocks):
        lanes = slice(g * 128, g * 128 + 128)
        flat[0:3, lanes] = payload[9 * g : 9 * g + 3, :]
        flat[8:11, lanes] = payload[9 * g + 3 : 9 * g + 6, :]
    row3 = lax.broadcasted_iota(jnp.int32, (3, 1), 0)
    origin = jnp.where(row3 == 0, origin[0], jnp.where(row3 == 1, origin[1], origin[2]))
    ones = jnp.ones((3, ncell), f32)
    blank = jnp.zeros((8, ncell), f32)
    c = cc_ref[...] - origin
    c1, c2, c3 = three(c)
    cq = jnp.concatenate(three(jnp.sum(c * c, axis=0, keepdims=True)), axis=0)
    cells_f[...] = jnp.transpose(
        jnp.concatenate([c1, c1, c2, c2, c1, c3, cq, ones, blank], axis=0)
    ).astype(bf16)
    p = flat[0:3, :] - origin
    p1, p2, p3 = three(-2.0 * p)
    pq = jnp.concatenate(three(1.0 + jnp.sum(p * p, axis=0, keepdims=True)), axis=0)
    segs_f[...] = jnp.concatenate(
        [p1, p2, p1, p2, p3, p1, ones, pq, blank], axis=0
    ).astype(bf16)

    def region_of(dx, dy):
        return lax.rem(y + dy, 4) * 4 + lax.rem(x + dx, 4)

    def weights(region, first):
        at = pl.multiple_of(region * per, 256)
        dist = jnp.dot(cells_f[pl.ds(at, per), :], segs_f[...], preferred_element_type=f32)
        w = pl.reciprocal(dist, approx=True)
        if first:
            cell_id = at + lax.broadcasted_iota(jnp.int32, (per, 128), 0)
            w = jnp.concatenate(
                [
                    jnp.where(
                        cell_id == cell_ref[g : g + 1, :], 0.0, w[:, g * 128 : g * 128 + 128]
                    )
                    for g in range(nblocks)
                ],
                axis=1,
            )
        hi = w.astype(bf16)
        return hi, (w - hi.astype(f32)).astype(bf16)

    def product(dx, dy, hi, lo):
        m = moments[dx, dy]
        m = jnp.concatenate([m[0:9], m[9:18]], axis=1)
        m = jnp.concatenate([m, jnp.zeros((7, per), f32)], axis=0)
        m_hi = m.astype(bf16)
        m = jnp.concatenate([m_hi, (m - m_hi.astype(f32)).astype(bf16)], axis=0)
        return jnp.dot(m, hi, preferred_element_type=f32) + jnp.dot(
            m, lo, preferred_element_type=f32
        )

    def make(k, carry):
        early[k, 0], early[k, 1] = weights(region_of(lax.div(k, 4), lax.rem(k, 4)), False)
        return carry

    def two(j, carry):
        k = 2 * j
        dx, dy = lax.div(k, 4), lax.rem(k, 4)
        hi, lo = weights(region_of(dx, dy), False)
        hi2, lo2 = weights(region_of(dx, dy + 1), False)
        acc[...] += product(dx, dy, hi, lo) + product(dx, dy + 1, hi2, lo2)
        return carry

    early[0, 0], early[0, 1] = weights(space, True)

    arrived(twin, twin_recv)
    pair_sum[...] = mine[...] + twin[...]
    for copy in to_z:
        copy.start()
    for j in (0, 1):
        spread(0, j).start()
    lax.fori_loop(1, 4, make, 0)

    region = pair_sum[...]
    for k in range(3):
        arrived(parts.at[k], p_recv.at[k])
        region = region + parts[k]
    moments[0, 0] = region
    for copy in to_y:
        copy.start()
    for group in (1, 2):
        arrived(place(group, 0), x_recv.at[group - 1])
        for j in (0, 1):
            spread(group, j).start()
    lax.fori_loop(4, 6, make, 0)
    acc[...] = product(0, 0, early[0, 0], early[0, 1])

    for k in range(3):
        arrived(moments.at[0, k + 1], y_recv.at[k])
    for copy in to_x:
        copy.start()
    for j in (0, 1):
        arrived(place(0, j + 1), z_recv.at[0, j])
    forward(0).start()
    acc[...] += (
        product(0, 1, early[1, 0], early[1, 1])
        + product(0, 2, early[2, 0], early[2, 1])
        + product(0, 3, early[3, 0], early[3, 1])
    )

    arrived(moments.at[1], m_recv.at[0])
    acc[...] += product(1, 0, early[4, 0], early[4, 1]) + product(1, 1, early[5, 0], early[5, 1])
    for j in (0, 1):
        arrived(place(1, j + 1), z_recv.at[1, j])
    forward(1).start()
    lax.fori_loop(3, 4, two, 0)
    arrived(moments.at[2], m_recv.at[1])
    lax.fori_loop(4, 5, two, 0)
    for j in (0, 1):
        arrived(place(2, j + 1), z_recv.at[2, j])
    forward(2).start()
    relay(1).start()
    arrived(place(0, 3), z_recv.at[0, 2])
    own_copy.wait()
    relay(0).start()
    lax.fori_loop(5, 6, two, 0)
    arrived(moments.at[3], m_recv.at[2])
    lax.fori_loop(6, 7, two, 0)
    for group in (1, 2):
        arrived(place(group, 3), z_recv.at[group, 2])
    relay(2).start()
    lax.fori_loop(7, 8, two, 0)

    grid = acc[0:9, :] + acc[16:25, :]
    line = flat[8:11, :]
    for a in range(3):
        far_ref[a : a + 1, :] = jnp.sum(
            grid[3 * a : 3 * a + 3, :] * line, axis=0, keepdims=True
        )

    far_copy = pltpu.make_async_copy(far_ref, far_hbm, far_sem)
    far_copy.start()

    for i, (lo, hi) in enumerate(relayed):
        arrived(win.at[1 - core, lo:hi], r_recv.at[i])
    for copy in [to_twin, after, before] + to_z + to_y + to_x:
        copy.wait_send()
    for group in range(3):
        for j in (0, 1):
            spread(group, j).wait_send()
        forward(group).wait_send()
    for i in range(len(relayed)):
        relay(i).wait_send()
    far_copy.wait()


def arrangement():
    q = lax.broadcasted_iota(jnp.int32, (256, 64), 0)
    r = lax.broadcasted_iota(jnp.int32, (256, 64), 1)
    kind, col = q // 128, q % 128
    group, line = col // 16, col % 16
    mate = jnp.where(group < 3, group, jnp.where(group < 5, group - 3, 0))
    same = (group < 6) & (r == mate * 16 + line)
    dist = (kind == 0) & same & (line < 3)
    extra = (kind == 0) & (group == 6) & (
        ((line < 3) & (r == 48 + 3 + line)) | ((line >= 3) & (line < 6) & (r == 48))
    )
    couple = (kind == 1) & same & (line >= 3) & (line < 12)
    return jnp.where(dist, -2.0, jnp.where(extra | couple, 1.0, 0.0)).astype(bf16)


def block_rows(ref, row, origin, first, second):
    row16 = lax.broadcasted_iota(jnp.int32, (16, 128), 0)
    u = [ref[pl.ds(row + first + k, 1), :] for k in range(3)]
    v = [ref[pl.ds(row + second + k, 1), :] for k in range(3)]
    left = jnp.where(row16 < 6, u[0], jnp.where(row16 < 9, u[1], u[2]))
    place = row16 % 3
    right = jnp.where(place == 0, v[0], jnp.where(place == 1, v[1], v[2]))
    both = jnp.where(row16 < 12, left * right, 0.0)
    return jnp.where(row16 < 3, ref[pl.ds(row, 16), :] - origin, both)


def split_rows(x, plus):
    row16 = lax.broadcasted_iota(jnp.int32, (16, 128), 0)
    a, b, c = three(x)
    sq = jnp.sum(jnp.where(row16 < 3, x * x, 0.0), axis=0, keepdims=True) + plus
    s1, s2, s3 = three(sq)
    ext = jnp.where(
        row16 < 3, 1.0,
        jnp.where(row16 == 3, s1, jnp.where(row16 == 4, s2, jnp.where(row16 == 5, s3, 0.0))),
    )
    return a.astype(bf16), b.astype(bf16), c.astype(bf16), ext.astype(bf16)


def build_list(pair_ref, space, sub, nblocks, hots, listed, table, sem):
    first_block = ((space * 8 + sub) * nblocks).astype(f32)
    target = jnp.concatenate(
        [pair_ref[d, 0:1, :] for d in range(24)] + [pair_ref[sub % 2 * 12, 0:1, :]],
        axis=0,
    )
    source = jnp.concatenate(
        [pair_ref[d, 1:2, :] for d in range(24)] + [pair_ref[sub % 2 * 12, 1:2, :]],
        axis=0,
    )
    is_own = lax.broadcasted_iota(jnp.int32, (25, 128), 0) == 24
    mine = jnp.where(is_own, target, source) - first_block
    theirs = jnp.where(is_own, source, target)
    used = (source >= 0) & (mine >= 0) & (mine < nblocks)
    mine = jnp.where(used, mine, -1.0)
    owner = jnp.floor(theirs * (1.0 / 32))
    their_space = jnp.floor(owner * (1.0 / 8))
    their_sub = owner - 8.0 * their_space
    their_z = jnp.floor(their_sub * 0.5)
    ahead = their_space - space.astype(f32)
    ahead = jnp.where(ahead < -8, ahead + 16.0, jnp.where(ahead > 8, ahead - 16.0, ahead))
    dz = their_z - (sub // 2).astype(f32)
    dz = jnp.where(dz < 0, dz + 4.0, dz)
    dz = jnp.where(dz == 3, 2.0, jnp.where(dz == 2, 3.0, dz))
    dev = (their_sub - 2.0 * their_z) * 12.0 + jnp.where(
        ahead == 0, dz, 4.0 + 2.0 * dz + (ahead > 0).astype(f32)
    )
    local = theirs - 32.0 * owner
    before = (
        lax.broadcasted_iota(jnp.int32, (128, 128), 0)
        < lax.broadcasted_iota(jnp.int32, (128, 128), 1)
    ).astype(bf16)
    block_id = lax.broadcasted_iota(jnp.int32, (32, 128), 0).astype(f32)
    run = jnp.zeros((32, 1), f32)
    hots[...] = jnp.concatenate(
        [(mine[r : r + 1] == block_id).astype(f32) for r in range(25)], axis=0
    )
    within = jnp.dot(hots[...].astype(bf16), before, preferred_element_type=f32)
    sums = jnp.sum(hots[...], axis=1, keepdims=True)
    runs = []
    for r in range(25):
        runs.append(run)
        run = run + sums[32 * r : 32 * r + 32]
    even = 2.0 * jnp.floor((run + 1.0) * 0.5)
    above = (
        lax.broadcasted_iota(jnp.int32, (32, 32), 1)
        < lax.broadcasted_iota(jnp.int32, (32, 32), 0)
    ).astype(f32)
    starts = jnp.dot(
        above, jnp.broadcast_to(even, (32, 128)), precision=lax.Precision.HIGHEST,
        preferred_element_type=f32,
    )[:, 0:1]
    count = jnp.sum(even).astype(jnp.int32)
    ranks = []
    for r in range(25):
        h = hots[32 * r : 32 * r + 32, :]
        at = within[32 * r : 32 * r + 32] + (runs[r] + starts)
        ranks.append(jnp.sum(h * at, axis=0, keepdims=True))
    rank = jnp.where(used, jnp.concatenate(ranks, axis=0), -1.0)
    pad = jnp.full((128 - 25, 128), -1.0, f32)
    rank_t = jnp.transpose(jnp.concatenate([rank, pad], axis=0))
    lane = lax.broadcasted_iota(jnp.int32, (128, 128), 1).astype(f32)
    row8 = lax.broadcasted_iota(jnp.int32, (8, 128), 0)
    ends = starts + even

    def rows_of(kr):
        got = jnp.zeros((8, 128), f32)
        want = lane + (kr * 128).astype(f32)
        for r in range(25):
            hot = (rank_t[:, r : r + 1] == want).astype(bf16)
            vals = jnp.where(row8 == 0, dev[r : r + 1], jnp.where(row8 == 1, local[r : r + 1], 1.0))
            vals = jnp.where((row8 < 3) & used[r : r + 1], vals, 0.0)
            got = got + jnp.dot(vals.astype(bf16), hot, preferred_element_type=f32)
        other = got[0:1] * float(ROWS) + got[1:2] * 9.0
        own = jnp.sum((ends <= want[0:32]).astype(f32), axis=0, keepdims=True)
        own = jnp.minimum(own, 31.0)
        rows = jnp.where(
            row8 == 0, other, jnp.where(row8 == 1, own, jnp.where(row8 == 2, got[2:3], 0.0))
        )
        return rows.astype(jnp.int32)

    for kr in range(2):
        listed[8 * kr : 8 * kr + 8, :] = rows_of(jnp.int32(kr))
    first = pltpu.make_async_copy(listed.at[0:16], table.at[0:16], sem.at[0])
    first.start()

    def fill(kr, carry):
        listed[16:24, :] = rows_of(kr)
        copy = pltpu.make_async_copy(listed.at[16:24], table.at[pl.ds(kr * 8, 8)], sem.at[1])
        copy.start()
        copy.wait()
        return carry

    lax.fori_loop(2, lax.div(count + 127, 128), fill, 0)
    return count, first


def near_kernel(
    win_hbm, pair_hbm, far_hbm, out_ref,
    win_ref, pair_ref, own_ref, far_ref, feats, arrange, unit, acc, hots, listed, table, sem, in_sem,
):
    space, sub = lax.axis_index("space"), lax.axis_index("sub")
    nblocks = out_ref.shape[1]
    my_row = pl.multiple_of(sub % 2 * 12 * ROWS, 8)
    pairs_in = pltpu.make_async_copy(pair_hbm.at[:, 288:296], pair_ref, in_sem.at[0])
    own_in = pltpu.make_async_copy(win_hbm.at[pl.ds(my_row, ROWS)], own_ref, in_sem.at[1])
    win_in = pltpu.make_async_copy(win_hbm, win_ref, in_sem.at[2])
    far_in = pltpu.make_async_copy(far_hbm, far_ref, in_sem.at[3])
    for copy in (pairs_in, own_in, win_in, far_in):
        copy.start()
    pairs_in.wait()
    count, listing = build_list(pair_ref, space, sub, nblocks, hots, listed, table, sem)
    own_in.wait()
    origin = jnp.where(
        lax.broadcasted_iota(jnp.int32, (16, 1), 0) < 3, own_ref[0:16, 0:1], 0.0
    )

    arrange[...] = arrangement()
    acc[...] = jnp.zeros_like(acc)
    row16 = lax.broadcasted_iota(jnp.int32, (16, 128), 0)
    for q in range(0, nblocks, 8):
        parts = []
        for g in range(q, q + 8):
            x = block_rows(own_ref, 9 * g, origin, 6, 3)
            size = jnp.max(jnp.where(row16 < 3, 0.0, jnp.abs(x)), axis=0, keepdims=True)
            size = jnp.maximum(jnp.max(size, axis=1, keepdims=True), 1e-30)
            unit[g : g + 1, :] = jnp.broadcast_to(size, (1, 128))
            x = jnp.where(row16 < 3, x, x * (1.0 / size))
            parts.append(jnp.concatenate(split_rows(x, 0.25), axis=0))
        f = jnp.dot(
            arrange[...], jnp.concatenate(parts, axis=1), preferred_element_type=f32
        ).astype(bf16)
        for g in range(8):
            feats[q + g, :, 0:128] = f[0:128, g * 128 : g * 128 + 128]
            feats[q + g, :, 128:256] = f[128:256, g * 128 : g * 128 + 128]

    listing.wait()
    win_in.wait()
    top = lax.broadcasted_iota(jnp.int32, (16, 128), 0) < 3

    def items(step, carry):
        work = []
        for u in range(UNROLL):
            k = (step * UNROLL + u) * 2
            inside = k < count
            k = jnp.minimum(k, count - 2)
            row = lax.div(k, 128) * 8
            col = lax.rem(k, 128)
            own = table[row + 1, col]
            rhs = []
            alive = []
            for v in range(2):
                other = table[row, col + v]
                alive.append(jnp.where(inside, table[row + 2, col + v], 0).astype(f32))
                a, b, c, ext = split_rows(block_rows(win_ref, other, origin, 3, 6), 0.0)
                rhs.append(
                    jnp.concatenate(
                        [a, a, a, b, b, c, ext, jnp.zeros((16, 128), bf16)], axis=0
                    )
                )
            work.append((own, alive, jnp.concatenate(rhs, axis=1)))
        outs = [
            lax.dot_general(
                rhs, feats[own], (((0,), (0,)), ((), ())), preferred_element_type=f32
            )
            for own, _, rhs in work
        ]
        sums = []
        for (own, alive, rhs), out in zip(work, outs):
            inv = lax.rsqrt(jnp.maximum(out[:, 0:128], 0.25))
            live = jnp.concatenate([inv[0:128] * alive[0], inv[128:256] * alive[1]], axis=0)
            g = (inv * inv) * live * out[:, 128:256]
            hi = g.astype(bf16)
            lo = (g - hi.astype(f32)).astype(bf16)
            lhs = jnp.concatenate([rhs[0:16], rhs[48:64], rhs[80:112]], axis=0)
            r = jnp.dot(lhs, hi, preferred_element_type=f32)
            r = r + jnp.dot(lhs, lo, preferred_element_type=f32)
            sums.append((own, jnp.where(top, r[0:16] + r[16:32] + r[32:48], r[48:49])))
        for own, r in sums:
            acc[own] += r
        return carry

    lax.fori_loop(0, (count // 2 + UNROLL - 1) // UNROLL, items, 0)

    far_in.wait()
    for g in range(nblocks):
        p = own_ref[9 * g : 9 * g + 16, :] - origin
        t = acc[g]
        near = (p[0:3] * t[3:4] - t[0:3]) * unit[g : g + 1, :]
        force = far_ref[0:3, g * 128 : g * 128 + 128] + near
        for a in range(3):
            out_ref[a, g : g + 1, :] = force[a : a + 1]


def on_device(seg_data, cell_of_block, cell_center, pairs, live_count):
    nblocks, _, width = seg_data.shape
    ncell = cell_center.shape[1]
    slots = pairs.shape[0]
    vmem = pl.BlockSpec(memory_space=pltpu.VMEM)
    hbm = pl.BlockSpec(memory_space=pltpu.HBM)
    dma = pltpu.SemaphoreType.DMA
    far, window = pl.pallas_call(
        exchange_and_far,
        out_shape=(
            jax.ShapeDtypeStruct((3, nblocks * width), f32),
            jax.ShapeDtypeStruct((2, 12, ROWS, width), f32),
        ),
        in_specs=[hbm] * 5,
        out_specs=(hbm, hbm),
        scratch_shapes=[
            pltpu.VMEM((9, nblocks, width), f32),
            pltpu.VMEM((1, nblocks), jnp.int32),
            pltpu.VMEM((3, ncell), f32),
            pltpu.VMEM((2, slots), jnp.int32),
            pltpu.VMEM((1, 1), jnp.int32),
            pltpu.VMEM((nblocks, width), jnp.int32),
            pltpu.VMEM((ROWS, width), f32),
            pltpu.VMEM((16, nblocks * width), f32),
            pltpu.VMEM((18, 128), f32),
            pltpu.VMEM((18, 128), f32),
            pltpu.VMEM((18, 128), f32),
            pltpu.VMEM((3, 18, 128), f32),
            pltpu.VMEM((4, 4, 18, 128), f32),
            pltpu.VMEM((ncell, 32), bf16),
            pltpu.VMEM((32, nblocks * width), bf16),
            pltpu.VMEM((32, nblocks * width), f32),
            pltpu.VMEM((6, 2, ncell // 16, nblocks * width), bf16),
            pltpu.VMEM((3, nblocks * width), f32),
            dma((5,)), dma((2,)), dma((2,)), dma((3, 3)), dma((3, 3)), dma((3,)), dma((3,)),
            dma, dma, dma((3,)), dma((3,)), dma((3,)), dma((3,)), dma((3,)), dma((3,)), dma, dma,
        ],
        compiler_params=pltpu.CompilerParams(
            collective_id=0, has_side_effects=True, vmem_limit_bytes=56 << 20
        ),
    )(
        seg_data.transpose(1, 0, 2), cell_of_block[None, :], cell_center, pairs.T,
        live_count[None, :],
    )
    force = pl.pallas_call(
        near_kernel,
        out_shape=jax.ShapeDtypeStruct((3, nblocks, width), f32),
        in_specs=[hbm] * 3,
        out_specs=vmem,
        scratch_shapes=[
            pltpu.VMEM((24 * ROWS, width), f32),
            pltpu.VMEM((24, 8, width), f32),
            pltpu.VMEM((ROWS, width), f32),
            pltpu.VMEM((3, nblocks * width), f32),
            pltpu.VMEM((nblocks, 128, 256), bf16),
            pltpu.VMEM((256, 64), bf16),
            pltpu.VMEM((nblocks, width), f32),
            pltpu.VMEM((nblocks, 16, width), f32),
            pltpu.VMEM((25 * 32, width), f32),
            pltpu.VMEM((24, width), jnp.int32),
            pltpu.SMEM((26 * 8, width), jnp.int32),
            dma((2,)), dma((4,)),
        ],
        compiler_params=pltpu.CompilerParams(vmem_limit_bytes=56 << 20),
    )(window.reshape(24 * ROWS, width), window.reshape(24, ROWS, width), far)
    return force.transpose(1, 0, 2)


def solution(mesh):
    placed = (
        P(("space", "sub"), None, None),
        P(("space", "sub")),
        P(),
        P(("space", "sub"), None),
        P(("space", "sub")),
    )
    return jax.shard_map(
        on_device,
        mesh=mesh,
        in_specs=placed,
        out_specs=P(("space", "sub"), None, None),
        check_vma=False,
    )
```

```python
import functools

import jax
import jax.numpy as jnp
from jax import lax
from jax.experimental import pallas as pl
from jax.experimental.pallas import tpu as pltpu
from jax.sharding import PartitionSpec as P

MESH = pl.DeviceIdType.MESH
f32 = jnp.float32
bf16 = jnp.bfloat16
ROWS = 296
UNROLL = 12


def three(x):
    a = x.astype(bf16).astype(f32)
    r = x - a
    b = r.astype(bf16).astype(f32)
    return a, b, (r - b).astype(bf16).astype(f32)


def exchange_and_far(
    seg_hbm, cell_hbm, cc_hbm, pair_hbm, live_hbm, far_hbm, win,
    seg_ref, cell_row, cc_ref, pair_ref, live_ref, cell_ref,
    payload, flat, mine, twin, pair_sum, parts, moments, cells_f, segs_f, acc, early, far_ref,
    in_sem, x_send, x_recv, z_send, z_recv, r_send, r_recv,
    twin_send, twin_recv, p_send, p_recv, y_send, y_recv, m_send, m_recv, own_sem, far_sem,
):
    space = lax.axis_index("space")
    sub = lax.axis_index("sub")
    y, x = lax.div(space, 4), lax.rem(space, 4)
    z, core = lax.div(sub, 2), lax.rem(sub, 2)
    nblocks = seg_ref.shape[1]
    ncell = cc_ref.shape[1]
    per = ncell // 16
    other_core = (space, z * 2 + 1 - core)

    def along_z(k):
        return (space, lax.rem(z + k, 4) * 2 + core)

    def along_y(k):
        return (lax.rem(y + k, 4) * 4 + x, sub)

    def along_x(k):
        return (y * 4 + lax.rem(x + k, 4), sub)

    def along_space(k):
        return (lax.rem(space + k, 16), sub)

    ins = [
        pltpu.make_async_copy(src, dst, in_sem.at[i])
        for i, (src, dst) in enumerate(
            [
                (cell_hbm, cell_row), (cc_hbm, cc_ref), (seg_hbm, seg_ref),
                (pair_hbm, pair_ref), (live_hbm, live_ref),
            ]
        )
    ]
    for copy in ins:
        copy.start()
    barrier = pltpu.get_barrier_semaphore()
    partners = [other_core, along_space(1), along_space(15)]
    partners += [to(k) for to in (along_z, along_y, along_x) for k in (1, 2, 3)]
    for to in partners:
        pl.semaphore_signal(barrier, inc=1, device_id=to, device_id_type=MESH)

    for copy in ins:
        copy.wait()

    base = space * per
    own_cc = cc_ref[:, pl.ds(pl.multiple_of(base, 256), per)]
    square = lax.broadcasted_iota(jnp.int32, (nblocks, nblocks), 0)
    lane = lax.broadcasted_iota(jnp.int32, (nblocks, nblocks), 1)
    cell = jnp.sum(
        jnp.where(square == lane, cell_row[...].astype(f32), 0.0), axis=1, keepdims=True
    )
    cell_ref[...] = jnp.broadcast_to(cell, (nblocks, 128)).astype(jnp.int32)
    hot = (
        cell.astype(jnp.int32) - base
        == lax.broadcasted_iota(jnp.int32, (nblocks, per), 1)
    ).astype(f32)
    origin = []
    for a in range(3):
        centre = jnp.sum(hot * own_cc[a : a + 1], axis=1, keepdims=True)
        origin.append(centre[0:1])
        payload[pl.ds(a, nblocks, stride=9), :] = seg_ref[a] + centre
    for a in range(3, 9):
        payload[pl.ds(a, nblocks, stride=9), :] = seg_ref[a]
    alive = lax.broadcasted_iota(jnp.int32, (2, 128), 1) < live_ref[...]
    payload[288:290, :] = jnp.where(alive, pair_ref[...].astype(f32), -1.0)
    payload[290:296, :] = jnp.zeros((6, 128), f32)
    for a in range(3):
        for b in range(3):
            outer = jnp.sum(seg_ref[6 + a] * seg_ref[3 + b], axis=1, keepdims=True)
            row = jnp.sum(hot * outer, axis=0, keepdims=True)
            mine[3 * a + b : 3 * a + b + 1, :] = row[:, 0:128]
            mine[9 + 3 * a + b : 10 + 3 * a + b, :] = row[:, 128:256]

    def send(src, dst, send_sem, recv_sem, to):
        return pltpu.make_async_remote_copy(
            src_ref=src, dst_ref=dst, send_sem=send_sem, recv_sem=recv_sem,
            device_id=to, device_id_type=MESH,
        )

    def arrived(ref, sem):
        pltpu.make_async_copy(ref, ref, sem).wait()

    own_copy = pltpu.make_async_copy(payload, win.at[core, 0], own_sem)
    own_copy.start()
    pl.semaphore_wait(barrier, len(partners))

    to_twin = send(mine, twin, twin_send, twin_recv, other_core)
    to_z = [
        send(pair_sum, parts.at[3 - k], p_send.at[k - 1], p_recv.at[3 - k], along_z(k))
        for k in (1, 2, 3)
    ]
    to_y = [
        send(moments.at[0, 0], moments.at[0, 4 - k], y_send.at[k - 1], y_recv.at[3 - k], along_y(k))
        for k in (1, 2, 3)
    ]
    to_x = [
        send(moments.at[0], moments.at[4 - k], m_send.at[k - 1], m_recv.at[3 - k], along_x(k))
        for k in (1, 2, 3)
    ]
    after = send(payload, win.at[core, 4], x_send.at[0], x_recv.at[0], along_space(1))
    before = send(payload, win.at[core, 5], x_send.at[1], x_recv.at[1], along_space(15))
    step = 1 + 2 * core

    def place(group, j):
        return win.at[core, j if group == 0 else 3 + group + 2 * j]

    def spread(group, j):
        return send(
            payload if group == 0 else place(group, 0), place(group, 2 - j),
            z_send.at[group, j], z_recv.at[group, 1 - j], along_z(1 + 2 * j),
        )

    def forward(group):
        return send(
            place(group, 2 - core), place(group, 3),
            z_send.at[group, 2], z_recv.at[group, 2], along_z(step),
        )

    relayed = [(0, 4), (4, 10), (10, 12)]

    def relay(i):
        part = win.at[core, relayed[i][0] : relayed[i][1]]
        return send(part, part, r_send.at[i], r_recv.at[i], other_core)

    to_twin.start()
    after.start()
    before.start()

    for g in range(nblocks):
        lanes = slice(g * 128, g * 128 + 128)
        flat[0:3, lanes] = payload[9 * g : 9 * g + 3, :]
        flat[8:11, lanes] = payload[9 * g + 3 : 9 * g + 6, :]
    row3 = lax.broadcasted_iota(jnp.int32, (3, 1), 0)
    origin = jnp.where(row3 == 0, origin[0], jnp.where(row3 == 1, origin[1], origin[2]))
    ones = jnp.ones((3, ncell), f32)
    blank = jnp.zeros((8, ncell), f32)
    c = cc_ref[...] - origin
    c1, c2, c3 = three(c)
    cq = jnp.concatenate(three(jnp.sum(c * c, axis=0, keepdims=True)), axis=0)
    cells_f[...] = jnp.transpose(
        jnp.concatenate([c1, c1, c2, c2, c1, c3, cq, ones, blank], axis=0)
    ).astype(bf16)
    p = flat[0:3, :] - origin
    p1, p2, p3 = three(-2.0 * p)
    pq = jnp.concatenate(three(1.0 + jnp.sum(p * p, axis=0, keepdims=True)), axis=0)
    segs_f[...] = jnp.concatenate(
        [p1, p2, p1, p2, p3, p1, ones, pq, blank], axis=0
    ).astype(bf16)

    def region_of(dx, dy):
        return lax.rem(y + dy, 4) * 4 + lax.rem(x + dx, 4)

    def weights(region, first):
        at = pl.multiple_of(region * per, 256)
        dist = jnp.dot(cells_f[pl.ds(at, per), :], segs_f[...], preferred_element_type=f32)
        w = pl.reciprocal(dist, approx=True)
        if first:
            cell_id = at + lax.broadcasted_iota(jnp.int32, (per, 128), 0)
            w = jnp.concatenate(
                [
                    jnp.where(
                        cell_id == cell_ref[g : g + 1, :], 0.0, w[:, g * 128 : g * 128 + 128]
                    )
                    for g in range(nblocks)
                ],
                axis=1,
            )
        hi = w.astype(bf16)
        return hi, (w - hi.astype(f32)).astype(bf16)

    def product(dx, dy, hi, lo):
        m = moments[dx, dy]
        m = jnp.concatenate([m[0:9], m[9:18]], axis=1)
        m = jnp.concatenate([m, jnp.zeros((7, per), f32)], axis=0)
        m_hi = m.astype(bf16)
        m = jnp.concatenate([m_hi, (m - m_hi.astype(f32)).astype(bf16)], axis=0)
        return jnp.dot(m, hi, preferred_element_type=f32) + jnp.dot(
            m, lo, preferred_element_type=f32
        )

    def make(k, carry):
        early[k, 0], early[k, 1] = weights(region_of(lax.div(k, 4), lax.rem(k, 4)), False)
        return carry

    def two(j, carry):
        k = 2 * j
        dx, dy = lax.div(k, 4), lax.rem(k, 4)
        hi, lo = weights(region_of(dx, dy), False)
        hi2, lo2 = weights(region_of(dx, dy + 1), False)
        acc[...] += product(dx, dy, hi, lo) + product(dx, dy + 1, hi2, lo2)
        return carry

    early[0, 0], early[0, 1] = weights(space, True)

    arrived(twin, twin_recv)
    pair_sum[...] = mine[...] + twin[...]
    for copy in to_z:
        copy.start()
    for j in (0, 1):
        spread(0, j).start()
    lax.fori_loop(1, 4, make, 0)

    region = pair_sum[...]
    for k in range(3):
        arrived(parts.at[k], p_recv.at[k])
        region = region + parts[k]
    moments[0, 0] = region
    for copy in to_y:
        copy.start()
    for group in (1, 2):
        arrived(place(group, 0), x_recv.at[group - 1])
        for j in (0, 1):
            spread(group, j).start()
    lax.fori_loop(4, 6, make, 0)

    for k in range(3):
        arrived(moments.at[0, k + 1], y_recv.at[k])
    for copy in to_x:
        copy.start()
    for j in (0, 1):
        arrived(place(0, j + 1), z_recv.at[0, j])
    forward(0).start()
    acc[...] = product(0, 0, early[0, 0], early[0, 1])
    acc[...] += (
        product(0, 1, early[1, 0], early[1, 1])
        + product(0, 2, early[2, 0], early[2, 1])
        + product(0, 3, early[3, 0], early[3, 1])
    )

    arrived(moments.at[1], m_recv.at[0])
    acc[...] += product(1, 0, early[4, 0], early[4, 1]) + product(1, 1, early[5, 0], early[5, 1])
    for j in (0, 1):
        arrived(place(1, j + 1), z_recv.at[1, j])
    forward(1).start()
    lax.fori_loop(3, 4, two, 0)
    arrived(moments.at[2], m_recv.at[1])
    lax.fori_loop(4, 5, two, 0)
    for j in (0, 1):
        arrived(place(2, j + 1), z_recv.at[2, j])
    forward(2).start()
    relay(1).start()
    arrived(place(0, 3), z_recv.at[0, 2])
    own_copy.wait()
    relay(0).start()
    lax.fori_loop(5, 6, two, 0)
    arrived(moments.at[3], m_recv.at[2])
    lax.fori_loop(6, 7, two, 0)
    for group in (1, 2):
        arrived(place(group, 3), z_recv.at[group, 2])
    relay(2).start()
    lax.fori_loop(7, 8, two, 0)

    grid = acc[0:9, :] + acc[16:25, :]
    line = flat[8:11, :]
    for a in range(3):
        far_ref[a : a + 1, :] = jnp.sum(
            grid[3 * a : 3 * a + 3, :] * line, axis=0, keepdims=True
        )

    far_copy = pltpu.make_async_copy(far_ref, far_hbm, far_sem)
    far_copy.start()

    for i, (lo, hi) in enumerate(relayed):
        arrived(win.at[1 - core, lo:hi], r_recv.at[i])
    for copy in [to_twin, after, before] + to_z + to_y + to_x:
        copy.wait_send()
    for group in range(3):
        for j in (0, 1):
            spread(group, j).wait_send()
        forward(group).wait_send()
    for i in range(len(relayed)):
        relay(i).wait_send()
    far_copy.wait()


def arrangement():
    q = lax.broadcasted_iota(jnp.int32, (256, 64), 0)
    r = lax.broadcasted_iota(jnp.int32, (256, 64), 1)
    kind, col = q // 128, q % 128
    group, line = col // 16, col % 16
    mate = jnp.where(group < 3, group, jnp.where(group < 5, group - 3, 0))
    same = (group < 6) & (r == mate * 16 + line)
    dist = (kind == 0) & same & (line < 3)
    extra = (kind == 0) & (group == 6) & (
        ((line < 3) & (r == 48 + 3 + line)) | ((line >= 3) & (line < 6) & (r == 48))
    )
    couple = (kind == 1) & same & (line >= 3) & (line < 12)
    return jnp.where(dist, -2.0, jnp.where(extra | couple, 1.0, 0.0)).astype(bf16)


def block_rows(ref, row, origin, first, second):
    row16 = lax.broadcasted_iota(jnp.int32, (16, 128), 0)
    u = [ref[pl.ds(row + first + k, 1), :] for k in range(3)]
    v = [ref[pl.ds(row + second + k, 1), :] for k in range(3)]
    left = jnp.where(row16 < 6, u[0], jnp.where(row16 < 9, u[1], u[2]))
    place = row16 % 3
    right = jnp.where(place == 0, v[0], jnp.where(place == 1, v[1], v[2]))
    both = jnp.where(row16 < 12, left * right, 0.0)
    return jnp.where(row16 < 3, ref[pl.ds(row, 16), :] - origin, both)


def split_rows(x, plus):
    row16 = lax.broadcasted_iota(jnp.int32, (16, 128), 0)
    a, b, c = three(x)
    sq = jnp.sum(jnp.where(row16 < 3, x * x, 0.0), axis=0, keepdims=True) + plus
    s1, s2, s3 = three(sq)
    ext = jnp.where(
        row16 < 3, 1.0,
        jnp.where(row16 == 3, s1, jnp.where(row16 == 4, s2, jnp.where(row16 == 5, s3, 0.0))),
    )
    return a.astype(bf16), b.astype(bf16), c.astype(bf16), ext.astype(bf16)


def build_list(pair_ref, space, sub, nblocks, hots, listed, table, sem):
    first_block = ((space * 8 + sub) * nblocks).astype(f32)
    target = jnp.concatenate(
        [pair_ref[d, 0:1, :] for d in range(24)] + [pair_ref[sub % 2 * 12, 0:1, :]],
        axis=0,
    )
    source = jnp.concatenate(
        [pair_ref[d, 1:2, :] for d in range(24)] + [pair_ref[sub % 2 * 12, 1:2, :]],
        axis=0,
    )
    is_own = lax.broadcasted_iota(jnp.int32, (25, 128), 0) == 24
    mine = jnp.where(is_own, target, source) - first_block
    theirs = jnp.where(is_own, source, target)
    used = (source >= 0) & (mine >= 0) & (mine < nblocks)
    mine = jnp.where(used, mine, -1.0)
    owner = jnp.floor(theirs * (1.0 / 32))
    their_space = jnp.floor(owner * (1.0 / 8))
    their_sub = owner - 8.0 * their_space
    their_z = jnp.floor(their_sub * 0.5)
    ahead = their_space - space.astype(f32)
    ahead = jnp.where(ahead < -8, ahead + 16.0, jnp.where(ahead > 8, ahead - 16.0, ahead))
    dz = their_z - (sub // 2).astype(f32)
    dz = jnp.where(dz < 0, dz + 4.0, dz)
    dz = jnp.where(dz == 3, 2.0, jnp.where(dz == 2, 3.0, dz))
    dev = (their_sub - 2.0 * their_z) * 12.0 + jnp.where(
        ahead == 0, dz, 4.0 + 2.0 * dz + (ahead > 0).astype(f32)
    )
    local = theirs - 32.0 * owner
    before = (
        lax.broadcasted_iota(jnp.int32, (128, 128), 0)
        < lax.broadcasted_iota(jnp.int32, (128, 128), 1)
    ).astype(bf16)
    block_id = lax.broadcasted_iota(jnp.int32, (32, 128), 0).astype(f32)
    run = jnp.zeros((32, 1), f32)
    hots[...] = jnp.concatenate(
        [(mine[r : r + 1] == block_id).astype(f32) for r in range(25)], axis=0
    )
    within = jnp.dot(hots[...].astype(bf16), before, preferred_element_type=f32)
    sums = jnp.sum(hots[...], axis=1, keepdims=True)
    runs = []
    for r in range(25):
        runs.append(run)
        run = run + sums[32 * r : 32 * r + 32]
    even = 2.0 * jnp.floor((run + 1.0) * 0.5)
    above = (
        lax.broadcasted_iota(jnp.int32, (32, 32), 1)
        < lax.broadcasted_iota(jnp.int32, (32, 32), 0)
    ).astype(f32)
    starts = jnp.dot(
        above, jnp.broadcast_to(even, (32, 128)), precision=lax.Precision.HIGHEST,
        preferred_element_type=f32,
    )[:, 0:1]
    count = jnp.sum(even).astype(jnp.int32)
    ranks = []
    for r in range(25):
        h = hots[32 * r : 32 * r + 32, :]
        at = within[32 * r : 32 * r + 32] + (runs[r] + starts)
        ranks.append(jnp.sum(h * at, axis=0, keepdims=True))
    rank = jnp.where(used, jnp.concatenate(ranks, axis=0), -1.0)
    pad = jnp.full((128 - 25, 128), -1.0, f32)
    rank_t = jnp.transpose(jnp.concatenate([rank, pad], axis=0))
    lane = lax.broadcasted_iota(jnp.int32, (128, 128), 1).astype(f32)
    row8 = lax.broadcasted_iota(jnp.int32, (8, 128), 0)
    ends = starts + even

    def rows_of(kr):
        got = jnp.zeros((8, 128), f32)
        want = lane + (kr * 128).astype(f32)
        for r in range(25):
            hot = (rank_t[:, r : r + 1] == want).astype(bf16)
            vals = jnp.where(row8 == 0, dev[r : r + 1], jnp.where(row8 == 1, local[r : r + 1], 1.0))
            vals = jnp.where((row8 < 3) & used[r : r + 1], vals, 0.0)
            got = got + jnp.dot(vals.astype(bf16), hot, preferred_element_type=f32)
        other = got[0:1] * float(ROWS) + got[1:2] * 9.0
        own = jnp.sum((ends <= want[0:32]).astype(f32), axis=0, keepdims=True)
        own = jnp.minimum(own, 31.0)
        rows = jnp.where(
            row8 == 0, other, jnp.where(row8 == 1, own, jnp.where(row8 == 2, got[2:3], 0.0))
        )
        return rows.astype(jnp.int32)

    for kr in range(2):
        listed[8 * kr : 8 * kr + 8, :] = rows_of(jnp.int32(kr))
    first = pltpu.make_async_copy(listed.at[0:16], table.at[0:16], sem.at[0])
    first.start()

    def fill(kr, carry):
        listed[16:24, :] = rows_of(kr)
        copy = pltpu.make_async_copy(listed.at[16:24], table.at[pl.ds(kr * 8, 8)], sem.at[1])
        copy.start()
        copy.wait()
        return carry

    lax.fori_loop(2, lax.div(count + 127, 128), fill, 0)
    return count, first


def near_kernel(
    win_hbm, pair_hbm, far_hbm, out_ref,
    win_ref, pair_ref, own_ref, far_ref, feats, arrange, unit, acc, hots, listed, table, sem, in_sem,
):
    space, sub = lax.axis_index("space"), lax.axis_index("sub")
    nblocks = out_ref.shape[1]
    my_row = pl.multiple_of(sub % 2 * 12 * ROWS, 8)
    pairs_in = pltpu.make_async_copy(pair_hbm.at[:, 288:296], pair_ref, in_sem.at[0])
    own_in = pltpu.make_async_copy(win_hbm.at[pl.ds(my_row, ROWS)], own_ref, in_sem.at[1])
    win_in = pltpu.make_async_copy(win_hbm, win_ref, in_sem.at[2])
    far_in = pltpu.make_async_copy(far_hbm, far_ref, in_sem.at[3])
    for copy in (pairs_in, own_in, win_in, far_in):
        copy.start()
    pairs_in.wait()
    count, listing = build_list(pair_ref, space, sub, nblocks, hots, listed, table, sem)
    own_in.wait()
    origin = jnp.where(
        lax.broadcasted_iota(jnp.int32, (16, 1), 0) < 3, own_ref[0:16, 0:1], 0.0
    )

    arrange[...] = arrangement()
    acc[...] = jnp.zeros_like(acc)
    row16 = lax.broadcasted_iota(jnp.int32, (16, 128), 0)
    for q in range(0, nblocks, 8):
        parts = []
        for g in range(q, q + 8):
            x = block_rows(own_ref, 9 * g, origin, 6, 3)
            size = jnp.max(jnp.where(row16 < 3, 0.0, jnp.abs(x)), axis=0, keepdims=True)
            size = jnp.maximum(jnp.max(size, axis=1, keepdims=True), 1e-30)
            unit[g : g + 1, :] = jnp.broadcast_to(size, (1, 128))
            x = jnp.where(row16 < 3, x, x * (1.0 / size))
            parts.append(jnp.concatenate(split_rows(x, 0.25), axis=0))
        f = jnp.dot(
            arrange[...], jnp.concatenate(parts, axis=1), preferred_element_type=f32
        ).astype(bf16)
        for g in range(8):
            feats[q + g, :, 0:128] = f[0:128, g * 128 : g * 128 + 128]
            feats[q + g, :, 128:256] = f[128:256, g * 128 : g * 128 + 128]

    listing.wait()
    win_in.wait()
    top = lax.broadcasted_iota(jnp.int32, (16, 128), 0) < 3

    def items(step, carry):
        work = []
        for u in range(UNROLL):
            k = (step * UNROLL + u) * 2
            inside = k < count
            k = jnp.minimum(k, count - 2)
            row = lax.div(k, 128) * 8
            col = lax.rem(k, 128)
            own = table[row + 1, col]
            rhs = []
            alive = []
            for v in range(2):
                other = table[row, col + v]
                alive.append(jnp.where(inside, table[row + 2, col + v], 0).astype(f32))
                a, b, c, ext = split_rows(block_rows(win_ref, other, origin, 3, 6), 0.0)
                rhs.append(
                    jnp.concatenate(
                        [a, a, a, b, b, c, ext, jnp.zeros((16, 128), bf16)], axis=0
                    )
                )
            work.append((own, alive, jnp.concatenate(rhs, axis=1)))
        outs = [
            lax.dot_general(
                rhs, feats[own], (((0,), (0,)), ((), ())), preferred_element_type=f32
            )
            for own, _, rhs in work
        ]
        sums = []
        for (own, alive, rhs), out in zip(work, outs):
            inv = lax.rsqrt(jnp.maximum(out[:, 0:128], 0.25))
            live = jnp.concatenate([inv[0:128] * alive[0], inv[128:256] * alive[1]], axis=0)
            g = (inv * inv) * live * out[:, 128:256]
            hi = g.astype(bf16)
            lo = (g - hi.astype(f32)).astype(bf16)
            lhs = jnp.concatenate([rhs[0:16], rhs[48:64], rhs[80:112]], axis=0)
            r = jnp.dot(lhs, hi, preferred_element_type=f32)
            r = r + jnp.dot(lhs, lo, preferred_element_type=f32)
            sums.append((own, jnp.where(top, r[0:16] + r[16:32] + r[32:48], r[48:49])))
        for own, r in sums:
            acc[own] += r
        return carry

    lax.fori_loop(0, (count // 2 + UNROLL - 1) // UNROLL, items, 0)

    far_in.wait()
    for g in range(nblocks):
        p = own_ref[9 * g : 9 * g + 16, :] - origin
        t = acc[g]
        near = (p[0:3] * t[3:4] - t[0:3]) * unit[g : g + 1, :]
        force = far_ref[0:3, g * 128 : g * 128 + 128] + near
        for a in range(3):
            out_ref[a, g : g + 1, :] = force[a : a + 1]


def on_device(seg_data, cell_of_block, cell_center, pairs, live_count):
    nblocks, _, width = seg_data.shape
    ncell = cell_center.shape[1]
    slots = pairs.shape[0]
    vmem = pl.BlockSpec(memory_space=pltpu.VMEM)
    hbm = pl.BlockSpec(memory_space=pltpu.HBM)
    dma = pltpu.SemaphoreType.DMA
    far, window = pl.pallas_call(
        exchange_and_far,
        out_shape=(
            jax.ShapeDtypeStruct((3, nblocks * width), f32),
            jax.ShapeDtypeStruct((2, 12, ROWS, width), f32),
        ),
        in_specs=[hbm] * 5,
        out_specs=(hbm, hbm),
        scratch_shapes=[
            pltpu.VMEM((9, nblocks, width), f32),
            pltpu.VMEM((1, nblocks), jnp.int32),
            pltpu.VMEM((3, ncell), f32),
            pltpu.VMEM((2, slots), jnp.int32),
            pltpu.VMEM((1, 1), jnp.int32),
            pltpu.VMEM((nblocks, width), jnp.int32),
            pltpu.VMEM((ROWS, width), f32),
            pltpu.VMEM((16, nblocks * width), f32),
            pltpu.VMEM((18, 128), f32),
            pltpu.VMEM((18, 128), f32),
            pltpu.VMEM((18, 128), f32),
            pltpu.VMEM((3, 18, 128), f32),
            pltpu.VMEM((4, 4, 18, 128), f32),
            pltpu.VMEM((ncell, 32), bf16),
            pltpu.VMEM((32, nblocks * width), bf16),
            pltpu.VMEM((32, nblocks * width), f32),
            pltpu.VMEM((6, 2, ncell // 16, nblocks * width), bf16),
            pltpu.VMEM((3, nblocks * width), f32),
            dma((5,)), dma((2,)), dma((2,)), dma((3, 3)), dma((3, 3)), dma((3,)), dma((3,)),
            dma, dma, dma((3,)), dma((3,)), dma((3,)), dma((3,)), dma((3,)), dma((3,)), dma, dma,
        ],
        compiler_params=pltpu.CompilerParams(
            collective_id=0, has_side_effects=True, vmem_limit_bytes=56 << 20
        ),
    )(
        seg_data.transpose(1, 0, 2), cell_of_block[None, :], cell_center, pairs.T,
        live_count[None, :],
    )
    force = pl.pallas_call(
        near_kernel,
        out_shape=jax.ShapeDtypeStruct((3, nblocks, width), f32),
        in_specs=[hbm] * 3,
        out_specs=vmem,
        scratch_shapes=[
            pltpu.VMEM((24 * ROWS, width), f32),
            pltpu.VMEM((24, 8, width), f32),
            pltpu.VMEM((ROWS, width), f32),
            pltpu.VMEM((3, nblocks * width), f32),
            pltpu.VMEM((nblocks, 128, 256), bf16),
            pltpu.VMEM((256, 64), bf16),
            pltpu.VMEM((nblocks, width), f32),
            pltpu.VMEM((nblocks, 16, width), f32),
            pltpu.VMEM((25 * 32, width), f32),
            pltpu.VMEM((24, width), jnp.int32),
            pltpu.SMEM((26 * 8, width), jnp.int32),
            dma((2,)), dma((4,)),
        ],
        compiler_params=pltpu.CompilerParams(vmem_limit_bytes=56 << 20),
    )(window.reshape(24 * ROWS, width), window.reshape(24, ROWS, width), far)
    return force.transpose(1, 0, 2)


def solution(mesh):
    placed = (
        P(("space", "sub"), None, None),
        P(("space", "sub")),
        P(),
        P(("space", "sub"), None),
        P(("space", "sub")),
    )
    return jax.shard_map(
        on_device,
        mesh=mesh,
        in_specs=placed,
        out_specs=P(("space", "sub"), None, None),
        check_vma=False,
    )
```
